512 devices in a mesh: gx: 16 (over x_lo, y), gy: 32 (over x_hi, z, core).
Axes of the slice: x: 4 (x_hi: 2, x_lo: 2; x = x_hi * 2 + x_lo), y: 8, z: 8, core: 2. Of those that a mesh axis runs over, the one named last changes fastest.
Arguments:
- fluid_pops: float32 [19, 2, 256, 4096], P(None, None, 'gx', 'gy'), may hold values from 0.01 to 0.6, as said below
- magnet_pops: float32 [3, 7, 2, 256, 4096], P(None, None, None, 'gx', 'gy'), may hold values from -0.12 to 0.12
Outputs:
- fluid_next: float32 [19, 2, 256, 4096], P(None, None, 'gx', 'gy')
- magnet_next: float32 [3, 7, 2, 256, 4096], P(None, None, None, 'gx', 'gy')
The draws below stay inside these ranges and needn't reach their ends.
Inputs may be any that keep to these rules, and one draw needn't show every extreme that they name: `fluid_pops`: every fluid population is positive.
All inputs are finite; a program needn't handle non-finite values.
Results may differ from the reference program's by a relative error of at most 0.0001.
Values sent between devices are 32-bit elements; how exact they have to be, the bound alone decides.
A program may use at most 64 MiB of HBM per device.

```python
import jax
import jax.numpy as jnp
import numpy as np

NZ = 2
STEPS = 2
NX = 256
NY = 4096


FLUID_WEIGHT_TABLE = np.array([1.0 / 3.0] + [1.0 / 18.0] * 6 + [1.0 / 36.0] * 12, dtype=np.float32)


MAGNET_WEIGHT_TABLE = np.array([0.25] + [0.125] * 6, dtype=np.float32)


def draw_fluid_pops(key, part):
    key = jax.random.fold_in(key, 11)
    key_density, key_jitter = jax.random.split(key)
    density = jax.random.uniform(key_density, (NZ, NX, NY), jnp.float32, 0.8, 1.2)
    jitter = 0.25 * jax.random.uniform(key_jitter, (19, NZ, NX, NY), jnp.float32, -1.0, 1.0)
    weights = jnp.asarray(FLUID_WEIGHT_TABLE).reshape(19, 1, 1, 1)
    return weights * density[None] * (1.0 + jitter)


def draw_magnet_pops(key, part):
    key = jax.random.fold_in(key, 23)
    key_field, key_jitter = jax.random.split(key)
    induction = jax.random.uniform(key_field, (3, 1, NZ, NX, NY), jnp.float32, -0.3, 0.3)
    jitter = jax.random.uniform(key_jitter, (3, 7, NZ, NX, NY), jnp.float32, -0.1, 0.1)
    weights = jnp.asarray(MAGNET_WEIGHT_TABLE).reshape(1, 7, 1, 1, 1)
    return weights * (induction + jitter)


def setup_inputs(seed: int = 0) -> dict:
    keys = jax.random.split(jax.random.key(seed), 3)
    fluid_pops = draw_fluid_pops(jax.random.fold_in(keys[2], 71), 0)
    magnet_pops = draw_magnet_pops(jax.random.fold_in(keys[2], 71), 0)
    return {"fluid_pops": fluid_pops, "magnet_pops": magnet_pops}


FLUID_VELOCITY = np.array([[0, 0, 0], [1, 0, 0], [-1, 0, 0], [0, 1, 0], [0, -1, 0], [0, 0, 1], [0, 0, -1],
                           [1, 1, 0], [-1, -1, 0], [1, -1, 0], [-1, 1, 0], [1, 0, 1], [-1, 0, -1], [1, 0, -1],
                           [-1, 0, 1], [0, 1, 1], [0, -1, -1], [0, 1, -1], [0, -1, 1]])
FLUID_WEIGHT = [1.0 / 3.0] + [1.0 / 18.0] * 6 + [1.0 / 36.0] * 12
MAGNET_WEIGHT = [0.25] + [0.125] * 6
TAU_FLUID = 0.9
TAU_MAGNET = 0.8


def collide(fluid_pops, magnet_pops):
    density = jnp.sum(fluid_pops, axis=0)
    velocity = []
    for comp in range(3):
        moment = jnp.zeros_like(density)
        for index in range(19):
            if FLUID_VELOCITY[index, comp] != 0:
                moment = moment + float(FLUID_VELOCITY[index, comp]) * fluid_pops[index]
        velocity.append(moment / density)
    induction = [jnp.sum(magnet_pops[comp], axis=0) for comp in range(3)]
    field_sq = induction[0] * induction[0] + induction[1] * induction[1] + induction[2] * induction[2]
    stress = [[density * velocity[one] * velocity[two] - induction[one] * induction[two]
               + (0.5 * field_sq if one == two else 0.0) for two in range(3)] for one in range(3)]
    stress_trace = stress[0][0] + stress[1][1] + stress[2][2]
    fluid_post = []
    for index in range(19):
        speed = jnp.zeros_like(density)
        contract = jnp.zeros_like(density)
        for one in range(3):
            if FLUID_VELOCITY[index, one] != 0:
                speed = speed + float(FLUID_VELOCITY[index, one]) * velocity[one]
                for two in range(3):
                    if FLUID_VELOCITY[index, two] != 0:
                        contract = contract + float(FLUID_VELOCITY[index, one] * FLUID_VELOCITY[index, two]) * stress[one][two]
        balance = FLUID_WEIGHT[index] * (density + 3.0 * density * speed + 4.5 * (contract - stress_trace / 3.0))
        fluid_post.append(fluid_pops[index] - (fluid_pops[index] - balance) / TAU_FLUID)
    magnet_post = []
    for comp in range(3):
        rows = []
        for index in range(7):
            flux = jnp.zeros_like(density)
            for other in range(3):
                if FLUID_VELOCITY[index, other] != 0:
                    flux = flux + float(FLUID_VELOCITY[index, other]) * (velocity[other] * induction[comp] - induction[other] * velocity[comp])
            balance = MAGNET_WEIGHT[index] * (induction[comp] + 4.0 * flux)
            rows.append(magnet_pops[comp, index] - (magnet_pops[comp, index] - balance) / TAU_MAGNET)
        magnet_post.append(jnp.stack(rows))
    return jnp.stack(fluid_post), jnp.stack(magnet_post)


def advect(plane, index):
    step_x, step_y, step_z = (int(v) for v in FLUID_VELOCITY[index])
    return jnp.roll(plane, (step_z, step_x, step_y), axis=(0, 1, 2))


def reference(fluid_pops, magnet_pops):
    for step_index in range(STEPS):
        fluid_post, magnet_post = collide(fluid_pops, magnet_pops)
        fluid_pops = jnp.stack([advect(fluid_post[index], index) for index in range(19)])
        magnet_pops = jnp.stack([jnp.stack([advect(magnet_post[comp, index], index) for index in range(7)]) for comp in range(3)])
    return fluid_pops, magnet_pops
```

```python
import functools

import jax
import jax.numpy as jnp
from jax import lax
from jax.experimental import pallas as pl
from jax.experimental.pallas import tpu as pltpu
from jax.sharding import PartitionSpec as P

MESH = pl.DeviceIdType.MESH
F32 = jnp.float32

FLUID = [
    (0, 0, 0),
    (1, 0, 0), (-1, 0, 0), (0, 1, 0), (0, -1, 0), (0, 0, 1), (0, 0, -1),
    (1, 1, 0), (-1, -1, 0), (1, -1, 0), (-1, 1, 0),
    (1, 0, 1), (-1, 0, -1), (1, 0, -1), (-1, 0, 1),
    (0, 1, 1), (0, -1, -1), (0, 1, -1), (0, -1, 1),
]
VEL = FLUID + FLUID[:7] * 3
NPOP = 40
OM_F = 1.0 / 0.9
OM_G = 1.0 / 0.8

XP = [p for p in range(NPOP) if VEL[p][0] == 1]
X0 = [p for p in range(NPOP) if VEL[p][0] == 0]
XM = [p for p in range(NPOP) if VEL[p][0] == -1]
ORDER = XP + X0 + XM
POS = {p: i for i, p in enumerate(ORDER)}
XOFF = {}
for i, p in enumerate(XP):
    XOFF[p] = i
for i, p in enumerate(X0):
    XOFF[p] = 8 + i
for i, p in enumerate(XM):
    XOFF[p] = 40 + i
YP = [p for p in range(NPOP) if VEL[p][1] == 1]
Y0 = [p for p in range(NPOP) if VEL[p][1] == 0]
YM = [p for p in range(NPOP) if VEL[p][1] == -1]
SLOT = {}
for i, p in enumerate(Y0):
    SLOT[p] = i
for i, p in enumerate(YP):
    SLOT[p] = 24 + 2 * i
for i, p in enumerate(YM):
    SLOT[p] = 25 + 2 * i
NX, NY, NZ = 16, 128, 2
PAD = 8
RX = NX + 2 * PAD


def zflip(p):
    return abs(VEL[p][2])


def plane(p, z, r, count=8):
    first = (POS[p] * NZ + z) * RX + PAD + r
    return slice(first, first + count)


def collide(pops):
    f, g = pops[:19], [pops[19 + 7 * a : 26 + 7 * a] for a in range(3)]
    pairs = [(i, i + 1) for i in range(1, 19, 2)]
    even = [f[i] + f[j] for i, j in pairs]
    odd = [f[i] - f[j] for i, j in pairs]
    rho = f[0] + ((even[0] + even[1]) + (even[2] + even[3])) + ((even[4] + even[5]) + ((even[6] + even[7]) + even[8]))
    mom = []
    for a in range(3):
        terms = [(odd[k], VEL[pairs[k][0]][a]) for k in range(9) if VEL[pairs[k][0]][a]]
        total = terms[0][0]
        for value, sign in terms[1:]:
            total = total + value if sign > 0 else total - value
        mom.append(total)
    inv = 1.0 / rho
    u = [m * inv for m in mom]
    b = [((g[a][0] + g[a][1]) + (g[a][2] + g[a][3])) + ((g[a][4] + g[a][5]) + g[a][6]) for a in range(3)]
    half = 0.5 * (b[0] * b[0] + b[1] * b[1] + b[2] * b[2])
    diag = [mom[a] * u[a] - b[a] * b[a] + half for a in range(3)]
    cross = {(a, c): mom[a] * u[c] - b[a] * b[c] for a, c in ((0, 1), (0, 2), (1, 2))}
    trace = diag[0] + diag[1] + diag[2]
    base = (OM_F / 36.0) * (rho - 1.5 * trace)
    d45 = [(4.5 * OM_F / 36.0) * d for d in diag]
    c9 = {k: (9.0 * OM_F / 36.0) * v for k, v in cross.items()}
    m3 = [(3.0 * OM_F / 36.0) * m for m in mom]
    keep = 1.0 - OM_F
    out = [None] * NPOP
    out[0] = keep * f[0] + 12.0 * base
    for k, (i, j) in enumerate(pairs):
        c = VEL[i]
        axes = [a for a in range(3) if c[a]]
        if len(axes) == 1:
            s = 2.0 * (base + d45[axes[0]])
            t = 2.0 * m3[axes[0]]
        else:
            a, d = axes
            s = base + d45[a] + d45[d]
            if c[a] * c[d] > 0:
                s = s + c9[(a, d)]
            else:
                s = s - c9[(a, d)]
            first = m3[a] if c[a] > 0 else -m3[a]
            t = first + m3[d] if c[d] > 0 else first - m3[d]
        out[i] = keep * f[i] + (s + t)
        out[j] = keep * f[j] + (s - t)
    keep = 1.0 - OM_G
    for a in range(3):
        rest = (OM_G / 8.0) * b[a]
        out[19 + 7 * a] = keep * g[a][0] + 2.0 * rest
        for d in range(3):
            plus, minus = rest, rest
            if d != a:
                flux = (4.0 * OM_G / 8.0) * (u[d] * b[a] - b[d] * u[a])
                plus, minus = rest + flux, rest - flux
            out[19 + 7 * a + 1 + 2 * d] = keep * g[a][1 + 2 * d] + plus
            out[19 + 7 * a + 2 + 2 * d] = keep * g[a][2 + 2 * d] + minus
    return out


def exchange(sizes, f_hbm, g_hbm, q, xb, ao, yb, fv, gv, xs, load_sem, send_sem, recv_sem):
    nx_dev, ny_dev = sizes
    ix, iy = lax.axis_index("gx"), lax.axis_index("gy")

    def device(dx, dy):
        return (lax.rem(ix + dx + nx_dev, nx_dev), lax.rem(iy + dy + ny_dev, ny_dev))

    around = [(dx, dy) for dx in (-1, 0, 1) for dy in (-1, 0, 1) if dx or dy]
    barrier = pltpu.get_barrier_semaphore()
    for dx, dy in around:
        pl.semaphore_signal(barrier, inc=1, device_id=device(dx, dy), device_id_type=MESH)

    load_f = pltpu.make_async_copy(f_hbm, fv, load_sem.at[0])
    load_g = pltpu.make_async_copy(g_hbm, gv, load_sem.at[1])
    load_f.start()
    load_g.start()
    load_f.wait()
    load_g.wait()

    lane = lax.broadcasted_iota(jnp.int32, (8, NY), 1)
    for half in range(2):
        rows = slice(8 * half, 8 * half + 8)
        at = slice(PAD + 8 * half, PAD + 8 * half + 8)
        up = [jnp.zeros((8, NY), F32) for _ in range(NZ)]
        down = [jnp.zeros((8, NY), F32) for _ in range(NZ)]
        for z in range(NZ):
            pops = [fv[p, z, rows, :] for p in range(19)]
            pops += [gv[a, j, z, rows, :] for a in range(3) for j in range(7)]
            post = collide(pops)
            for p in range(NPOP):
                zz = z ^ zflip(p)
                q[plane(p, zz, 8 * half), :] = post[p]
                s = SLOT[p]
                if VEL[p][1] == 0:
                    moved = pltpu.roll(post[p], s + 1, 1)
                    up[zz] = jnp.where(lane == s, moved, up[zz])
                    down[zz] = jnp.where(lane == s + 1, moved, down[zz])
                elif VEL[p][1] == 1:
                    moved = pltpu.roll(post[p], s + 2, 1)
                    up[zz] = jnp.where((lane == s) | (lane == s + 1), moved, up[zz])
                else:
                    moved = pltpu.roll(post[p], s, 1)
                    down[zz] = jnp.where((lane == s) | (lane == s + 1), moved, down[zz])
        for z in range(NZ):
            ao[0, z, at, :] = up[z]
            ao[1, z, at, :] = down[z]

    def row(first, count, z, r):
        return q[pl.ds(first * NZ * RX + z * RX + PAD + r, count, stride=NZ * RX), :]

    for z in range(NZ):
        xs[0, z, 0:8, :] = row(0, 8, z, NX - 2)
        xs[0, z, 8:32, :] = row(8, 24, z, NX - 1)
        xs[0, z, 32:40, :] = row(0, 8, z, NX - 1)
        xs[1, z, 0:24, :] = row(8, 24, z, 0)
        xs[1, z, 24:32, :] = row(32, 8, z, 0)
        xs[1, z, 32:40, :] = row(32, 8, z, 1)
        xb[0, z, 40:48, :] = row(32, 8, z, 0)
        xb[1, z, 0:8, :] = row(0, 8, z, NX - 1)

    pl.semaphore_wait(barrier, len(around))
    low, high, own = slice(0, 8), slice(24, 32), slice(8, 24)
    first, last = slice(8, 16), slice(16, 24)
    moves = []
    for side, dy in ((0, 1), (1, -1)):
        moves.append((ao.at[side, :, last], yb.at[side, :, low], 1, dy))
        moves.append((ao.at[side, :, first], yb.at[side, :, high], -1, dy))
        moves.append((ao.at[side, :, own], yb.at[side, :, own], 0, dy))
    moves.append((xs.at[0], xb.at[0, :, 0:40], 1, 0))
    moves.append((xs.at[1], xb.at[1, :, 8:48], -1, 0))
    moves.append((ao.at[:, :, last], ao.at[:, :, low], 1, 0))
    moves.append((ao.at[:, :, first], ao.at[:, :, high], -1, 0))
    copies = [
        pltpu.make_async_remote_copy(
            src_ref=src, dst_ref=dst, send_sem=send_sem.at[k], recv_sem=recv_sem.at[k],
            device_id=device(dx, dy), device_id_type=MESH,
        )
        for k, (src, dst, dx, dy) in enumerate(moves)
    ]
    for copy in copies:
        copy.start()
    for copy in copies:
        copy.wait()
    for i in range(8):
        for z in range(NZ):
            q[plane(XP[i], z, -1, 1), :] = xb[0, z, 32 + i : 33 + i, :]
            q[plane(XM[i], z, NX, 1), :] = xb[1, z, 32 + i : 33 + i, :]


def finish(q, xb, ao, yb, f_hbm, g_hbm, w, tr, res, uu, fo, go, out_sem):
    lane = lax.broadcasted_iota(jnp.int32, (8, NY), 1)
    lanes = lax.broadcasted_iota(jnp.int32, (NZ * RX, NY), 1)
    mine = (lanes >= 25) & (lanes < 40) & (lanes % 2 == 1)
    left = jnp.where(mine, ao[1], yb[0])
    right = jnp.where(mine, ao[0], yb[1])
    right = pltpu.roll(right, NY - 1, 1)
    turned = jnp.concatenate([left, right], axis=0).T[0:40]
    tr[0] = turned
    tr[1] = pltpu.roll(turned, 1, 1)
    tr[2] = pltpu.roll(turned, NY - 1, 1)
    ring = collide([tr[VEL[p][0] % 3, SLOT[p] : SLOT[p] + 1, :] for p in range(NPOP)])
    for k in range(8):
        for base, p in ((0, YP[k]), (8, YM[k])):
            uu[base + k : base + k + 1, :] = pltpu.roll(ring[p], VEL[p][0] % NY, 1)
    sides = uu[...].T

    def edge(side, cx):
        a = yb[side, pl.ds(PAD - 1 - cx, 2, stride=RX), :]
        b = yb[side, pl.ds(PAD + NX - cx, 2, stride=RX), :]
        return jnp.concatenate([a, b], axis=0)

    edges = {(side, cx): edge(side, cx) for side in range(2) for cx in (-1, 0, 1)}
    lane4 = lax.broadcasted_iota(jnp.int32, (4, NY), 1)

    def shift_y(p, value, beside, at, lane):
        if VEL[p][1] == 1:
            return jnp.where(lane == 0, pltpu.roll(beside, (NY - at) % NY, 1), pltpu.roll(value, 1, 1))
        if VEL[p][1] == -1:
            return jnp.where(lane == NY - 1, pltpu.roll(beside, NY - 1 - at, 1), pltpu.roll(value, NY - 1, 1))
        return value

    def kth(p):
        return YP.index(p) if VEL[p][1] == 1 else YM.index(p)

    rows = []
    for p in range(NPOP):
        value = xb[pl.ds(XOFF[p], 4, stride=48), :]
        if VEL[p][1]:
            value = shift_y(p, value, edges[0 if VEL[p][1] == 1 else 1, VEL[p][0]], 25 + 2 * kth(p), lane4)
        rows.append(value)
    ring = collide(rows)
    for p in range(NPOP):
        for z in range(NZ):
            zz = z ^ zflip(p)
            if VEL[p][0] == 1:
                w[plane(p, zz, -1, 1), :] = ring[p][z : z + 1]
            elif VEL[p][0] == -1:
                w[plane(p, zz, NX, 1), :] = ring[p][2 + z : 3 + z]

    for z in range(NZ):
        for half in range(2):
            pops = []
            for p in range(NPOP):
                start = 8 * half - VEL[p][0]
                value = q[plane(p, z, start), :]
                if VEL[p][1]:
                    first = z * RX + PAD + start
                    beside = yb[0 if VEL[p][1] == 1 else 1, first : first + 8, :]
                    value = shift_y(p, value, beside, 25 + 2 * kth(p), lane)
                pops.append(value)
            post = collide(pops)
            for p in range(NPOP):
                w[plane(p, z ^ zflip(p), 8 * half), :] = post[p]

    res[...] = sides
    for p in range(NPOP):
        for z in range(NZ):
            for half in range(2):
                value = w[plane(p, z, 8 * half - VEL[p][0]), :]
                if VEL[p][1]:
                    side, at = (0, kth(p)) if VEL[p][1] == 1 else (1, 8 + kth(p))
                    first = (side * NZ + (z ^ zflip(p))) * RX + PAD + 8 * half
                    value = shift_y(p, value, res[first : first + 8, :], at, lane)
                to = slice(8 * half, 8 * half + 8)
                if p < 19:
                    fo[p, z, to, :] = value
                else:
                    go[(p - 19) // 7, (p - 19) % 7, z, to, :] = value
    store_f = pltpu.make_async_copy(fo, f_hbm, out_sem.at[0])
    store_g = pltpu.make_async_copy(go, g_hbm, out_sem.at[1])
    store_f.start()
    store_g.start()
    store_f.wait()
    store_g.wait()


def per_device(sizes, fluid_pops, magnet_pops):
    vmem = pl.BlockSpec(memory_space=pltpu.VMEM)
    hbm = pl.BlockSpec(memory_space=pltpu.HBM)
    fluid, magnet = (19, NZ, NX, NY), (3, 7, NZ, NX, NY)
    halos = [
        pltpu.VMEM((NPOP * NZ * RX, NY), F32),
        pltpu.VMEM((2, NZ, 48, NY), F32),
        pltpu.VMEM((2, NZ, RX, NY), F32),
        pltpu.VMEM((2, NZ, RX, NY), F32),
    ]
    q, xb, ao, yb = pl.pallas_call(
        functools.partial(exchange, sizes),
        out_shape=halos,
        in_specs=[hbm] * 2,
        out_specs=[vmem] * 4,
        scratch_shapes=[
            pltpu.VMEM(fluid, F32),
            pltpu.VMEM(magnet, F32),
            pltpu.VMEM((2, NZ, 40, NY), F32),
            pltpu.SemaphoreType.DMA((2,)),
            pltpu.SemaphoreType.DMA((10,)),
            pltpu.SemaphoreType.DMA((10,)),
        ],
        compiler_params=pltpu.CompilerParams(
            collective_id=0, has_side_effects=True, vmem_limit_bytes=VMEM_LIMIT
        ),
    )(fluid_pops, magnet_pops)
    return pl.pallas_call(
        finish,
        out_shape=[jax.ShapeDtypeStruct(fluid, F32), jax.ShapeDtypeStruct(magnet, F32)],
        in_specs=[vmem] * 4,
        out_specs=[hbm] * 2,
        scratch_shapes=[
            pltpu.VMEM((NPOP * NZ * RX, NY), F32),
            pltpu.VMEM((3, 40, NY), F32),
            pltpu.VMEM((NY, NY), F32),
            pltpu.VMEM((NY, NY), F32),
            pltpu.VMEM(fluid, F32),
            pltpu.VMEM(magnet, F32),
            pltpu.SemaphoreType.DMA((2,)),
        ],
        compiler_params=pltpu.CompilerParams(vmem_limit_bytes=VMEM_LIMIT),
    )(
        q,
        xb.reshape(2 * NZ * 48, NY),
        ao.reshape(2, NZ * RX, NY),
        yb.reshape(2, NZ * RX, NY),
    )


VMEM_LIMIT = 48 << 20


def solution(mesh):
    specs = (P(None, None, "gx", "gy"), P(None, None, None, "gx", "gy"))
    return jax.shard_map(
        functools.partial(per_device, (mesh.shape["gx"], mesh.shape["gy"])),
        mesh=mesh,
        in_specs=specs,
        out_specs=specs,
        check_vma=False,
    )
```

```python
import functools

import jax
import jax.numpy as jnp
from jax import lax
from jax.experimental import pallas as pl
from jax.experimental.pallas import tpu as pltpu
from jax.sharding import PartitionSpec as P

MESH = pl.DeviceIdType.MESH
F32 = jnp.float32

FLUID = [
    (0, 0, 0),
    (1, 0, 0), (-1, 0, 0), (0, 1, 0), (0, -1, 0), (0, 0, 1), (0, 0, -1),
    (1, 1, 0), (-1, -1, 0), (1, -1, 0), (-1, 1, 0),
    (1, 0, 1), (-1, 0, -1), (1, 0, -1), (-1, 0, 1),
    (0, 1, 1), (0, -1, -1), (0, 1, -1), (0, -1, 1),
]
VEL = FLUID + FLUID[:7] * 3
NPOP = 40
OM_F = 1.0 / 0.9
OM_G = 1.0 / 0.8

XP = [p for p in range(NPOP) if VEL[p][0] == 1]
X0 = [p for p in range(NPOP) if VEL[p][0] == 0]
XM = [p for p in range(NPOP) if VEL[p][0] == -1]
ORDER = XP + X0 + XM
POS = {p: i for i, p in enumerate(ORDER)}
XOFF = {}
for i, p in enumerate(XP):
    XOFF[p] = i
for i, p in enumerate(X0):
    XOFF[p] = 8 + i
for i, p in enumerate(XM):
    XOFF[p] = 40 + i
YP = [p for p in range(NPOP) if VEL[p][1] == 1]
Y0 = [p for p in range(NPOP) if VEL[p][1] == 0]
YM = [p for p in range(NPOP) if VEL[p][1] == -1]
SLOT = {}
for i, p in enumerate(Y0):
    SLOT[p] = i
for i, p in enumerate(YP):
    SLOT[p] = 24 + 2 * i
for i, p in enumerate(YM):
    SLOT[p] = 25 + 2 * i
NX, NY, NZ = 16, 128, 2
PAD = 8
RX = NX + 2 * PAD


def zflip(p):
    return abs(VEL[p][2])


def plane(p, z, r, count=8):
    first = (POS[p] * NZ + z) * RX + PAD + r
    return slice(first, first + count)


def collide(pops):
    f, g = pops[:19], [pops[19 + 7 * a : 26 + 7 * a] for a in range(3)]
    pairs = [(i, i + 1) for i in range(1, 19, 2)]
    even = [f[i] + f[j] for i, j in pairs]
    odd = [f[i] - f[j] for i, j in pairs]
    rho = f[0] + ((even[0] + even[1]) + (even[2] + even[3])) + ((even[4] + even[5]) + ((even[6] + even[7]) + even[8]))
    mom = []
    for a in range(3):
        terms = [(odd[k], VEL[pairs[k][0]][a]) for k in range(9) if VEL[pairs[k][0]][a]]
        total = terms[0][0]
        for value, sign in terms[1:]:
            total = total + value if sign > 0 else total - value
        mom.append(total)
    inv = 1.0 / rho
    u = [m * inv for m in mom]
    b = [((g[a][0] + g[a][1]) + (g[a][2] + g[a][3])) + ((g[a][4] + g[a][5]) + g[a][6]) for a in range(3)]
    half = 0.5 * (b[0] * b[0] + b[1] * b[1] + b[2] * b[2])
    diag = [mom[a] * u[a] - b[a] * b[a] + half for a in range(3)]
    cross = {(a, c): mom[a] * u[c] - b[a] * b[c] for a, c in ((0, 1), (0, 2), (1, 2))}
    trace = diag[0] + diag[1] + diag[2]
    base = (OM_F / 36.0) * (rho - 1.5 * trace)
    d45 = [(4.5 * OM_F / 36.0) * d for d in diag]
    c9 = {k: (9.0 * OM_F / 36.0) * v for k, v in cross.items()}
    m3 = [(3.0 * OM_F / 36.0) * m for m in mom]
    keep = 1.0 - OM_F
    out = [None] * NPOP
    out[0] = keep * f[0] + 12.0 * base
    for k, (i, j) in enumerate(pairs):
        c = VEL[i]
        axes = [a for a in range(3) if c[a]]
        if len(axes) == 1:
            s = 2.0 * (base + d45[axes[0]])
            t = 2.0 * m3[axes[0]]
        else:
            a, d = axes
            s = base + d45[a] + d45[d]
            if c[a] * c[d] > 0:
                s = s + c9[(a, d)]
            else:
                s = s - c9[(a, d)]
            first = m3[a] if c[a] > 0 else -m3[a]
            t = first + m3[d] if c[d] > 0 else first - m3[d]
        out[i] = keep * f[i] + (s + t)
        out[j] = keep * f[j] + (s - t)
    keep = 1.0 - OM_G
    for a in range(3):
        rest = (OM_G / 8.0) * b[a]
        out[19 + 7 * a] = keep * g[a][0] + 2.0 * rest
        for d in range(3):
            plus, minus = rest, rest
            if d != a:
                flux = (4.0 * OM_G / 8.0) * (u[d] * b[a] - b[d] * u[a])
                plus, minus = rest + flux, rest - flux
            out[19 + 7 * a + 1 + 2 * d] = keep * g[a][1 + 2 * d] + plus
            out[19 + 7 * a + 2 + 2 * d] = keep * g[a][2 + 2 * d] + minus
    return out


def exchange(sizes, f_hbm, g_hbm, q, xb, ao, yb, fv, gv, xs, load_sem, send_sem, recv_sem, ready):
    nx_dev, ny_dev = sizes
    ix, iy = lax.axis_index("gx"), lax.axis_index("gy")

    def device(dx, dy):
        return (lax.rem(ix + dx + nx_dev, nx_dev), lax.rem(iy + dy + ny_dev, ny_dev))

    block = SEAM if ny_dev % SEAM == 0 else ny_dev
    place = lax.rem(iy, block)
    is_first, is_last, is_before = place == 0, place == block - 1, place == block - 2

    load_f = pltpu.make_async_copy(f_hbm, fv, load_sem.at[0])
    load_g = pltpu.make_async_copy(g_hbm, gv, load_sem.at[1])
    load_f.start()
    load_g.start()

    barrier = pltpu.get_barrier_semaphore()

    def greet(steps, semaphore):
        for dx, dy in steps:
            pl.semaphore_signal(semaphore, inc=1, device_id=device(dx, dy), device_id_type=MESH)

    beside = [(-1, 0), (1, 0)]
    above = [(-1, 1), (0, 1), (1, 1)]
    below = [(-1, -1), (0, -1), (1, -1)]

    @pl.when(is_last)
    def _():
        greet(below, barrier)
        pl.semaphore_wait(barrier, 3)
        greet(above, ready)

    @pl.when(jnp.logical_not(is_last))
    def _():
        greet(below + beside, barrier)

        @pl.when(jnp.logical_not(is_before))
        def _():
            greet(above, barrier)

    load_f.wait()
    load_g.wait()

    lane = lax.broadcasted_iota(jnp.int32, (8, NY), 1)
    for half in range(2):
        rows = slice(8 * half, 8 * half + 8)
        at = slice(PAD + 8 * half, PAD + 8 * half + 8)
        up = [jnp.zeros((8, NY), F32) for _ in range(NZ)]
        down = [jnp.zeros((8, NY), F32) for _ in range(NZ)]
        for z in range(NZ):
            pops = [fv[p, z, rows, :] for p in range(19)]
            pops += [gv[a, j, z, rows, :] for a in range(3) for j in range(7)]
            post = collide(pops)
            for p in range(NPOP):
                zz = z ^ zflip(p)
                q[plane(p, zz, 8 * half), :] = post[p]
                s = SLOT[p]
                if VEL[p][1] == 0:
                    moved = pltpu.roll(post[p], s + 1, 1)
                    up[zz] = jnp.where(lane == s, moved, up[zz])
                    down[zz] = jnp.where(lane == s + 1, moved, down[zz])
                elif VEL[p][1] == 1:
                    moved = pltpu.roll(post[p], s + 2, 1)
                    up[zz] = jnp.where((lane == s) | (lane == s + 1), moved, up[zz])
                else:
                    moved = pltpu.roll(post[p], s, 1)
                    down[zz] = jnp.where((lane == s) | (lane == s + 1), moved, down[zz])
        for z in range(NZ):
            ao[0, z, at, :] = up[z]
            ao[1, z, at, :] = down[z]

    low, high, own = slice(0, 8), slice(24, 32), slice(8, 24)
    first, last = slice(8, 16), slice(16, 24)
    slots = iter(range(10))

    def to(src, dst, dx, dy):
        k = next(slots)
        return pltpu.make_async_remote_copy(
            src_ref=src, dst_ref=dst, send_sem=send_sem.at[k], recv_sem=recv_sem.at[k],
            device_id=device(dx, dy), device_id_type=MESH,
        )

    def to_row(side, dy):
        return [
            to(ao.at[side, :, last], yb.at[side, :, low], 1, dy),
            to(ao.at[side, :, first], yb.at[side, :, high], -1, dy),
            to(ao.at[side, :, own], yb.at[side, :, own], 0, dy),
        ]

    to_above = to_row(0, 1)
    to_below = to_row(1, -1)
    to_beside = [
        to(xs.at[0], xb.at[0, :, 0:40], 1, 0),
        to(xs.at[1], xb.at[1, :, 8:48], -1, 0),
        to(ao.at[:, :, last], ao.at[:, :, low], 1, 0),
        to(ao.at[:, :, first], ao.at[:, :, high], -1, 0),
    ]

    def start(copies):
        for copy in copies:
            copy.start()

    @pl.when(is_first)
    def _():
        pl.semaphore_wait(barrier, 5)

    @pl.when(jnp.logical_not(is_first | is_last))
    def _():
        pl.semaphore_wait(barrier, 8)

    @pl.when(is_before)
    def _():
        greet([(0, 1)], ready)

    start(to_above)

    def row(first, count, z, r):
        return q[pl.ds(first * NZ * RX + z * RX + PAD + r, count, stride=NZ * RX), :]

    for z in range(NZ):
        xs[0, z, 0:8, :] = row(0, 8, z, NX - 2)
        xs[0, z, 8:32, :] = row(8, 24, z, NX - 1)
        xs[0, z, 32:40, :] = row(0, 8, z, NX - 1)
        xs[1, z, 0:24, :] = row(8, 24, z, 0)
        xs[1, z, 24:32, :] = row(32, 8, z, 0)
        xs[1, z, 32:40, :] = row(32, 8, z, 1)
        xb[0, z, 40:48, :] = row(32, 8, z, 0)
        xb[1, z, 0:8, :] = row(0, 8, z, NX - 1)

    @pl.when(jnp.logical_not(is_last))
    def _():
        start(to_beside)

    @pl.when(is_first)
    def _():
        pl.semaphore_wait(ready, 3)

    @pl.when(is_last)
    def _():
        pl.semaphore_wait(ready, 1)
        start(to_beside)

    start(to_below)
    for copy in to_above + to_below + to_beside:
        copy.wait()
    for i in range(8):
        for z in range(NZ):
            q[plane(XP[i], z, -1, 1), :] = xb[0, z, 32 + i : 33 + i, :]
            q[plane(XM[i], z, NX, 1), :] = xb[1, z, 32 + i : 33 + i, :]


def finish(q, xb, ao, yb, f_hbm, g_hbm, w, tr, res, uu, fo, go, out_sem):
    lane = lax.broadcasted_iota(jnp.int32, (8, NY), 1)
    lanes = lax.broadcasted_iota(jnp.int32, (NZ * RX, NY), 1)
    mine = (lanes >= 25) & (lanes < 40) & (lanes % 2 == 1)
    left = jnp.where(mine, ao[1], yb[0])
    right = jnp.where(mine, ao[0], yb[1])
    right = pltpu.roll(right, NY - 1, 1)
    turned = jnp.concatenate([left, right], axis=0).T[0:40]
    tr[0] = turned
    tr[1] = pltpu.roll(turned, 1, 1)
    tr[2] = pltpu.roll(turned, NY - 1, 1)
    ring = collide([tr[VEL[p][0] % 3, SLOT[p] : SLOT[p] + 1, :] for p in range(NPOP)])
    for k in range(8):
        for base, p in ((0, YP[k]), (8, YM[k])):
            uu[base + k : base + k + 1, :] = pltpu.roll(ring[p], VEL[p][0] % NY, 1)
    sides = uu[...].T

    def edge(side, cx):
        a = yb[side, pl.ds(PAD - 1 - cx, 2, stride=RX), :]
        b = yb[side, pl.ds(PAD + NX - cx, 2, stride=RX), :]
        return jnp.concatenate([a, b], axis=0)

    edges = {(side, cx): edge(side, cx) for side in range(2) for cx in (-1, 0, 1)}
    lane4 = lax.broadcasted_iota(jnp.int32, (4, NY), 1)

    def shift_y(p, value, beside, at, lane):
        if VEL[p][1] == 1:
            return jnp.where(lane == 0, pltpu.roll(beside, (NY - at) % NY, 1), pltpu.roll(value, 1, 1))
        if VEL[p][1] == -1:
            return jnp.where(lane == NY - 1, pltpu.roll(beside, NY - 1 - at, 1), pltpu.roll(value, NY - 1, 1))
        return value

    def kth(p):
        return YP.index(p) if VEL[p][1] == 1 else YM.index(p)

    rows = []
    for p in range(NPOP):
        value = xb[pl.ds(XOFF[p], 4, stride=48), :]
        if VEL[p][1]:
            value = shift_y(p, value, edges[0 if VEL[p][1] == 1 else 1, VEL[p][0]], 25 + 2 * kth(p), lane4)
        rows.append(value)
    ring = collide(rows)
    for p in range(NPOP):
        for z in range(NZ):
            zz = z ^ zflip(p)
            if VEL[p][0] == 1:
                w[plane(p, zz, -1, 1), :] = ring[p][z : z + 1]
            elif VEL[p][0] == -1:
                w[plane(p, zz, NX, 1), :] = ring[p][2 + z : 3 + z]

    for z in range(NZ):
        for half in range(2):
            pops = []
            for p in range(NPOP):
                start = 8 * half - VEL[p][0]
                value = q[plane(p, z, start), :]
                if VEL[p][1]:
                    first = z * RX + PAD + start
                    beside = yb[0 if VEL[p][1] == 1 else 1, first : first + 8, :]
                    value = shift_y(p, value, beside, 25 + 2 * kth(p), lane)
                pops.append(value)
            post = collide(pops)
            for p in range(NPOP):
                w[plane(p, z ^ zflip(p), 8 * half), :] = post[p]

    res[...] = sides
    for p in range(NPOP):
        for z in range(NZ):
            for half in range(2):
                value = w[plane(p, z, 8 * half - VEL[p][0]), :]
                if VEL[p][1]:
                    side, at = (0, kth(p)) if VEL[p][1] == 1 else (1, 8 + kth(p))
                    first = (side * NZ + (z ^ zflip(p))) * RX + PAD + 8 * half
                    value = shift_y(p, value, res[first : first + 8, :], at, lane)
                to = slice(8 * half, 8 * half + 8)
                if p < 19:
                    fo[p, z, to, :] = value
                else:
                    go[(p - 19) // 7, (p - 19) % 7, z, to, :] = value
    store_f = pltpu.make_async_copy(fo, f_hbm, out_sem.at[0])
    store_g = pltpu.make_async_copy(go, g_hbm, out_sem.at[1])
    store_f.start()
    store_g.start()
    store_f.wait()
    store_g.wait()


def per_device(sizes, fluid_pops, magnet_pops):
    vmem = pl.BlockSpec(memory_space=pltpu.VMEM)
    hbm = pl.BlockSpec(memory_space=pltpu.HBM)
    fluid, magnet = (19, NZ, NX, NY), (3, 7, NZ, NX, NY)
    halos = [
        pltpu.VMEM((NPOP * NZ * RX, NY), F32),
        pltpu.VMEM((2, NZ, 48, NY), F32),
        pltpu.VMEM((2, NZ, RX, NY), F32),
        pltpu.VMEM((2, NZ, RX, NY), F32),
    ]
    q, xb, ao, yb = pl.pallas_call(
        functools.partial(exchange, sizes),
        out_shape=halos,
        in_specs=[hbm] * 2,
        out_specs=[vmem] * 4,
        scratch_shapes=[
            pltpu.VMEM(fluid, F32),
            pltpu.VMEM(magnet, F32),
            pltpu.VMEM((2, NZ, 40, NY), F32),
            pltpu.SemaphoreType.DMA((2,)),
            pltpu.SemaphoreType.DMA((10,)),
            pltpu.SemaphoreType.DMA((10,)),
            pltpu.SemaphoreType.REGULAR,
        ],
        compiler_params=pltpu.CompilerParams(
            collective_id=0, has_side_effects=True, vmem_limit_bytes=VMEM_LIMIT
        ),
    )(
        pltpu.with_memory_space_constraint(fluid_pops, pltpu.HBM),
        pltpu.with_memory_space_constraint(magnet_pops, pltpu.HBM),
    )
    return pl.pallas_call(
        finish,
        out_shape=[jax.ShapeDtypeStruct(fluid, F32), jax.ShapeDtypeStruct(magnet, F32)],
        in_specs=[vmem] * 4,
        out_specs=[hbm] * 2,
        scratch_shapes=[
            pltpu.VMEM((NPOP * NZ * RX, NY), F32),
            pltpu.VMEM((3, 40, NY), F32),
            pltpu.VMEM((NY, NY), F32),
            pltpu.VMEM((NY, NY), F32),
            pltpu.VMEM(fluid, F32),
            pltpu.VMEM(magnet, F32),
            pltpu.SemaphoreType.DMA((2,)),
        ],
        compiler_params=pltpu.CompilerParams(vmem_limit_bytes=VMEM_LIMIT),
    )(
        q,
        xb.reshape(2 * NZ * 48, NY),
        ao.reshape(2, NZ * RX, NY),
        yb.reshape(2, NZ * RX, NY),
    )


VMEM_LIMIT = 48 << 20
SEAM = 16


def solution(mesh):
    specs = (P(None, None, "gx", "gy"), P(None, None, None, "gx", "gy"))
    return jax.shard_map(
        functools.partial(per_device, (mesh.shape["gx"], mesh.shape["gy"])),
        mesh=mesh,
        in_specs=specs,
        out_specs=specs,
        check_vma=False,
    )
```

```python
import functools

import jax
import jax.numpy as jnp
from jax import lax
from jax.experimental import pallas as pl
from jax.experimental.pallas import tpu as pltpu
from jax.sharding import PartitionSpec as P

MESH = pl.DeviceIdType.MESH
F32 = jnp.float32

FLUID = [
    (0, 0, 0),
    (1, 0, 0), (-1, 0, 0), (0, 1, 0), (0, -1, 0), (0, 0, 1), (0, 0, -1),
    (1, 1, 0), (-1, -1, 0), (1, -1, 0), (-1, 1, 0),
    (1, 0, 1), (-1, 0, -1), (1, 0, -1), (-1, 0, 1),
    (0, 1, 1), (0, -1, -1), (0, 1, -1), (0, -1, 1),
]
VEL = FLUID + FLUID[:7] * 3
NPOP = 40
OM_F = 1.0 / 0.9
OM_G = 1.0 / 0.8

XP = [p for p in range(NPOP) if VEL[p][0] == 1]
X0 = [p for p in range(NPOP) if VEL[p][0] == 0]
XM = [p for p in range(NPOP) if VEL[p][0] == -1]
ORDER = XP + X0 + XM
POS = {p: i for i, p in enumerate(ORDER)}
XOFF = {}
for i, p in enumerate(XP):
    XOFF[p] = i
for i, p in enumerate(X0):
    XOFF[p] = 8 + i
for i, p in enumerate(XM):
    XOFF[p] = 40 + i
YP = [p for p in range(NPOP) if VEL[p][1] == 1]
Y0 = [p for p in range(NPOP) if VEL[p][1] == 0]
YM = [p for p in range(NPOP) if VEL[p][1] == -1]
SLOT = {}
for i, p in enumerate(Y0):
    SLOT[p] = i
for i, p in enumerate(YP):
    SLOT[p] = 24 + 2 * i
for i, p in enumerate(YM):
    SLOT[p] = 25 + 2 * i
NX, NY, NZ = 16, 128, 2
PAD = 8
RX = NX + 2 * PAD


def zflip(p):
    return abs(VEL[p][2])


def plane(p, z, r, count=8):
    first = (POS[p] * NZ + z) * RX + PAD + r
    return slice(first, first + count)


def collide(pops):
    f, g = pops[:19], [pops[19 + 7 * a : 26 + 7 * a] for a in range(3)]
    pairs = [(i, i + 1) for i in range(1, 19, 2)]
    even = [f[i] + f[j] for i, j in pairs]
    odd = [f[i] - f[j] for i, j in pairs]
    rho = f[0] + ((even[0] + even[1]) + (even[2] + even[3])) + ((even[4] + even[5]) + ((even[6] + even[7]) + even[8]))
    mom = []
    for a in range(3):
        terms = [(odd[k], VEL[pairs[k][0]][a]) for k in range(9) if VEL[pairs[k][0]][a]]
        total = terms[0][0]
        for value, sign in terms[1:]:
            total = total + value if sign > 0 else total - value
        mom.append(total)
    inv = 1.0 / rho
    u = [m * inv for m in mom]
    b = [((g[a][0] + g[a][1]) + (g[a][2] + g[a][3])) + ((g[a][4] + g[a][5]) + g[a][6]) for a in range(3)]
    half = 0.5 * (b[0] * b[0] + b[1] * b[1] + b[2] * b[2])
    diag = [mom[a] * u[a] - b[a] * b[a] + half for a in range(3)]
    cross = {(a, c): mom[a] * u[c] - b[a] * b[c] for a, c in ((0, 1), (0, 2), (1, 2))}
    trace = diag[0] + diag[1] + diag[2]
    base = (OM_F / 36.0) * (rho - 1.5 * trace)
    d45 = [(4.5 * OM_F / 36.0) * d for d in diag]
    c9 = {k: (9.0 * OM_F / 36.0) * v for k, v in cross.items()}
    m3 = [(3.0 * OM_F / 36.0) * m for m in mom]
    keep = 1.0 - OM_F
    out = [None] * NPOP
    out[0] = keep * f[0] + 12.0 * base
    for k, (i, j) in enumerate(pairs):
        c = VEL[i]
        axes = [a for a in range(3) if c[a]]
        if len(axes) == 1:
            s = 2.0 * (base + d45[axes[0]])
            t = 2.0 * m3[axes[0]]
        else:
            a, d = axes
            s = base + d45[a] + d45[d]
            if c[a] * c[d] > 0:
                s = s + c9[(a, d)]
            else:
                s = s - c9[(a, d)]
            first = m3[a] if c[a] > 0 else -m3[a]
            t = first + m3[d] if c[d] > 0 else first - m3[d]
        out[i] = keep * f[i] + (s + t)
        out[j] = keep * f[j] + (s - t)
    keep = 1.0 - OM_G
    for a in range(3):
        rest = (OM_G / 8.0) * b[a]
        out[19 + 7 * a] = keep * g[a][0] + 2.0 * rest
        for d in range(3):
            plus, minus = rest, rest
            if d != a:
                flux = (4.0 * OM_G / 8.0) * (u[d] * b[a] - b[d] * u[a])
                plus, minus = rest + flux, rest - flux
            out[19 + 7 * a + 1 + 2 * d] = keep * g[a][1 + 2 * d] + plus
            out[19 + 7 * a + 2 + 2 * d] = keep * g[a][2 + 2 * d] + minus
    return out


def exchange(sizes, f_hbm, g_hbm, fo, go, ao, yb, fv, gv, q, w, xs, xb, load_sem, send_sem, recv_sem, ready):
    nx_dev, ny_dev = sizes
    ix, iy = lax.axis_index("gx"), lax.axis_index("gy")

    def device(dx, dy):
        return (lax.rem(ix + dx + nx_dev, nx_dev), lax.rem(iy + dy + ny_dev, ny_dev))

    block = SEAM if ny_dev % SEAM == 0 else ny_dev
    place = lax.rem(iy, block)
    is_first, is_last, is_before = place == 0, place == block - 1, place == block - 2

    loads = []
    for half in range(2):
        for z in range(NZ):
            rows = slice(8 * half, 8 * half + 8)
            piece = (
                pltpu.make_async_copy(f_hbm.at[:, z, rows], fv.at[:, z, rows], load_sem.at[half, z, 0]),
                pltpu.make_async_copy(g_hbm.at[:, :, z, rows], gv.at[:, :, z, rows], load_sem.at[half, z, 1]),
            )
            loads.append(piece)
            for copy in piece:
                copy.start()

    barrier = pltpu.get_barrier_semaphore()

    def greet(steps, semaphore):
        for dx, dy in steps:
            pl.semaphore_signal(semaphore, inc=1, device_id=device(dx, dy), device_id_type=MESH)

    beside = [(-1, 0), (1, 0)]
    above = [(-1, 1), (0, 1), (1, 1)]
    below = [(-1, -1), (0, -1), (1, -1)]

    @pl.when(is_last)
    def _():
        greet(below, barrier)
        pl.semaphore_wait(barrier, 3)
        greet(above, ready)

    @pl.when(jnp.logical_not(is_last))
    def _():
        greet(below + beside, barrier)

        @pl.when(jnp.logical_not(is_before))
        def _():
            greet(above, barrier)

    low, high, own = slice(0, 8), slice(24, 32), slice(8, 24)
    first, last = slice(8, 16), slice(16, 24)
    slots = iter(range(10))

    def to(src, dst, dx, dy):
        k = next(slots)
        return pltpu.make_async_remote_copy(
            src_ref=src, dst_ref=dst, send_sem=send_sem.at[k], recv_sem=recv_sem.at[k],
            device_id=device(dx, dy), device_id_type=MESH,
        )

    def to_row(side, dy):
        return [
            to(ao.at[:, first], yb.at[side, :, high], -1, dy),
            to(ao.at[:, last], yb.at[side, :, low], 1, dy),
            to(ao.at[:, own], yb.at[side, :, own], 0, dy),
        ]

    to_above = to_row(0, 1)
    to_below = to_row(1, -1)
    to_beside = [
        to(xs.at[0], xb.at[0, :, 0:40], 1, 0),
        to(xs.at[1], xb.at[1, :, 8:48], -1, 0),
        to(ao.at[:, last], ao.at[:, low], 1, 0),
        to(ao.at[:, first], ao.at[:, high], -1, 0),
    ]

    def start(copies):
        for copy in copies:
            copy.start()

    lane = lax.broadcasted_iota(jnp.int32, (8, NY), 1)
    for half in range(2):
        rows = slice(8 * half, 8 * half + 8)
        at = slice(PAD + 8 * half, PAD + 8 * half + 8)
        up = [jnp.zeros((8, NY), F32) for _ in range(NZ)]
        down = [jnp.zeros((8, NY), F32) for _ in range(NZ)]
        for z in range(NZ):
            for copy in loads[half * NZ + z]:
                copy.wait()
            pops = [fv[p, z, rows, :] for p in range(19)]
            pops += [gv[a, j, z, rows, :] for a in range(3) for j in range(7)]
            post = collide(pops)
            for p in range(NPOP):
                zz = z ^ zflip(p)
                q[plane(p, zz, 8 * half), :] = post[p]
                s = SLOT[p]
                if VEL[p][1] == 0:
                    moved = pltpu.roll(post[p], s + 1, 1)
                    up[zz] = jnp.where(lane == s, moved, up[zz])
                    down[zz] = jnp.where(lane == s + 1, moved, down[zz])
                elif VEL[p][1] == 1:
                    moved = pltpu.roll(post[p], s + 2, 1)
                    up[zz] = jnp.where((lane == s) | (lane == s + 1), moved, up[zz])
                else:
                    moved = pltpu.roll(post[p], s, 1)
                    down[zz] = jnp.where((lane == s) | (lane == s + 1), moved, down[zz])
        for z in range(NZ):
            here = jnp.where((lane < 24) | ((lane < 40) & (lane % 2 == 0)), up[z], down[z])
            there = jnp.where((lane >= 25) & (lane < 40) & (lane % 2 == 1), up[z], down[z])
            ao[z, at, :] = jnp.where(lane < 64, here, pltpu.roll(there, 63, 1))
        if half == 0:

            @pl.when(is_last)
            def _():
                start(to_above[:1])

    @pl.when(is_first)
    def _():
        pl.semaphore_wait(barrier, 5)

    @pl.when(jnp.logical_not(is_first | is_last))
    def _():
        pl.semaphore_wait(barrier, 8)

    @pl.when(is_before)
    def _():
        greet([(0, 1)], ready)

    @pl.when(jnp.logical_not(is_last))
    def _():
        start(to_above[:1])

    start(to_above[1:])

    def row(first, count, z, r):
        return q[pl.ds(first * NZ * RX + z * RX + PAD + r, count, stride=NZ * RX), :]

    for z in range(NZ):
        xs[0, z, 0:8, :] = row(0, 8, z, NX - 2)
        xs[0, z, 8:32, :] = row(8, 24, z, NX - 1)
        xs[0, z, 32:40, :] = row(0, 8, z, NX - 1)
        xs[1, z, 0:24, :] = row(8, 24, z, 0)
        xs[1, z, 24:32, :] = row(32, 8, z, 0)
        xs[1, z, 32:40, :] = row(32, 8, z, 1)
        xb[0, z, 40:48, :] = row(32, 8, z, 0)
        xb[1, z, 0:8, :] = row(0, 8, z, NX - 1)

    @pl.when(is_last)
    def _():
        pl.semaphore_wait(ready, 1)

    start(to_beside)

    @pl.when(jnp.logical_not(is_first))
    def _():
        start(to_below)

    for copy in to_beside:
        copy.wait()

    def turn(p, value):
        return pltpu.roll(value, VEL[p][1] % NY, 1) if VEL[p][1] else value

    for i in range(8):
        for z in range(NZ):
            q[plane(XP[i], z, -1, 1), :] = xb[0, z, 32 + i : 33 + i, :]
            q[plane(XM[i], z, NX, 1), :] = xb[1, z, 32 + i : 33 + i, :]
    edges = []
    for p in range(NPOP):
        at = slice(XOFF[p], XOFF[p] + 1)
        edges.append(turn(p, jnp.concatenate([xb[side, z, at, :] for side in range(2) for z in range(NZ)], axis=0)))
    edges = collide(edges)
    for p in range(NPOP):
        for z in range(NZ):
            zz = z ^ zflip(p)
            if VEL[p][0] == 1:
                w[plane(p, zz, -1, 1), :] = edges[p][z : z + 1]
            elif VEL[p][0] == -1:
                w[plane(p, zz, NX, 1), :] = edges[p][NZ + z : NZ + z + 1]
    for z in range(NZ):
        for half in range(2):
            post = collide([turn(p, q[plane(p, z, 8 * half - VEL[p][0]), :]) for p in range(NPOP)])
            for p in range(NPOP):
                w[plane(p, z ^ zflip(p), 8 * half), :] = post[p]
    for p in range(NPOP):
        for z in range(NZ):
            for half in range(2):
                value = turn(p, w[plane(p, z, 8 * half - VEL[p][0]), :])
                rows = slice(8 * half, 8 * half + 8)
                if p < 19:
                    fo[p, z, rows, :] = value
                else:
                    go[(p - 19) // 7, (p - 19) % 7, z, rows, :] = value

    @pl.when(is_first)
    def _():
        pl.semaphore_wait(ready, 3)
        start(to_below)

    for copy in to_above + to_below:
        copy.wait()


def finish(fi, gi, ao, yb, f_hbm, g_hbm, tr, uu, mg, fo, go, out_sem):
    lane = lax.broadcasted_iota(jnp.int32, (NZ * RX, NY), 1)
    near_right = (lane < 24) | (((lane < 40) | ((lane >= 88) & (lane < 104))) & (lane % 2 == 0))
    tr[0:NY, 0 : NZ * RX] = jnp.where(near_right, yb[0], ao[...]).T
    tr[NY:, 0 : NZ * RX] = jnp.where(near_right, ao[...], yb[1]).T

    def turn(p, value):
        return pltpu.roll(value, VEL[p][0] % NY, 1) if VEL[p][0] else value

    post = collide([turn(p, tr[pl.ds(SLOT[p], 4, stride=64), :]) for p in range(NPOP)])
    shift = {}
    for p in range(NPOP):
        if VEL[p][1] == 0:
            s = 2 * SLOT[p]
            uu[s : s + 1, :] = post[p][2:3]
            uu[s + 1 : s + 2, :] = post[p][1:2]
            shift[p] = NY - 1 - s
        elif VEL[p][1] == 1:
            s = 48 + (SLOT[p] - 24)
            uu[s : s + 2, :] = post[p][0:2]
            shift[p] = NY - s
        else:
            s = 64 + (SLOT[p] - 25)
            uu[s : s + 2, :] = post[p][2:4]
            shift[p] = NY - 2 - s
    mg[...] = uu[:, 0 : NZ * RX].T
    lane = lax.broadcasted_iota(jnp.int32, (8, NY), 1)
    masks = {0: (lane == 0) | (lane == NY - 1), 1: lane < 2, -1: lane >= NY - 2}
    stores = [
        (9, fo.at[0:10], f_hbm.at[0:10]),
        (18, fo.at[10:19], f_hbm.at[10:19]),
        (25, go.at[0], g_hbm.at[0]),
        (32, go.at[1], g_hbm.at[1]),
        (39, go.at[2], g_hbm.at[2]),
    ]
    copies = []
    for p in range(NPOP):
        for z in range(NZ):
            for half in range(2):
                start = (z ^ zflip(p)) * RX + PAD + 8 * half - VEL[p][0]
                patch = pltpu.roll(mg[start : start + 8, :], shift[p], 1)
                rows = slice(8 * half, 8 * half + 8)
                if p < 19:
                    fo[p, z, rows, :] = jnp.where(masks[VEL[p][1]], patch, fi[p, z, rows, :])
                else:
                    a, j = (p - 19) // 7, (p - 19) % 7
                    go[a, j, z, rows, :] = jnp.where(masks[VEL[p][1]], patch, gi[a, j, z, rows, :])
        for k, (after, src, dst) in enumerate(stores):
            if after == p:
                copies.append(pltpu.make_async_copy(src, dst, out_sem.at[k]))
                copies[-1].start()
    for copy in copies:
        copy.wait()


def per_device(sizes, fluid_pops, magnet_pops):
    vmem = pl.BlockSpec(memory_space=pltpu.VMEM)
    hbm = pl.BlockSpec(memory_space=pltpu.HBM)
    fluid, magnet = (19, NZ, NX, NY), (3, 7, NZ, NX, NY)
    columns = (NZ, RX, NY)
    fo, go, ao, yb = pl.pallas_call(
        functools.partial(exchange, sizes),
        out_shape=[pltpu.VMEM(shape, F32) for shape in (fluid, magnet, columns, (2, *columns))],
        in_specs=[hbm] * 2,
        out_specs=[vmem] * 4,
        scratch_shapes=[
            pltpu.VMEM(fluid, F32),
            pltpu.VMEM(magnet, F32),
            pltpu.VMEM((NPOP * NZ * RX, NY), F32),
            pltpu.VMEM((NPOP * NZ * RX, NY), F32),
            pltpu.VMEM((2, NZ, 40, NY), F32),
            pltpu.VMEM((2, NZ, 48, NY), F32),
            pltpu.SemaphoreType.DMA((2, NZ, 2)),
            pltpu.SemaphoreType.DMA((10,)),
            pltpu.SemaphoreType.DMA((10,)),
            pltpu.SemaphoreType.REGULAR,
        ],
        compiler_params=pltpu.CompilerParams(
            collective_id=0, has_side_effects=True, vmem_limit_bytes=VMEM_LIMIT
        ),
    )(
        pltpu.with_memory_space_constraint(fluid_pops, pltpu.HBM),
        pltpu.with_memory_space_constraint(magnet_pops, pltpu.HBM),
    )
    return pl.pallas_call(
        finish,
        out_shape=[jax.ShapeDtypeStruct(fluid, F32), jax.ShapeDtypeStruct(magnet, F32)],
        in_specs=[vmem] * 4,
        out_specs=[hbm] * 2,
        scratch_shapes=[
            pltpu.VMEM((2 * NY, NY), F32),
            pltpu.VMEM((NY, NY), F32),
            pltpu.VMEM((NZ * RX, NY), F32),
            pltpu.VMEM(fluid, F32),
            pltpu.VMEM(magnet, F32),
            pltpu.SemaphoreType.DMA((5,)),
        ],
        compiler_params=pltpu.CompilerParams(vmem_limit_bytes=VMEM_LIMIT),
    )(fo, go, ao.reshape(NZ * RX, NY), yb.reshape(2, NZ * RX, NY))


VMEM_LIMIT = 48 << 20
SEAM = 16


def solution(mesh):
    specs = (P(None, None, "gx", "gy"), P(None, None, None, "gx", "gy"))
    return jax.shard_map(
        functools.partial(per_device, (mesh.shape["gx"], mesh.shape["gy"])),
        mesh=mesh,
        in_specs=specs,
        out_specs=specs,
        check_vma=False,
    )
```

```python
import functools

import jax
import jax.numpy as jnp
from jax import lax
from jax.experimental import pallas as pl
from jax.experimental.pallas import tpu as pltpu
from jax.sharding import PartitionSpec as P

MESH = pl.DeviceIdType.MESH
F32 = jnp.float32

FLUID = [
    (0, 0, 0),
    (1, 0, 0), (-1, 0, 0), (0, 1, 0), (0, -1, 0), (0, 0, 1), (0, 0, -1),
    (1, 1, 0), (-1, -1, 0), (1, -1, 0), (-1, 1, 0),
    (1, 0, 1), (-1, 0, -1), (1, 0, -1), (-1, 0, 1),
    (0, 1, 1), (0, -1, -1), (0, 1, -1), (0, -1, 1),
]
VEL = FLUID + FLUID[:7] * 3
NPOP = 40
OM_F = 1.0 / 0.9
OM_G = 1.0 / 0.8

XP = [p for p in range(NPOP) if VEL[p][0] == 1]
X0 = [p for p in range(NPOP) if VEL[p][0] == 0]
XM = [p for p in range(NPOP) if VEL[p][0] == -1]
ORDER = XP + X0 + XM
POS = {p: i for i, p in enumerate(ORDER)}
XOFF = {}
for i, p in enumerate(XP):
    XOFF[p] = i
for i, p in enumerate(X0):
    XOFF[p] = 8 + i
for i, p in enumerate(XM):
    XOFF[p] = 40 + i
YP = [p for p in range(NPOP) if VEL[p][1] == 1]
Y0 = [p for p in range(NPOP) if VEL[p][1] == 0]
YM = [p for p in range(NPOP) if VEL[p][1] == -1]
SLOT = {}
for i, p in enumerate(Y0):
    SLOT[p] = i
for i, p in enumerate(YP):
    SLOT[p] = 24 + 2 * i
for i, p in enumerate(YM):
    SLOT[p] = 25 + 2 * i
NX, NY, NZ = 16, 128, 2
PAD = 8
RX = NX + 2 * PAD


def zflip(p):
    return abs(VEL[p][2])


def plane(p, z, r, count=8):
    first = (POS[p] * NZ + z) * RX + PAD + r
    return slice(first, first + count)


def collide(pops):
    f, g = pops[:19], [pops[19 + 7 * a : 26 + 7 * a] for a in range(3)]
    pairs = [(i, i + 1) for i in range(1, 19, 2)]
    even = [f[i] + f[j] for i, j in pairs]
    odd = [f[i] - f[j] for i, j in pairs]
    rho = f[0] + ((even[0] + even[1]) + (even[2] + even[3])) + ((even[4] + even[5]) + ((even[6] + even[7]) + even[8]))
    mom = []
    for a in range(3):
        terms = [(odd[k], VEL[pairs[k][0]][a]) for k in range(9) if VEL[pairs[k][0]][a]]
        total = terms[0][0]
        for value, sign in terms[1:]:
            total = total + value if sign > 0 else total - value
        mom.append(total)
    inv = 1.0 / rho
    u = [m * inv for m in mom]
    b = [((g[a][0] + g[a][1]) + (g[a][2] + g[a][3])) + ((g[a][4] + g[a][5]) + g[a][6]) for a in range(3)]
    half = 0.5 * (b[0] * b[0] + b[1] * b[1] + b[2] * b[2])
    diag = [mom[a] * u[a] - b[a] * b[a] + half for a in range(3)]
    cross = {(a, c): mom[a] * u[c] - b[a] * b[c] for a, c in ((0, 1), (0, 2), (1, 2))}
    trace = diag[0] + diag[1] + diag[2]
    base = (OM_F / 36.0) * (rho - 1.5 * trace)
    d45 = [(4.5 * OM_F / 36.0) * d for d in diag]
    c9 = {k: (9.0 * OM_F / 36.0) * v for k, v in cross.items()}
    m3 = [(3.0 * OM_F / 36.0) * m for m in mom]
    keep = 1.0 - OM_F
    out = [None] * NPOP
    out[0] = keep * f[0] + 12.0 * base
    for k, (i, j) in enumerate(pairs):
        c = VEL[i]
        axes = [a for a in range(3) if c[a]]
        if len(axes) == 1:
            s = 2.0 * (base + d45[axes[0]])
            t = 2.0 * m3[axes[0]]
        else:
            a, d = axes
            s = base + d45[a] + d45[d]
            if c[a] * c[d] > 0:
                s = s + c9[(a, d)]
            else:
                s = s - c9[(a, d)]
            first = m3[a] if c[a] > 0 else -m3[a]
            t = first + m3[d] if c[d] > 0 else first - m3[d]
        out[i] = keep * f[i] + (s + t)
        out[j] = keep * f[j] + (s - t)
    keep = 1.0 - OM_G
    for a in range(3):
        rest = (OM_G / 8.0) * b[a]
        out[19 + 7 * a] = keep * g[a][0] + 2.0 * rest
        for d in range(3):
            plus, minus = rest, rest
            if d != a:
                flux = (4.0 * OM_G / 8.0) * (u[d] * b[a] - b[d] * u[a])
                plus, minus = rest + flux, rest - flux
            out[19 + 7 * a + 1 + 2 * d] = keep * g[a][1 + 2 * d] + plus
            out[19 + 7 * a + 2 + 2 * d] = keep * g[a][2 + 2 * d] + minus
    return out


def edge_rows(block, leading, tr, uu, mg):
    tr[:, 0 : NZ * RX] = block.T

    def turn(p, value):
        return pltpu.roll(value, VEL[p][0] % NY, 1) if VEL[p][0] else value

    post = collide([turn(p, tr[pl.ds(SLOT[p], 2, stride=64), :]) for p in range(NPOP)])
    own = 1 if leading == 1 else 0
    at = {}
    for p in range(NPOP):
        if VEL[p][1] == 0:
            at[p] = SLOT[p]
            uu[at[p] : at[p] + 1, :] = post[p][own : own + 1]
        elif VEL[p][1] == leading:
            at[p] = SLOT[p] - (0 if leading == 1 else 1)
            uu[at[p] : at[p] + 2, :] = post[p]
    mg[...] = uu[:, 0 : NZ * RX].T
    return at


def patched(p, z, half, leading, at, mg, value, lane):
    start = (z ^ zflip(p)) * RX + PAD + 8 * half - VEL[p][0]
    width = 2 if VEL[p][1] else 1
    first = 0 if leading == 1 else NY - width
    patch = pltpu.roll(mg[start : start + 8, :], (first - at[p]) % NY, 1)
    return jnp.where((lane >= first) & (lane < first + width), patch, value)


def near_right(shape):
    lane = lax.broadcasted_iota(jnp.int32, shape, 1)
    return (lane < 24) | (((lane < 40) | ((lane >= 88) & (lane < 104))) & (lane % 2 == 0))


def exchange(
    sizes, f_hbm, g_hbm, fo, go, ao, yb, fv, gv, fc, gc, corner, q, w, xs, xb, tr, uu, mg,
    load_sem, corner_sem, send_sem, recv_sem, ready,
):
    nx_dev, ny_dev = sizes
    ix, iy = lax.axis_index("gx"), lax.axis_index("gy")

    def device(dx, dy):
        return (lax.rem(ix + dx + nx_dev, nx_dev), lax.rem(iy + dy + ny_dev, ny_dev))

    block = SEAM if ny_dev % SEAM == 0 else ny_dev
    place = lax.rem(iy, block)
    is_first, is_last, is_before = place == 0, place == block - 1, place == block - 2

    barrier = pltpu.get_barrier_semaphore()

    def greet(steps, semaphore):
        for dx, dy in steps:
            pl.semaphore_signal(semaphore, inc=1, device_id=device(dx, dy), device_id_type=MESH)

    above = [(-1, 1), (0, 1), (1, 1)]

    @pl.when(is_last)
    def _():
        pl.semaphore_wait(barrier, 3)
        greet([(0, 1)], ready)

    corner_loads = []
    for z in range(NZ):
        for side, r in enumerate((0, NX - 2)):
            to = slice(4 * z + 2 * side, 4 * z + 2 * side + 2)
            corner_loads += [
                pltpu.make_async_copy(f_hbm.at[:, z, r : r + 2], fc.at[:, to], corner_sem.at[z, side, 0]),
                pltpu.make_async_copy(g_hbm.at[:, :, z, r : r + 2], gc.at[:, :, to], corner_sem.at[z, side, 1]),
            ]

    @pl.when(is_last)
    def _():
        for copy in corner_loads:
            copy.start()

    loads = []
    for half in range(2):
        for z in range(NZ):
            rows = slice(8 * half, 8 * half + 8)
            piece = (
                pltpu.make_async_copy(f_hbm.at[:, z, rows], fv.at[:, z, rows], load_sem.at[half, z, 0]),
                pltpu.make_async_copy(g_hbm.at[:, :, z, rows], gv.at[:, :, z, rows], load_sem.at[half, z, 1]),
            )
            loads.append(piece)
            for copy in piece:
                copy.start()

    beside = [(-1, 0), (1, 0)]
    below = [(-1, -1), (0, -1), (1, -1)]

    @pl.when(is_last)
    def _():
        greet(below, barrier)

    @pl.when(jnp.logical_not(is_last))
    def _():
        greet(below + beside, barrier)

        @pl.when(jnp.logical_not(is_before))
        def _():
            greet(above, barrier)

    low, high, own = slice(0, 8), slice(24, 32), slice(8, 24)
    first, last = slice(8, 16), slice(16, 24)
    slots = iter(range(10))

    def to(src, dst, dx, dy):
        k = next(slots)
        return pltpu.make_async_remote_copy(
            src_ref=src, dst_ref=dst, send_sem=send_sem.at[k], recv_sem=recv_sem.at[k],
            device_id=device(dx, dy), device_id_type=MESH,
        )

    def to_row(side, dy, dx):
        if dx == 0:
            return to(ao.at[:, own], yb.at[side, :, own], 0, dy)
        src, dst = (slice(8, 10), slice(24, 26)) if dx < 0 else (slice(22, 24), slice(6, 8))
        return to(ao.at[:, src], yb.at[side, :, dst], dx, dy)

    to_above = [to_row(0, 1, dx) for dx in (-1, 1, 0)]
    to_below = [to_row(1, -1, dx) for dx in (-1, 1, 0)]
    with_corners = pltpu.make_async_remote_copy(
        src_ref=ao.at[:, 6:26], dst_ref=yb.at[1, :, 6:26], send_sem=send_sem.at[5], recv_sem=recv_sem.at[5],
        device_id=device(0, -1), device_id_type=MESH,
    )
    to_beside = [
        to(xs.at[0], xb.at[0, :, 0:40], 1, 0),
        to(xs.at[1], xb.at[1, :, 8:48], -1, 0),
        to(ao.at[:, last], ao.at[:, low], 1, 0),
        to(ao.at[:, first], ao.at[:, high], -1, 0),
    ]

    early = [
        pltpu.make_async_remote_copy(
            src_ref=corner.at[:, src], dst_ref=yb.at[0, :, dst], send_sem=send_sem.at[k], recv_sem=recv_sem.at[k],
            device_id=device(dx, 1), device_id_type=MESH,
        )
        for k, src, dst, dx in ((0, slice(0, 2), slice(24, 26), -1), (1, slice(2, 4), slice(6, 8), 1))
    ]

    def start(copies):
        for copy in copies:
            copy.start()

    @pl.when(is_last)
    def _():
        for copy in corner_loads:
            copy.wait()
        pops = [fc[p] for p in range(19)] + [gc[a, j] for a in range(3) for j in range(7)]
        post = collide(pops)
        lane = lax.broadcasted_iota(jnp.int32, (8, NY), 1)
        up = [[jnp.zeros((8, NY), F32) for _ in range(4)] for _ in range(2)]
        for k, p in enumerate(Y0 + YP):
            s = SLOT[p]
            moved = pltpu.roll(post[p], s + 1 + VEL[p][1], 1)
            here = lane == s if VEL[p][1] == 0 else (lane == s) | (lane == s + 1)
            up[zflip(p)][k % 4] = jnp.where(here, moved, up[zflip(p)][k % 4])
        up = [(part[0] + part[1]) + (part[2] + part[3]) for part in up]
        both = up[0] + pltpu.roll(up[1], 4, 0)
        both = jnp.where(lane < 64, both, pltpu.roll(both, 63, 1))
        corner[0] = both[0:4]
        corner[1] = both[4:8]
        start(early)

    lane = lax.broadcasted_iota(jnp.int32, (8, NY), 1)
    for half in range(2):
        rows = slice(8 * half, 8 * half + 8)
        at = slice(PAD + 8 * half, PAD + 8 * half + 8)
        up = [jnp.zeros((8, NY), F32) for _ in range(NZ)]
        down = [jnp.zeros((8, NY), F32) for _ in range(NZ)]
        for z in range(NZ):
            for copy in loads[half * NZ + z]:
                copy.wait()
            pops = [fv[p, z, rows, :] for p in range(19)]
            pops += [gv[a, j, z, rows, :] for a in range(3) for j in range(7)]
            post = collide(pops)
            for p in range(NPOP):
                zz = z ^ zflip(p)
                q[plane(p, zz, 8 * half), :] = post[p]
                s = SLOT[p]
                if VEL[p][1] == 0:
                    moved = pltpu.roll(post[p], s + 1, 1)
                    up[zz] = jnp.where(lane == s, moved, up[zz])
                    down[zz] = jnp.where(lane == s + 1, moved, down[zz])
                elif VEL[p][1] == 1:
                    moved = pltpu.roll(post[p], s + 2, 1)
                    up[zz] = jnp.where((lane == s) | (lane == s + 1), moved, up[zz])
                else:
                    moved = pltpu.roll(post[p], s, 1)
                    down[zz] = jnp.where((lane == s) | (lane == s + 1), moved, down[zz])
        for z in range(NZ):
            here = jnp.where((lane < 24) | ((lane < 40) & (lane % 2 == 0)), up[z], down[z])
            there = jnp.where((lane >= 25) & (lane < 40) & (lane % 2 == 1), up[z], down[z])
            ao[z, at, :] = jnp.where(lane < 64, here, pltpu.roll(there, 63, 1))
    @pl.when(is_first)
    def _():
        pl.semaphore_wait(barrier, 5)

    @pl.when(jnp.logical_not(is_first | is_last))
    def _():
        pl.semaphore_wait(barrier, 8)

    @pl.when(is_before)
    def _():
        greet([(0, 1)], ready)

    @pl.when(jnp.logical_not(is_last))
    def _():
        start(to_above[:2])

    start(to_above[2:])

    def row(first, count, z, r):
        return q[pl.ds(first * NZ * RX + z * RX + PAD + r, count, stride=NZ * RX), :]

    for z in range(NZ):
        xs[0, z, 0:8, :] = row(0, 8, z, NX - 2)
        xs[0, z, 8:32, :] = row(8, 24, z, NX - 1)
        xs[0, z, 32:40, :] = row(0, 8, z, NX - 1)
        xs[1, z, 0:24, :] = row(8, 24, z, 0)
        xs[1, z, 24:32, :] = row(32, 8, z, 0)
        xs[1, z, 32:40, :] = row(32, 8, z, 1)
        xb[0, z, 40:48, :] = row(32, 8, z, 0)
        xb[1, z, 0:8, :] = row(0, 8, z, NX - 1)

    @pl.when(is_last)
    def _():
        pl.semaphore_wait(ready, 1)

    start(to_beside)

    @pl.when(jnp.logical_not(is_first))
    def _():
        start(to_below)

    for copy in to_beside:
        copy.wait()

    def turn(p, value):
        return pltpu.roll(value, VEL[p][1] % NY, 1) if VEL[p][1] else value

    for i in range(8):
        for z in range(NZ):
            q[plane(XP[i], z, -1, 1), :] = xb[0, z, 32 + i : 33 + i, :]
            q[plane(XM[i], z, NX, 1), :] = xb[1, z, 32 + i : 33 + i, :]
    edges = []
    for p in range(NPOP):
        at = slice(XOFF[p], XOFF[p] + 1)
        edges.append(turn(p, jnp.concatenate([xb[side, z, at, :] for side in range(2) for z in range(NZ)], axis=0)))
    edges = collide(edges)
    for p in range(NPOP):
        for z in range(NZ):
            zz = z ^ zflip(p)
            if VEL[p][0] == 1:
                w[plane(p, zz, -1, 1), :] = edges[p][z : z + 1]
            elif VEL[p][0] == -1:
                w[plane(p, zz, NX, 1), :] = edges[p][NZ + z : NZ + z + 1]
    for z in range(NZ):
        for half in range(2):
            post = collide([turn(p, q[plane(p, z, 8 * half - VEL[p][0]), :]) for p in range(NPOP)])
            for p in range(NPOP):
                w[plane(p, z ^ zflip(p), 8 * half), :] = post[p]
    for p in range(NPOP):
        for z in range(NZ):
            for half in range(2):
                value = turn(p, w[plane(p, z, 8 * half - VEL[p][0]), :])
                rows = slice(8 * half, 8 * half + 8)
                if p < 19:
                    fo[p, z, rows, :] = value
                else:
                    go[(p - 19) // 7, (p - 19) % 7, z, rows, :] = value

    @pl.when(is_last)
    def _():
        with_corners.wait_recv()

    @pl.when(jnp.logical_not(is_last))
    def _():
        for copy in to_below:
            copy.wait_recv()

    tall = near_right((NZ * RX, NY))
    flat = ao[...].reshape(NZ * RX, NY)

    def patch(leading, block):
        places = edge_rows(block, leading, tr, uu, mg)
        for p in places:
            for z in range(NZ):
                for half in range(2):
                    rows = slice(8 * half, 8 * half + 8)
                    if p < 19:
                        fo[p, z, rows, :] = patched(p, z, half, leading, places, mg, fo[p, z, rows, :], lane)
                    else:
                        a, j = (p - 19) // 7, (p - 19) % 7
                        go[a, j, z, rows, :] = patched(p, z, half, leading, places, mg, go[a, j, z, rows, :], lane)

    patch(-1, jnp.where(tall, flat, yb[1].reshape(NZ * RX, NY)))

    @pl.when(is_first)
    def _():
        pl.semaphore_wait(ready, 1)
        with_corners.start()

    to_above[2].wait_recv()
    middle = [
        part
        for z in range(NZ)
        for part in (ao[z, low], jnp.where(tall[0:NX], yb[0, z, own], ao[z, own]), ao[z, high])
    ]
    patch(1, jnp.concatenate(middle, axis=0))

    @pl.when(is_first)
    def _():
        with_corners.wait_send()

    @pl.when(jnp.logical_not(is_first))
    def _():
        for copy in to_below:
            copy.wait_send()

    for copy in to_above:
        copy.wait_send()
    for copy in to_above[:2]:
        copy.wait_recv()


def finish(fi, gi, ao, yb, f_hbm, g_hbm, near, post_rows, fo, go, out_sem):
    mask = near_right((2, NY))
    for cx in (-1, 0, 1):
        for z in range(NZ):
            for k, r in enumerate((-1, NX - 1)):
                first = z * RX + PAD + r - cx
                rows = slice(first, first + 2)
                near[cx % 3, 4 * z + 2 * k : 4 * z + 2 * k + 2, :] = jnp.where(mask, yb[0, rows, :], ao[rows, :])
    sources = [near[cx] for cx in range(3)]
    post = collide([pltpu.roll(sources[VEL[p][0] % 3], (64 - SLOT[p]) % NY, 1) for p in range(NPOP)])
    lane = lax.broadcasted_iota(jnp.int32, (8, NY), 1)
    row = lax.broadcasted_iota(jnp.int32, (8, NY), 0)
    for p in Y0 + YP:
        value = post[p]
        if VEL[p][1]:
            value = jnp.where(lane == 0, pltpu.roll(value, 64, 1), pltpu.roll(value, 1, 1))
        post_rows[8 + 8 * p : 16 + 8 * p, :] = value

    def fixed(p, z, half, value):
        cx, cy, _ = VEL[p]
        reach = {(0, 0): (0, 1, 1), (1, 0): (7, 1, 2), (0, 1): (0, 2, 0), (1, -1): (6, 2, 2)}.get((half, cx))
        if cy < 0 or reach is None:
            return value
        to, count, at = reach
        start = 8 + 8 * p + 4 * (z ^ zflip(p)) + at - to
        here = (row >= to) & (row < to + count) & (lane <= cy)
        return jnp.where(here, post_rows[start : start + 8, :], value)

    copies = []

    def put(pops, src, dst):
        for p in pops:
            for z in range(NZ):
                for half in range(2):
                    rows = slice(8 * half, 8 * half + 8)
                    if p < 19:
                        fo[p, z, rows, :] = fixed(p, z, half, fi[p, z, rows, :])
                    else:
                        a, j = (p - 19) // 7, (p - 19) % 7
                        go[a, j, z, rows, :] = fixed(p, z, half, gi[a, j, z, rows, :])
        copies.append(pltpu.make_async_copy(src, dst, out_sem.at[len(copies)]))
        copies[-1].start()

    put(range(0, 10), fo.at[0:10], f_hbm.at[0:10])
    put(range(10, 19), fo.at[10:19], f_hbm.at[10:19])
    put(range(19, 33), go.at[0:2], g_hbm.at[0:2])
    put(range(33, 40), go.at[2:3], g_hbm.at[2:3])
    for copy in copies:
        copy.wait()


def per_device(sizes, fluid_pops, magnet_pops):
    vmem = pl.BlockSpec(memory_space=pltpu.VMEM)
    hbm = pl.BlockSpec(memory_space=pltpu.HBM)
    fluid, magnet = (19, NZ, NX, NY), (3, 7, NZ, NX, NY)
    columns = (NZ, RX, NY)
    turned = [pltpu.VMEM((NY, NY), F32), pltpu.VMEM((NY, NY), F32), pltpu.VMEM((NZ * RX, NY), F32)]
    fo, go, ao, yb = pl.pallas_call(
        functools.partial(exchange, sizes),
        out_shape=[pltpu.VMEM(shape, F32) for shape in (fluid, magnet, columns, (2, *columns))],
        in_specs=[hbm] * 2,
        out_specs=[vmem] * 4,
        scratch_shapes=[
            pltpu.VMEM(fluid, F32),
            pltpu.VMEM(magnet, F32),
            pltpu.VMEM((19, 8, NY), F32),
            pltpu.VMEM((3, 7, 8, NY), F32),
            pltpu.VMEM((NZ, 4, NY), F32),
            pltpu.VMEM((NPOP * NZ * RX, NY), F32),
            pltpu.VMEM((NPOP * NZ * RX, NY), F32),
            pltpu.VMEM((2, NZ, 40, NY), F32),
            pltpu.VMEM((2, NZ, 48, NY), F32),
            *turned,
            pltpu.SemaphoreType.DMA((2, NZ, 2)),
            pltpu.SemaphoreType.DMA((NZ, 2, 2)),
            pltpu.SemaphoreType.DMA((10,)),
            pltpu.SemaphoreType.DMA((10,)),
            pltpu.SemaphoreType.REGULAR,
        ],
        compiler_params=pltpu.CompilerParams(
            collective_id=0, has_side_effects=True, vmem_limit_bytes=VMEM_LIMIT
        ),
    )(
        pltpu.with_memory_space_constraint(fluid_pops, pltpu.HBM),
        pltpu.with_memory_space_constraint(magnet_pops, pltpu.HBM),
    )
    return pl.pallas_call(
        finish,
        out_shape=[jax.ShapeDtypeStruct(fluid, F32), jax.ShapeDtypeStruct(magnet, F32)],
        in_specs=[vmem] * 4,
        out_specs=[hbm] * 2,
        scratch_shapes=[
            pltpu.VMEM((3, 8, NY), F32),
            pltpu.VMEM((8 * NPOP + 16, NY), F32),
            pltpu.VMEM(fluid, F32),
            pltpu.VMEM(magnet, F32),
            pltpu.SemaphoreType.DMA((4,)),
        ],
        compiler_params=pltpu.CompilerParams(vmem_limit_bytes=VMEM_LIMIT),
    )(fo, go, ao.reshape(NZ * RX, NY), yb.reshape(2, NZ * RX, NY))


VMEM_LIMIT = 48 << 20
SEAM = 16


def solution(mesh):
    specs = (P(None, None, "gx", "gy"), P(None, None, None, "gx", "gy"))
    return jax.shard_map(
        functools.partial(per_device, (mesh.shape["gx"], mesh.shape["gy"])),
        mesh=mesh,
        in_specs=specs,
        out_specs=specs,
        check_vma=False,
    )
```

```python
import functools

import jax
import jax.numpy as jnp
from jax import lax
from jax.experimental import pallas as pl
from jax.experimental.pallas import tpu as pltpu
from jax.sharding import PartitionSpec as P

MESH = pl.DeviceIdType.MESH
F32 = jnp.float32

FLUID = [
    (0, 0, 0),
    (1, 0, 0), (-1, 0, 0), (0, 1, 0), (0, -1, 0), (0, 0, 1), (0, 0, -1),
    (1, 1, 0), (-1, -1, 0), (1, -1, 0), (-1, 1, 0),
    (1, 0, 1), (-1, 0, -1), (1, 0, -1), (-1, 0, 1),
    (0, 1, 1), (0, -1, -1), (0, 1, -1), (0, -1, 1),
]
VEL = FLUID + FLUID[:7] * 3
NPOP = 40
OM_F = 1.0 / 0.9
OM_G = 1.0 / 0.8

XP = [p for p in range(NPOP) if VEL[p][0] == 1]
X0 = [p for p in range(NPOP) if VEL[p][0] == 0]
XM = [p for p in range(NPOP) if VEL[p][0] == -1]
ORDER = XP + X0 + XM
POS = {p: i for i, p in enumerate(ORDER)}
XOFF = {}
for i, p in enumerate(XP):
    XOFF[p] = i
for i, p in enumerate(X0):
    XOFF[p] = 8 + i
for i, p in enumerate(XM):
    XOFF[p] = 40 + i
YP = [p for p in range(NPOP) if VEL[p][1] == 1]
Y0 = [p for p in range(NPOP) if VEL[p][1] == 0]
YM = [p for p in range(NPOP) if VEL[p][1] == -1]
SLOT = {}
for i, p in enumerate(Y0):
    SLOT[p] = i
for i, p in enumerate(YP):
    SLOT[p] = 24 + 2 * i
for i, p in enumerate(YM):
    SLOT[p] = 25 + 2 * i
NX, NY, NZ = 16, 128, 2
PAD = 8
RX = NX + 2 * PAD


def zflip(p):
    return abs(VEL[p][2])


def plane(p, z, r, count=8):
    first = (POS[p] * NZ + z) * RX + PAD + r
    return slice(first, first + count)


def collide(pops):
    f, g = pops[:19], [pops[19 + 7 * a : 26 + 7 * a] for a in range(3)]
    pairs = [(i, i + 1) for i in range(1, 19, 2)]
    even = [f[i] + f[j] for i, j in pairs]
    odd = [f[i] - f[j] for i, j in pairs]
    rho = f[0] + ((even[0] + even[1]) + (even[2] + even[3])) + ((even[4] + even[5]) + ((even[6] + even[7]) + even[8]))
    mom = []
    for a in range(3):
        terms = [(odd[k], VEL[pairs[k][0]][a]) for k in range(9) if VEL[pairs[k][0]][a]]
        total = terms[0][0]
        for value, sign in terms[1:]:
            total = total + value if sign > 0 else total - value
        mom.append(total)
    inv = 1.0 / rho
    u = [m * inv for m in mom]
    b = [((g[a][0] + g[a][1]) + (g[a][2] + g[a][3])) + ((g[a][4] + g[a][5]) + g[a][6]) for a in range(3)]
    half = 0.5 * (b[0] * b[0] + b[1] * b[1] + b[2] * b[2])
    diag = [mom[a] * u[a] - b[a] * b[a] + half for a in range(3)]
    cross = {(a, c): mom[a] * u[c] - b[a] * b[c] for a, c in ((0, 1), (0, 2), (1, 2))}
    trace = diag[0] + diag[1] + diag[2]
    base = (OM_F / 36.0) * (rho - 1.5 * trace)
    d45 = [(4.5 * OM_F / 36.0) * d for d in diag]
    c9 = {k: (9.0 * OM_F / 36.0) * v for k, v in cross.items()}
    m3 = [(3.0 * OM_F / 36.0) * m for m in mom]
    keep = 1.0 - OM_F
    out = [None] * NPOP
    out[0] = keep * f[0] + 12.0 * base
    for k, (i, j) in enumerate(pairs):
        c = VEL[i]
        axes = [a for a in range(3) if c[a]]
        if len(axes) == 1:
            s = 2.0 * (base + d45[axes[0]])
            t = 2.0 * m3[axes[0]]
        else:
            a, d = axes
            s = base + d45[a] + d45[d]
            if c[a] * c[d] > 0:
                s = s + c9[(a, d)]
            else:
                s = s - c9[(a, d)]
            first = m3[a] if c[a] > 0 else -m3[a]
            t = first + m3[d] if c[d] > 0 else first - m3[d]
        out[i] = keep * f[i] + (s + t)
        out[j] = keep * f[j] + (s - t)
    keep = 1.0 - OM_G
    for a in range(3):
        rest = (OM_G / 8.0) * b[a]
        out[19 + 7 * a] = keep * g[a][0] + 2.0 * rest
        for d in range(3):
            plus, minus = rest, rest
            if d != a:
                flux = (4.0 * OM_G / 8.0) * (u[d] * b[a] - b[d] * u[a])
                plus, minus = rest + flux, rest - flux
            out[19 + 7 * a + 1 + 2 * d] = keep * g[a][1 + 2 * d] + plus
            out[19 + 7 * a + 2 + 2 * d] = keep * g[a][2 + 2 * d] + minus
    return out


def edge_rows(block, leading, tr, uu, mg):
    tr[:, 0 : NZ * RX] = block.T

    def turn(p, value):
        return pltpu.roll(value, VEL[p][0] % NY, 1) if VEL[p][0] else value

    post = collide([turn(p, tr[pl.ds(SLOT[p], 2, stride=64), :]) for p in range(NPOP)])
    own = 1 if leading == 1 else 0
    at = {}
    for p in range(NPOP):
        if VEL[p][1] == 0:
            at[p] = SLOT[p]
            uu[at[p] : at[p] + 1, :] = post[p][own : own + 1]
        elif VEL[p][1] == leading:
            at[p] = SLOT[p] - (0 if leading == 1 else 1)
            uu[at[p] : at[p] + 2, :] = post[p]
    mg[...] = uu[:, 0 : NZ * RX].T
    return at


def patched(p, z, half, leading, at, mg, value, lane):
    start = (z ^ zflip(p)) * RX + PAD + 8 * half - VEL[p][0]
    width = 2 if VEL[p][1] else 1
    first = 0 if leading == 1 else NY - width
    patch = pltpu.roll(mg[start : start + 8, :], (first - at[p]) % NY, 1)
    return jnp.where((lane >= first) & (lane < first + width), patch, value)


def near_right(shape):
    lane = lax.broadcasted_iota(jnp.int32, shape, 1)
    return (lane < 24) | (((lane < 40) | ((lane >= 88) & (lane < 104))) & (lane % 2 == 0))


def exchange(
    sizes, f_hbm, g_hbm, fo, go, fe, ge, ao, yb, fv, gv, fc, gc, corner, swap, q, w, xs, xb, tr, uu, mg,
    load_sem, corner_sem, send_sem, recv_sem, ready,
):
    nx_dev, ny_dev = sizes
    ix, iy = lax.axis_index("gx"), lax.axis_index("gy")

    def device(dx, dy):
        return (lax.rem(ix + dx + nx_dev, nx_dev), lax.rem(iy + dy + ny_dev, ny_dev))

    block = SEAM if ny_dev % SEAM == 0 else ny_dev
    place = lax.rem(iy, block)
    is_first, is_last, is_before = place == 0, place == block - 1, place == block - 2

    corner_loads = []
    for z in range(NZ):
        for side, r in enumerate((0, NX - 2)):
            to = slice(4 * z + 2 * side, 4 * z + 2 * side + 2)
            corner_loads += [
                pltpu.make_async_copy(f_hbm.at[:, z, r : r + 2], fc.at[:, to], corner_sem.at[z, side, 0]),
                pltpu.make_async_copy(g_hbm.at[:, :, z, r : r + 2], gc.at[:, :, to], corner_sem.at[z, side, 1]),
            ]

    @pl.when(is_last)
    def _():
        for copy in corner_loads:
            copy.start()

    barrier = pltpu.get_barrier_semaphore()

    def greet(steps, semaphore):
        for dx, dy in steps:
            pl.semaphore_signal(semaphore, inc=1, device_id=device(dx, dy), device_id_type=MESH)

    above = [(-1, 1), (0, 1), (1, 1)]

    @pl.when(is_last)
    def _():
        pl.semaphore_wait(barrier, 3)
        greet([(0, 1)], ready)

    loads = []
    for half in range(2):
        for z in range(NZ):
            rows = slice(8 * half, 8 * half + 8)
            piece = (
                pltpu.make_async_copy(f_hbm.at[:, z, rows], fv.at[:, z, rows], load_sem.at[half, z, 0]),
                pltpu.make_async_copy(g_hbm.at[:, :, z, rows], gv.at[:, :, z, rows], load_sem.at[half, z, 1]),
            )
            loads.append(piece)
            for copy in piece:
                copy.start()

    beside = [(-1, 0), (1, 0)]
    below = [(-1, -1), (0, -1), (1, -1)]

    @pl.when(is_last)
    def _():
        greet(below, barrier)

    @pl.when(jnp.logical_not(is_last))
    def _():
        greet(below + beside, barrier)

        @pl.when(jnp.logical_not(is_before))
        def _():
            greet(above, barrier)

    low, high, own = slice(0, 8), slice(24, 32), slice(8, 24)
    first, last = slice(8, 16), slice(16, 24)
    slots = iter(range(10))

    def to(src, dst, dx, dy):
        k = next(slots)
        return pltpu.make_async_remote_copy(
            src_ref=src, dst_ref=dst, send_sem=send_sem.at[k], recv_sem=recv_sem.at[k],
            device_id=device(dx, dy), device_id_type=MESH,
        )

    def to_row(side, dy, dx):
        if dx == 0:
            return to(ao.at[:, own], yb.at[side, :, own], 0, dy)
        src, dst = (slice(8, 10), slice(24, 26)) if dx < 0 else (slice(22, 24), slice(6, 8))
        return to(ao.at[:, src], yb.at[side, :, dst], dx, dy)

    to_above = [to_row(0, 1, dx) for dx in (-1, 1, 0)]
    to_below = [to_row(1, -1, dx) for dx in (-1, 1, 0)]
    with_corners = pltpu.make_async_remote_copy(
        src_ref=ao.at[:, 6:26], dst_ref=yb.at[1, :, 6:26], send_sem=send_sem.at[5], recv_sem=recv_sem.at[5],
        device_id=device(0, -1), device_id_type=MESH,
    )
    to_beside = [
        to(xs.at[0], xb.at[0, :, 0:40], 1, 0),
        to(xs.at[1], xb.at[1, :, 8:48], -1, 0),
        to(ao.at[:, last], ao.at[:, low], 1, 0),
        to(ao.at[:, first], ao.at[:, high], -1, 0),
    ]

    early = [
        pltpu.make_async_remote_copy(
            src_ref=corner.at[:, src], dst_ref=yb.at[0, :, dst], send_sem=send_sem.at[k], recv_sem=recv_sem.at[k],
            device_id=device(dx, 1), device_id_type=MESH,
        )
        for k, src, dst, dx in ((0, slice(0, 2), slice(24, 26), -1), (1, slice(2, 4), slice(6, 8), 1))
    ]

    def start(copies):
        for copy in copies:
            copy.start()

    @pl.when(is_last)
    def _():
        for copy in corner_loads:
            copy.wait()
        pops = [fc[p] for p in range(19)] + [gc[a, j] for a in range(3) for j in range(7)]
        post = collide(pops)
        lane = lax.broadcasted_iota(jnp.int32, (8, NY), 1)
        up = [[jnp.zeros((8, NY), F32) for _ in range(4)] for _ in range(2)]
        columns = [(p, SLOT[p], NY - 1 - (1 if VEL[p][1] else 0)) for p in Y0 + YP]
        columns += [(p, SLOT[p] + 64, NY - 1) for p in YP]
        for k, (p, s, column) in enumerate(columns):
            moved = pltpu.roll(post[p], (s - column) % NY, 1)
            up[zflip(p)][k % 4] = jnp.where(lane == s, moved, up[zflip(p)][k % 4])
        up = [(part[0] + part[1]) + (part[2] + part[3]) for part in up]
        swap[...] = up[1]
        corner[0] = up[0][0:4] + swap[4:8, :]
        corner[1] = up[0][4:8] + swap[0:4, :]
        start(early)

    lane = lax.broadcasted_iota(jnp.int32, (8, NY), 1)
    for half in range(2):
        rows = slice(8 * half, 8 * half + 8)
        at = slice(PAD + 8 * half, PAD + 8 * half + 8)
        up = [jnp.zeros((8, NY), F32) for _ in range(NZ)]
        down = [jnp.zeros((8, NY), F32) for _ in range(NZ)]
        for z in range(NZ):
            for copy in loads[half * NZ + z]:
                copy.wait()
            pops = [fv[p, z, rows, :] for p in range(19)]
            pops += [gv[a, j, z, rows, :] for a in range(3) for j in range(7)]
            post = collide(pops)
            for p in range(NPOP):
                zz = z ^ zflip(p)
                q[plane(p, zz, 8 * half), :] = post[p]
                s = SLOT[p]
                if VEL[p][1] == 0:
                    moved = pltpu.roll(post[p], s + 1, 1)
                    up[zz] = jnp.where(lane == s, moved, up[zz])
                    down[zz] = jnp.where(lane == s + 1, moved, down[zz])
                elif VEL[p][1] == 1:
                    moved = pltpu.roll(post[p], s + 2, 1)
                    up[zz] = jnp.where((lane == s) | (lane == s + 1), moved, up[zz])
                else:
                    moved = pltpu.roll(post[p], s, 1)
                    down[zz] = jnp.where((lane == s) | (lane == s + 1), moved, down[zz])
        for z in range(NZ):
            here = jnp.where((lane < 24) | ((lane < 40) & (lane % 2 == 0)), up[z], down[z])
            there = jnp.where((lane >= 25) & (lane < 40) & (lane % 2 == 1), up[z], down[z])
            ao[z, at, :] = jnp.where(lane < 64, here, pltpu.roll(there, 63, 1))
    @pl.when(is_first)
    def _():
        pl.semaphore_wait(barrier, 5)

    @pl.when(jnp.logical_not(is_first | is_last))
    def _():
        pl.semaphore_wait(barrier, 8)

    @pl.when(is_before)
    def _():
        greet([(0, 1)], ready)

    @pl.when(jnp.logical_not(is_last))
    def _():
        start(to_above[:2])

    start(to_above[2:])

    def row(first, count, z, r):
        return q[pl.ds(first * NZ * RX + z * RX + PAD + r, count, stride=NZ * RX), :]

    for z in range(NZ):
        xs[0, z, 0:8, :] = row(0, 8, z, NX - 2)
        xs[0, z, 8:32, :] = row(8, 24, z, NX - 1)
        xs[0, z, 32:40, :] = row(0, 8, z, NX - 1)
        xs[1, z, 0:24, :] = row(8, 24, z, 0)
        xs[1, z, 24:32, :] = row(32, 8, z, 0)
        xs[1, z, 32:40, :] = row(32, 8, z, 1)
        xb[0, z, 40:48, :] = row(32, 8, z, 0)
        xb[1, z, 0:8, :] = row(0, 8, z, NX - 1)

    @pl.when(is_last)
    def _():
        pl.semaphore_wait(ready, 1)

    start(to_beside)

    @pl.when(jnp.logical_not(is_first))
    def _():
        start(to_below)

    for copy in to_beside:
        copy.wait()

    def turn(p, value):
        return pltpu.roll(value, VEL[p][1] % NY, 1) if VEL[p][1] else value

    for i in range(8):
        for z in range(NZ):
            q[plane(XP[i], z, -1, 1), :] = xb[0, z, 32 + i : 33 + i, :]
            q[plane(XM[i], z, NX, 1), :] = xb[1, z, 32 + i : 33 + i, :]
    edges = []
    for p in range(NPOP):
        at = slice(XOFF[p], XOFF[p] + 1)
        edges.append(turn(p, jnp.concatenate([xb[side, z, at, :] for side in range(2) for z in range(NZ)], axis=0)))
    edges = collide(edges)
    for p in range(NPOP):
        for z in range(NZ):
            zz = z ^ zflip(p)
            if VEL[p][0] == 1:
                w[plane(p, zz, -1, 1), :] = edges[p][z : z + 1]
            elif VEL[p][0] == -1:
                w[plane(p, zz, NX, 1), :] = edges[p][NZ + z : NZ + z + 1]
    for z in range(NZ):
        for half in range(2):
            post = collide([turn(p, q[plane(p, z, 8 * half - VEL[p][0]), :]) for p in range(NPOP)])
            for p in range(NPOP):
                w[plane(p, z ^ zflip(p), 8 * half), :] = post[p]
    for p in range(NPOP):
        for z in range(NZ):
            for half in range(2):
                value = turn(p, w[plane(p, z, 8 * half - VEL[p][0]), :])
                rows = slice(8 * half, 8 * half + 8)
                if p < 19:
                    fo[p, z, rows, :] = value
                else:
                    go[(p - 19) // 7, (p - 19) % 7, z, rows, :] = value

    @pl.when(is_last)
    def _():
        with_corners.wait_recv()

    @pl.when(jnp.logical_not(is_last))
    def _():
        for copy in to_below:
            copy.wait_recv()

    tall = near_right((NZ * RX, NY))
    flat = ao[...].reshape(NZ * RX, NY)

    def patch(leading, block):
        places = edge_rows(block, leading, tr, uu, mg)
        for p in places:
            for z in range(NZ):
                for half in range(2):
                    rows = slice(8 * half, 8 * half + 8)
                    if p < 19:
                        fo[p, z, rows, :] = patched(p, z, half, leading, places, mg, fo[p, z, rows, :], lane)
                    else:
                        a, j = (p - 19) // 7, (p - 19) % 7
                        go[a, j, z, rows, :] = patched(p, z, half, leading, places, mg, go[a, j, z, rows, :], lane)

    patch(-1, jnp.where(tall, flat, yb[1].reshape(NZ * RX, NY)))

    @pl.when(is_first)
    def _():
        pl.semaphore_wait(ready, 1)
        with_corners.start()

    to_above[2].wait_recv()
    middle = [
        part
        for z in range(NZ)
        for part in (ao[z, low], jnp.where(tall[0:NX], yb[0, z, own], ao[z, own]), ao[z, high])
    ]
    patch(1, jnp.concatenate(middle, axis=0))
    for z in range(NZ):
        for side, r in enumerate((0, NX - 2)):
            to = slice(4 * z + 2 * side, 4 * z + 2 * side + 2)
            for p in range(19):
                fe[p, to, :] = fo[p, z, r : r + 2, :]
            for a in range(3):
                for j in range(7):
                    ge[a, j, to, :] = go[a, j, z, r : r + 2, :]

    @pl.when(is_first)
    def _():
        with_corners.wait_send()

    @pl.when(jnp.logical_not(is_first))
    def _():
        for copy in to_below:
            copy.wait_send()

    for copy in to_above:
        copy.wait_send()
    for copy in to_above[:2]:
        copy.wait_recv()


def finish(fi, gi, fe, ge, ao, yb, f_hbm, g_hbm, near, post_rows, fo, go, out_sem):
    copies = []

    def store(src, dst):
        copies.append(pltpu.make_async_copy(src, dst, out_sem.at[len(copies)]))
        copies[-1].start()

    store(fi.at[:, :, 2 : NX - 2], f_hbm.at[:, :, 2 : NX - 2])
    store(gi.at[:, :, :, 2 : NX - 2], g_hbm.at[:, :, :, 2 : NX - 2])

    mask = near_right((2, NY))
    for cx in (-1, 0, 1):
        for z in range(NZ):
            for k, r in enumerate((-1, NX - 1)):
                first = z * RX + PAD + r - cx
                rows = slice(first, first + 2)
                near[cx % 3, 4 * z + 2 * k : 4 * z + 2 * k + 2, :] = jnp.where(mask, yb[0, rows, :], ao[rows, :])
    sources = [near[cx] for cx in range(3)]
    post = collide([pltpu.roll(sources[VEL[p][0] % 3], (64 - SLOT[p]) % NY, 1) for p in range(NPOP)])
    lane = lax.broadcasted_iota(jnp.int32, (8, NY), 1)
    row = lax.broadcasted_iota(jnp.int32, (8, NY), 0)
    row = row % 4
    for p in range(NPOP):
        cx, cy, _ = VEL[p]
        at = (fe, fo, p) if p < 19 else (ge, go, ((p - 19) // 7, (p - 19) % 7))
        value = at[0][at[2]]
        if cy >= 0:
            new = post[p]
            if cy:
                new = jnp.where(lane == 0, pltpu.roll(new, 64, 1), pltpu.roll(new, 1, 1))
            turned = 4 * zflip(p)
            if turned or not cx:
                base = 16 * p
                post_rows[base : base + 8, :] = new
                post_rows[base + 8 : base + 16, :] = new
            if cx:
                if turned:
                    new = post_rows[base + turned : base + turned + 8, :]
                reached = row < 2 if cx > 0 else row >= 2
                value = jnp.where(reached & (lane <= cy), new, value)
            else:
                for shift, reached in ((1, row == 0), (-1, row == 3)):
                    first = base + (turned + shift) % 8
                    value = jnp.where(reached & (lane <= cy), post_rows[first : first + 8, :], value)
        at[1][at[2]] = value
    for z in range(NZ):
        for side, r in enumerate((0, NX - 2)):
            rows = slice(4 * z + 2 * side, 4 * z + 2 * side + 2)
            store(fo.at[:, rows], f_hbm.at[:, z, r : r + 2])
            store(go.at[:, :, rows], g_hbm.at[:, :, z, r : r + 2])
    for copy in copies:
        copy.wait()


def per_device(sizes, fluid_pops, magnet_pops):
    vmem = pl.BlockSpec(memory_space=pltpu.VMEM)
    hbm = pl.BlockSpec(memory_space=pltpu.HBM)
    fluid, magnet = (19, NZ, NX, NY), (3, 7, NZ, NX, NY)
    columns = (NZ, RX, NY)
    turned = [pltpu.VMEM((NY, NY), F32), pltpu.VMEM((NY, NY), F32), pltpu.VMEM((NZ * RX, NY), F32)]
    edge_f, edge_g = (19, 8, NY), (3, 7, 8, NY)
    fo, go, fe, ge, ao, yb = pl.pallas_call(
        functools.partial(exchange, sizes),
        out_shape=[pltpu.VMEM(shape, F32) for shape in (fluid, magnet, edge_f, edge_g, columns, (2, *columns))],
        in_specs=[hbm] * 2,
        out_specs=[vmem] * 6,
        scratch_shapes=[
            pltpu.VMEM(fluid, F32),
            pltpu.VMEM(magnet, F32),
            pltpu.VMEM((19, 8, NY), F32),
            pltpu.VMEM((3, 7, 8, NY), F32),
            pltpu.VMEM((NZ, 4, NY), F32),
            pltpu.VMEM((8, NY), F32),
            pltpu.VMEM((NPOP * NZ * RX, NY), F32),
            pltpu.VMEM((NPOP * NZ * RX, NY), F32),
            pltpu.VMEM((2, NZ, 40, NY), F32),
            pltpu.VMEM((2, NZ, 48, NY), F32),
            *turned,
            pltpu.SemaphoreType.DMA((2, NZ, 2)),
            pltpu.SemaphoreType.DMA((NZ, 2, 2)),
            pltpu.SemaphoreType.DMA((10,)),
            pltpu.SemaphoreType.DMA((10,)),
            pltpu.SemaphoreType.REGULAR,
        ],
        compiler_params=pltpu.CompilerParams(
            collective_id=0, has_side_effects=True, vmem_limit_bytes=VMEM_LIMIT
        ),
    )(
        pltpu.with_memory_space_constraint(fluid_pops, pltpu.HBM),
        pltpu.with_memory_space_constraint(magnet_pops, pltpu.HBM),
    )
    return pl.pallas_call(
        finish,
        out_shape=[jax.ShapeDtypeStruct(fluid, F32), jax.ShapeDtypeStruct(magnet, F32)],
        in_specs=[vmem] * 6,
        out_specs=[hbm] * 2,
        scratch_shapes=[
            pltpu.VMEM((3, 8, NY), F32),
            pltpu.VMEM((16 * NPOP, NY), F32),
            pltpu.VMEM(edge_f, F32),
            pltpu.VMEM(edge_g, F32),
            pltpu.SemaphoreType.DMA((10,)),
        ],
        compiler_params=pltpu.CompilerParams(vmem_limit_bytes=VMEM_LIMIT),
    )(fo, go, fe, ge, ao.reshape(NZ * RX, NY), yb.reshape(2, NZ * RX, NY))


VMEM_LIMIT = 48 << 20
SEAM = 16


def solution(mesh):
    specs = (P(None, None, "gx", "gy"), P(None, None, None, "gx", "gy"))
    return jax.shard_map(
        functools.partial(per_device, (mesh.shape["gx"], mesh.shape["gy"])),
        mesh=mesh,
        in_specs=specs,
        out_specs=specs,
        check_vma=False,
    )
```

```python
import functools

import jax
import jax.numpy as jnp
from jax import lax
from jax.experimental import pallas as pl
from jax.experimental.pallas import tpu as pltpu
from jax.sharding import PartitionSpec as P

MESH = pl.DeviceIdType.MESH
F32 = jnp.float32

FLUID = [
    (0, 0, 0),
    (1, 0, 0), (-1, 0, 0), (0, 1, 0), (0, -1, 0), (0, 0, 1), (0, 0, -1),
    (1, 1, 0), (-1, -1, 0), (1, -1, 0), (-1, 1, 0),
    (1, 0, 1), (-1, 0, -1), (1, 0, -1), (-1, 0, 1),
    (0, 1, 1), (0, -1, -1), (0, 1, -1), (0, -1, 1),
]
VEL = FLUID + FLUID[:7] * 3
NPOP = 40
OM_F = 1.0 / 0.9
OM_G = 1.0 / 0.8

XP = [p for p in range(NPOP) if VEL[p][0] == 1]
X0 = [p for p in range(NPOP) if VEL[p][0] == 0]
XM = [p for p in range(NPOP) if VEL[p][0] == -1]
ORDER = XP + X0 + XM
POS = {p: i for i, p in enumerate(ORDER)}
XOFF = {}
for i, p in enumerate(XP):
    XOFF[p] = i
for i, p in enumerate(X0):
    XOFF[p] = 8 + i
for i, p in enumerate(XM):
    XOFF[p] = 40 + i
YP = [p for p in range(NPOP) if VEL[p][1] == 1]
Y0 = [p for p in range(NPOP) if VEL[p][1] == 0]
YM = [p for p in range(NPOP) if VEL[p][1] == -1]
SLOT = {}
for i, p in enumerate(Y0):
    SLOT[p] = i
for i, p in enumerate(YP):
    SLOT[p] = 24 + 2 * i
for i, p in enumerate(YM):
    SLOT[p] = 25 + 2 * i
NX, NY, NZ = 16, 128, 2
PAD = 8
RX = NX + 2 * PAD


def zflip(p):
    return abs(VEL[p][2])


def plane(p, z, r, count=8):
    first = (POS[p] * NZ + z) * RX + PAD + r
    return slice(first, first + count)


def collide(pops):
    f, g = pops[:19], [pops[19 + 7 * a : 26 + 7 * a] for a in range(3)]
    pairs = [(i, i + 1) for i in range(1, 19, 2)]
    even = [f[i] + f[j] for i, j in pairs]
    odd = [f[i] - f[j] for i, j in pairs]
    rho = f[0] + ((even[0] + even[1]) + (even[2] + even[3])) + ((even[4] + even[5]) + ((even[6] + even[7]) + even[8]))
    mom = []
    for a in range(3):
        terms = [(odd[k], VEL[pairs[k][0]][a]) for k in range(9) if VEL[pairs[k][0]][a]]
        total = terms[0][0]
        for value, sign in terms[1:]:
            total = total + value if sign > 0 else total - value
        mom.append(total)
    inv = 1.0 / rho
    u = [m * inv for m in mom]
    b = [((g[a][0] + g[a][1]) + (g[a][2] + g[a][3])) + ((g[a][4] + g[a][5]) + g[a][6]) for a in range(3)]
    half = 0.5 * (b[0] * b[0] + b[1] * b[1] + b[2] * b[2])
    diag = [mom[a] * u[a] - b[a] * b[a] + half for a in range(3)]
    cross = {(a, c): mom[a] * u[c] - b[a] * b[c] for a, c in ((0, 1), (0, 2), (1, 2))}
    trace = diag[0] + diag[1] + diag[2]
    base = (OM_F / 36.0) * (rho - 1.5 * trace)
    d45 = [(4.5 * OM_F / 36.0) * d for d in diag]
    c9 = {k: (9.0 * OM_F / 36.0) * v for k, v in cross.items()}
    m3 = [(3.0 * OM_F / 36.0) * m for m in mom]
    keep = 1.0 - OM_F
    out = [None] * NPOP
    out[0] = keep * f[0] + 12.0 * base
    for k, (i, j) in enumerate(pairs):
        c = VEL[i]
        axes = [a for a in range(3) if c[a]]
        if len(axes) == 1:
            s = 2.0 * (base + d45[axes[0]])
            t = 2.0 * m3[axes[0]]
        else:
            a, d = axes
            s = base + d45[a] + d45[d]
            if c[a] * c[d] > 0:
                s = s + c9[(a, d)]
            else:
                s = s - c9[(a, d)]
            first = m3[a] if c[a] > 0 else -m3[a]
            t = first + m3[d] if c[d] > 0 else first - m3[d]
        out[i] = keep * f[i] + (s + t)
        out[j] = keep * f[j] + (s - t)
    keep = 1.0 - OM_G
    for a in range(3):
        rest = (OM_G / 8.0) * b[a]
        out[19 + 7 * a] = keep * g[a][0] + 2.0 * rest
        for d in range(3):
            plus, minus = rest, rest
            if d != a:
                flux = (4.0 * OM_G / 8.0) * (u[d] * b[a] - b[d] * u[a])
                plus, minus = rest + flux, rest - flux
            out[19 + 7 * a + 1 + 2 * d] = keep * g[a][1 + 2 * d] + plus
            out[19 + 7 * a + 2 + 2 * d] = keep * g[a][2 + 2 * d] + minus
    return out


def edge_rows(block, leading, tr, uu, mg):
    tr[:, 0 : NZ * RX] = block.T

    def turn(p, value):
        return pltpu.roll(value, VEL[p][0] % NY, 1) if VEL[p][0] else value

    post = collide([turn(p, tr[pl.ds(SLOT[p], 2, stride=64), :]) for p in range(NPOP)])
    own = 1 if leading == 1 else 0
    at = {}
    for p in range(NPOP):
        if VEL[p][1] == 0:
            at[p] = SLOT[p]
            uu[at[p] : at[p] + 1, :] = post[p][own : own + 1]
        elif VEL[p][1] == leading:
            at[p] = SLOT[p] - (0 if leading == 1 else 1)
            uu[at[p] : at[p] + 2, :] = post[p]
    mg[...] = uu[:, 0 : NZ * RX].T
    return at


def patched(p, z, half, leading, at, mg, value, lane):
    start = (z ^ zflip(p)) * RX + PAD + 8 * half - VEL[p][0]
    width = 2 if VEL[p][1] else 1
    first = 0 if leading == 1 else NY - width
    patch = pltpu.roll(mg[start : start + 8, :], (first - at[p]) % NY, 1)
    return jnp.where((lane >= first) & (lane < first + width), patch, value)


def near_right(shape):
    lane = lax.broadcasted_iota(jnp.int32, shape, 1)
    return (lane < 24) | (((lane < 40) | ((lane >= 88) & (lane < 104))) & (lane % 2 == 0))


def exchange(
    sizes, f_hbm, g_hbm, fo, go, fe, ge, ao, yb, fv, gv, fc, gc, corner, swap, q, w, xs, xb, tr, uu, mg,
    sems, ready,
):
    nx_dev, ny_dev = sizes
    ix, iy = lax.axis_index("gx"), lax.axis_index("gy")

    def device(dx, dy):
        return (lax.rem(ix + dx + nx_dev, nx_dev), lax.rem(iy + dy + ny_dev, ny_dev))

    block = SEAM if ny_dev % SEAM == 0 else ny_dev
    place = lax.rem(iy, block)
    is_first, is_last, is_before = place == 0, place == block - 1, place == block - 2

    corner_loaded, sent, centers_in, corners_in, below_in, beside_in = (sems.at[k] for k in range(6))
    loaded = [sems.at[6 + half] for half in range(2)]

    def wait(semaphore, rows):
        pltpu.make_async_copy(q.at[0:rows], q.at[0:rows], semaphore).wait()

    corner_loads = []
    for z in range(NZ):
        for side, r in enumerate((0, NX - 2)):
            to = slice(4 * z + 2 * side, 4 * z + 2 * side + 2)
            corner_loads += [
                pltpu.make_async_copy(f_hbm.at[:, z, r : r + 2], fc.at[:, to], corner_loaded),
                pltpu.make_async_copy(g_hbm.at[:, :, z, r : r + 2], gc.at[:, :, to], corner_loaded),
            ]

    @pl.when(is_last)
    def _():
        for copy in corner_loads:
            copy.start()

    barrier = pltpu.get_barrier_semaphore()

    def greet(steps, semaphore):
        for dx, dy in steps:
            pl.semaphore_signal(semaphore, inc=1, device_id=device(dx, dy), device_id_type=MESH)

    above = [(-1, 1), (0, 1), (1, 1)]

    @pl.when(is_last)
    def _():
        pl.semaphore_wait(barrier, 3)
        greet([(0, 1)], ready)

    for half in range(2):
        rows = slice(8 * half, 8 * half + 8)
        pltpu.make_async_copy(f_hbm.at[:, :, rows], fv.at[:, :, rows], loaded[half]).start()
        pltpu.make_async_copy(g_hbm.at[:, :, :, rows], gv.at[:, :, :, rows], loaded[half]).start()

    beside = [(-1, 0), (1, 0)]
    below = [(-1, -1), (0, -1), (1, -1)]

    @pl.when(is_last)
    def _():
        greet(below, barrier)

    @pl.when(jnp.logical_not(is_last))
    def _():
        greet(below + beside, barrier)

        @pl.when(jnp.logical_not(is_before))
        def _():
            greet(above, barrier)

    low, high, own = slice(0, 8), slice(24, 32), slice(8, 24)
    first, last = slice(8, 16), slice(16, 24)

    def to(src, dst, dx, dy, semaphore):
        return pltpu.make_async_remote_copy(
            src_ref=src, dst_ref=dst, send_sem=sent, recv_sem=semaphore,
            device_id=device(dx, dy), device_id_type=MESH,
        )

    def corners(block, side, dy, semaphore, lo, hi):
        return [
            to(block.at[:, lo : lo + 2], yb.at[side, :, 24:26], -1, dy, semaphore),
            to(block.at[:, hi : hi + 2], yb.at[side, :, 6:8], 1, dy, semaphore),
        ]

    early = corners(corner, 0, 1, corners_in, 0, 2)
    above_corners = corners(ao, 0, 1, corners_in, 8, 22)
    above_center = to(ao.at[:, own], yb.at[0, :, own], 0, 1, centers_in)
    to_below = corners(ao, 1, -1, below_in, 8, 22) + [to(ao.at[:, own], yb.at[1, :, own], 0, -1, below_in)]
    with_corners = to(ao.at[:, 6:26], yb.at[1, :, 6:26], 0, -1, below_in)
    to_beside = [
        to(xs.at[0], xb.at[0, :, 0:40], 1, 0, beside_in),
        to(xs.at[1], xb.at[1, :, 8:48], -1, 0, beside_in),
        to(ao.at[:, last], ao.at[:, low], 1, 0, beside_in),
        to(ao.at[:, first], ao.at[:, high], -1, 0, beside_in),
    ]

    def start(copies):
        for copy in copies:
            copy.start()

    @pl.when(is_last)
    def _():
        wait(corner_loaded, 8 * NPOP)
        pops = [fc[p] for p in range(19)] + [gc[a, j] for a in range(3) for j in range(7)]
        post = collide(pops)
        lane = lax.broadcasted_iota(jnp.int32, (8, NY), 1)
        up = [[jnp.zeros((8, NY), F32) for _ in range(4)] for _ in range(2)]
        columns = [(p, SLOT[p], NY - 1 - (1 if VEL[p][1] else 0)) for p in Y0 + YP]
        columns += [(p, SLOT[p] + 64, NY - 1) for p in YP]
        for k, (p, s, column) in enumerate(columns):
            moved = pltpu.roll(post[p], (s - column) % NY, 1)
            up[zflip(p)][k % 4] = jnp.where(lane == s, moved, up[zflip(p)][k % 4])
        up = [(part[0] + part[1]) + (part[2] + part[3]) for part in up]
        swap[...] = up[1]
        corner[0] = up[0][0:4] + swap[4:8, :]
        corner[1] = up[0][4:8] + swap[0:4, :]
        start(early)

    lane = lax.broadcasted_iota(jnp.int32, (8, NY), 1)
    for half in range(2):
        rows = slice(8 * half, 8 * half + 8)
        at = slice(PAD + 8 * half, PAD + 8 * half + 8)
        up = [jnp.zeros((8, NY), F32) for _ in range(NZ)]
        down = [jnp.zeros((8, NY), F32) for _ in range(NZ)]
        wait(loaded[half], 8 * NZ * NPOP)
        for z in range(NZ):
            pops = [fv[p, z, rows, :] for p in range(19)]
            pops += [gv[a, j, z, rows, :] for a in range(3) for j in range(7)]
            post = collide(pops)
            for p in range(NPOP):
                zz = z ^ zflip(p)
                q[plane(p, zz, 8 * half), :] = post[p]
                s = SLOT[p]
                if VEL[p][1] == 0:
                    moved = pltpu.roll(post[p], s + 1, 1)
                    up[zz] = jnp.where(lane == s, moved, up[zz])
                    down[zz] = jnp.where(lane == s + 1, moved, down[zz])
                elif VEL[p][1] == 1:
                    moved = pltpu.roll(post[p], s + 2, 1)
                    up[zz] = jnp.where((lane == s) | (lane == s + 1), moved, up[zz])
                else:
                    moved = pltpu.roll(post[p], s, 1)
                    down[zz] = jnp.where((lane == s) | (lane == s + 1), moved, down[zz])
        for z in range(NZ):
            here = jnp.where((lane < 24) | ((lane < 40) & (lane % 2 == 0)), up[z], down[z])
            there = jnp.where((lane >= 25) & (lane < 40) & (lane % 2 == 1), up[z], down[z])
            ao[z, at, :] = jnp.where(lane < 64, here, pltpu.roll(there, 63, 1))
    @pl.when(is_first)
    def _():
        pl.semaphore_wait(barrier, 5)

    @pl.when(jnp.logical_not(is_first | is_last))
    def _():
        pl.semaphore_wait(barrier, 8)

    @pl.when(is_before)
    def _():
        greet([(0, 1)], ready)

    @pl.when(jnp.logical_not(is_last))
    def _():
        start(above_corners)

    above_center.start()

    def row(first, count, z, r):
        return q[pl.ds(first * NZ * RX + z * RX + PAD + r, count, stride=NZ * RX), :]

    for z in range(NZ):
        xs[0, z, 0:8, :] = row(0, 8, z, NX - 2)
        xs[0, z, 8:32, :] = row(8, 24, z, NX - 1)
        xs[0, z, 32:40, :] = row(0, 8, z, NX - 1)
        xs[1, z, 0:24, :] = row(8, 24, z, 0)
        xs[1, z, 24:32, :] = row(32, 8, z, 0)
        xs[1, z, 32:40, :] = row(32, 8, z, 1)
        xb[0, z, 40:48, :] = row(32, 8, z, 0)
        xb[1, z, 0:8, :] = row(0, 8, z, NX - 1)

    @pl.when(is_last)
    def _():
        pl.semaphore_wait(ready, 1)

    start(to_beside)

    @pl.when(jnp.logical_not(is_first))
    def _():
        start(to_below)

    wait(beside_in, 2 * NZ * 48)

    def turn(p, value):
        return pltpu.roll(value, VEL[p][1] % NY, 1) if VEL[p][1] else value

    for i in range(8):
        for z in range(NZ):
            q[plane(XP[i], z, -1, 1), :] = xb[0, z, 32 + i : 33 + i, :]
            q[plane(XM[i], z, NX, 1), :] = xb[1, z, 32 + i : 33 + i, :]
    edges = []
    for p in range(NPOP):
        at = slice(XOFF[p], XOFF[p] + 1)
        edges.append(turn(p, jnp.concatenate([xb[side, z, at, :] for side in range(2) for z in range(NZ)], axis=0)))
    edges = collide(edges)
    for p in range(NPOP):
        for z in range(NZ):
            zz = z ^ zflip(p)
            if VEL[p][0] == 1:
                w[plane(p, zz, -1, 1), :] = edges[p][z : z + 1]
            elif VEL[p][0] == -1:
                w[plane(p, zz, NX, 1), :] = edges[p][NZ + z : NZ + z + 1]
    for z in range(NZ):
        for half in range(2):
            post = collide([turn(p, q[plane(p, z, 8 * half - VEL[p][0]), :]) for p in range(NPOP)])
            for p in range(NPOP):
                w[plane(p, z ^ zflip(p), 8 * half), :] = post[p]
    for p in range(NPOP):
        for z in range(NZ):
            for half in range(2):
                value = turn(p, w[plane(p, z, 8 * half - VEL[p][0]), :])
                rows = slice(8 * half, 8 * half + 8)
                if p < 19:
                    fo[p, z, rows, :] = value
                else:
                    go[(p - 19) // 7, (p - 19) % 7, z, rows, :] = value

    wait(below_in, NZ * 20)
    tall = near_right((NZ * RX, NY))
    flat = ao[...].reshape(NZ * RX, NY)

    def patch(leading, block):
        places = edge_rows(block, leading, tr, uu, mg)
        for p in places:
            for z in range(NZ):
                for half in range(2):
                    rows = slice(8 * half, 8 * half + 8)
                    if p < 19:
                        fo[p, z, rows, :] = patched(p, z, half, leading, places, mg, fo[p, z, rows, :], lane)
                    else:
                        a, j = (p - 19) // 7, (p - 19) % 7
                        go[a, j, z, rows, :] = patched(p, z, half, leading, places, mg, go[a, j, z, rows, :], lane)

    patch(-1, jnp.where(tall, flat, yb[1].reshape(NZ * RX, NY)))

    @pl.when(is_first)
    def _():
        pl.semaphore_wait(ready, 1)
        with_corners.start()

    wait(centers_in, NZ * NX)
    middle = [
        part
        for z in range(NZ)
        for part in (ao[z, low], jnp.where(tall[0:NX], yb[0, z, own], ao[z, own]), ao[z, high])
    ]
    patch(1, jnp.concatenate(middle, axis=0))
    for z in range(NZ):
        for side, r in enumerate((0, NX - 2)):
            to = slice(4 * z + 2 * side, 4 * z + 2 * side + 2)
            for p in range(19):
                fe[p, to, :] = fo[p, z, r : r + 2, :]
            for a in range(3):
                for j in range(7):
                    ge[a, j, to, :] = go[a, j, z, r : r + 2, :]

    wait(sent, NZ * (20 + 20) + 2 * NZ * 48)
    wait(corners_in, NZ * 4)


def finish(fi, gi, fe, ge, ao, yb, f_hbm, g_hbm, near, post_rows, fo, go, out_sem):
    stored_f, stored_g = out_sem.at[0], out_sem.at[1]
    pltpu.make_async_copy(fi.at[:, :, 2 : NX - 2], f_hbm.at[:, :, 2 : NX - 2], stored_f).start()
    pltpu.make_async_copy(gi.at[:, :, :, 2 : NX - 2], g_hbm.at[:, :, :, 2 : NX - 2], stored_g).start()

    mask = near_right((2, NY))
    for cx in (-1, 0, 1):
        for z in range(NZ):
            for k, r in enumerate((-1, NX - 1)):
                first = z * RX + PAD + r - cx
                rows = slice(first, first + 2)
                near[cx % 3, 4 * z + 2 * k : 4 * z + 2 * k + 2, :] = jnp.where(mask, yb[0, rows, :], ao[rows, :])
    sources = [near[cx] for cx in range(3)]
    post = collide([pltpu.roll(sources[VEL[p][0] % 3], (64 - SLOT[p]) % NY, 1) for p in range(NPOP)])
    lane = lax.broadcasted_iota(jnp.int32, (8, NY), 1)
    row = lax.broadcasted_iota(jnp.int32, (8, NY), 0)
    row = row % 4
    for p in range(NPOP):
        cx, cy, _ = VEL[p]
        at = (fe, fo, p) if p < 19 else (ge, go, ((p - 19) // 7, (p - 19) % 7))
        value = at[0][at[2]]
        if cy >= 0:
            new = post[p]
            if cy:
                new = jnp.where(lane == 0, pltpu.roll(new, 64, 1), pltpu.roll(new, 1, 1))
            turned = 4 * zflip(p)
            if turned or not cx:
                base = 16 * p
                post_rows[base : base + 8, :] = new
                post_rows[base + 8 : base + 16, :] = new
            if cx:
                if turned:
                    new = post_rows[base + turned : base + turned + 8, :]
                reached = row < 2 if cx > 0 else row >= 2
                value = jnp.where(reached & (lane <= cy), new, value)
            else:
                for shift, reached in ((1, row == 0), (-1, row == 3)):
                    first = base + (turned + shift) % 8
                    value = jnp.where(reached & (lane <= cy), post_rows[first : first + 8, :], value)
        at[1][at[2]] = value
    for z in range(NZ):
        for side, r in enumerate((0, NX - 2)):
            rows = slice(4 * z + 2 * side, 4 * z + 2 * side + 2)
            pltpu.make_async_copy(fo.at[:, rows], f_hbm.at[:, z, r : r + 2], stored_f).start()
            pltpu.make_async_copy(go.at[:, :, rows], g_hbm.at[:, :, z, r : r + 2], stored_g).start()
    pltpu.make_async_copy(fi, f_hbm, stored_f).wait()
    pltpu.make_async_copy(gi, g_hbm, stored_g).wait()


def per_device(sizes, fluid_pops, magnet_pops):
    vmem = pl.BlockSpec(memory_space=pltpu.VMEM)
    hbm = pl.BlockSpec(memory_space=pltpu.HBM)
    fluid, magnet = (19, NZ, NX, NY), (3, 7, NZ, NX, NY)
    columns = (NZ, RX, NY)
    turned = [pltpu.VMEM((NY, NY), F32), pltpu.VMEM((NY, NY), F32), pltpu.VMEM((NZ * RX, NY), F32)]
    edge_f, edge_g = (19, 8, NY), (3, 7, 8, NY)
    fo, go, fe, ge, ao, yb = pl.pallas_call(
        functools.partial(exchange, sizes),
        out_shape=[pltpu.VMEM(shape, F32) for shape in (fluid, magnet, edge_f, edge_g, columns, (2, *columns))],
        in_specs=[hbm] * 2,
        out_specs=[vmem] * 6,
        scratch_shapes=[
            pltpu.VMEM(fluid, F32),
            pltpu.VMEM(magnet, F32),
            pltpu.VMEM((19, 8, NY), F32),
            pltpu.VMEM((3, 7, 8, NY), F32),
            pltpu.VMEM((NZ, 4, NY), F32),
            pltpu.VMEM((8, NY), F32),
            pltpu.VMEM((NPOP * NZ * RX, NY), F32),
            pltpu.VMEM((NPOP * NZ * RX, NY), F32),
            pltpu.VMEM((2, NZ, 40, NY), F32),
            pltpu.VMEM((2, NZ, 48, NY), F32),
            *turned,
            pltpu.SemaphoreType.DMA((8,)),
            pltpu.SemaphoreType.REGULAR,
        ],
        compiler_params=pltpu.CompilerParams(
            collective_id=0, has_side_effects=True, vmem_limit_bytes=VMEM_LIMIT
        ),
    )(
        pltpu.with_memory_space_constraint(fluid_pops, pltpu.HBM),
        pltpu.with_memory_space_constraint(magnet_pops, pltpu.HBM),
    )
    return pl.pallas_call(
        finish,
        out_shape=[jax.ShapeDtypeStruct(fluid, F32), jax.ShapeDtypeStruct(magnet, F32)],
        in_specs=[vmem] * 6,
        out_specs=[hbm] * 2,
        scratch_shapes=[
            pltpu.VMEM((3, 8, NY), F32),
            pltpu.VMEM((16 * NPOP, NY), F32),
            pltpu.VMEM(edge_f, F32),
            pltpu.VMEM(edge_g, F32),
            pltpu.SemaphoreType.DMA((2,)),
        ],
        compiler_params=pltpu.CompilerParams(vmem_limit_bytes=VMEM_LIMIT),
    )(fo, go, fe, ge, ao.reshape(NZ * RX, NY), yb.reshape(2, NZ * RX, NY))


VMEM_LIMIT = 48 << 20
SEAM = 16


def solution(mesh):
    specs = (P(None, None, "gx", "gy"), P(None, None, None, "gx", "gy"))
    return jax.shard_map(
        functools.partial(per_device, (mesh.shape["gx"], mesh.shape["gy"])),
        mesh=mesh,
        in_specs=specs,
        out_specs=specs,
        check_vma=False,
    )
```

```python
import functools

import jax
import jax.numpy as jnp
from jax import lax
from jax.experimental import pallas as pl
from jax.experimental.pallas import tpu as pltpu
from jax.sharding import PartitionSpec as P

MESH = pl.DeviceIdType.MESH
F32 = jnp.float32

FLUID = [
    (0, 0, 0),
    (1, 0, 0), (-1, 0, 0), (0, 1, 0), (0, -1, 0), (0, 0, 1), (0, 0, -1),
    (1, 1, 0), (-1, -1, 0), (1, -1, 0), (-1, 1, 0),
    (1, 0, 1), (-1, 0, -1), (1, 0, -1), (-1, 0, 1),
    (0, 1, 1), (0, -1, -1), (0, 1, -1), (0, -1, 1),
]
VEL = FLUID + FLUID[:7] * 3
NPOP = 40
OM_F = 1.0 / 0.9
OM_G = 1.0 / 0.8

XP = [p for p in range(NPOP) if VEL[p][0] == 1]
X0 = [p for p in range(NPOP) if VEL[p][0] == 0]
XM = [p for p in range(NPOP) if VEL[p][0] == -1]
ORDER = XP + X0 + XM
POS = {p: i for i, p in enumerate(ORDER)}
XOFF = {}
for i, p in enumerate(XP):
    XOFF[p] = i
for i, p in enumerate(X0):
    XOFF[p] = 8 + i
for i, p in enumerate(XM):
    XOFF[p] = 40 + i
YP = [p for p in range(NPOP) if VEL[p][1] == 1]
Y0 = [p for p in range(NPOP) if VEL[p][1] == 0]
YM = [p for p in range(NPOP) if VEL[p][1] == -1]
SLOT = {}
for i, p in enumerate(Y0):
    SLOT[p] = i
for i, p in enumerate(YP):
    SLOT[p] = 24 + 2 * i
for i, p in enumerate(YM):
    SLOT[p] = 25 + 2 * i
NX, NY, NZ = 16, 128, 2
PAD = 8
RX = NX + 2 * PAD


def zflip(p):
    return abs(VEL[p][2])


def plane(p, z, r, count=8):
    first = (POS[p] * NZ + z) * RX + PAD + r
    return slice(first, first + count)


def collide(pops):
    f, g = pops[:19], [pops[19 + 7 * a : 26 + 7 * a] for a in range(3)]
    pairs = [(i, i + 1) for i in range(1, 19, 2)]
    even = [f[i] + f[j] for i, j in pairs]
    odd = [f[i] - f[j] for i, j in pairs]
    rho = f[0] + ((even[0] + even[1]) + (even[2] + even[3])) + ((even[4] + even[5]) + ((even[6] + even[7]) + even[8]))
    mom = []
    for a in range(3):
        terms = [(odd[k], VEL[pairs[k][0]][a]) for k in range(9) if VEL[pairs[k][0]][a]]
        total = terms[0][0]
        for value, sign in terms[1:]:
            total = total + value if sign > 0 else total - value
        mom.append(total)
    u = [m / rho for m in mom]
    b = [((g[a][0] + g[a][1]) + (g[a][2] + g[a][3])) + ((g[a][4] + g[a][5]) + g[a][6]) for a in range(3)]
    half = 0.5 * (b[0] * b[0] + b[1] * b[1] + b[2] * b[2])
    diag = [mom[a] * u[a] - b[a] * b[a] + half for a in range(3)]
    cross = {(a, c): mom[a] * u[c] - b[a] * b[c] for a, c in ((0, 1), (0, 2), (1, 2))}
    trace = diag[0] + diag[1] + diag[2]
    base = (OM_F / 36.0) * (rho - 1.5 * trace)
    d45 = [(4.5 * OM_F / 36.0) * d for d in diag]
    c9 = {k: (9.0 * OM_F / 36.0) * v for k, v in cross.items()}
    m3 = [(3.0 * OM_F / 36.0) * m for m in mom]
    keep = 1.0 - OM_F
    out = [None] * NPOP
    out[0] = keep * f[0] + 12.0 * base
    for k, (i, j) in enumerate(pairs):
        c = VEL[i]
        axes = [a for a in range(3) if c[a]]
        if len(axes) == 1:
            s = 2.0 * (base + d45[axes[0]])
            t = 2.0 * m3[axes[0]]
        else:
            a, d = axes
            s = base + d45[a] + d45[d]
            if c[a] * c[d] > 0:
                s = s + c9[(a, d)]
            else:
                s = s - c9[(a, d)]
            first = m3[a] if c[a] > 0 else -m3[a]
            t = first + m3[d] if c[d] > 0 else first - m3[d]
        out[i] = keep * f[i] + (s + t)
        out[j] = keep * f[j] + (s - t)
    keep = 1.0 - OM_G
    for a in range(3):
        rest = (OM_G / 8.0) * b[a]
        out[19 + 7 * a] = keep * g[a][0] + 2.0 * rest
        for d in range(3):
            plus, minus = rest, rest
            if d != a:
                flux = (4.0 * OM_G / 8.0) * (u[d] * b[a] - b[d] * u[a])
                plus, minus = rest + flux, rest - flux
            out[19 + 7 * a + 1 + 2 * d] = keep * g[a][1 + 2 * d] + plus
            out[19 + 7 * a + 2 + 2 * d] = keep * g[a][2 + 2 * d] + minus
    return out


def edge_rows(block, leading, tr, uu, mg):
    tr[0:NY, 0 : NZ * RX] = block.T

    def turn(p, value):
        return pltpu.roll(value, VEL[p][0] % NY, 1) if VEL[p][0] else value

    post = collide([turn(p, tr[pl.ds(SLOT[p], 2, stride=64), :]) for p in range(NPOP)])
    own = 1 if leading == 1 else 0
    at = {}
    for p in range(NPOP):
        if VEL[p][1] == 0:
            at[p] = SLOT[p]
            uu[at[p] : at[p] + 1, :] = post[p][own : own + 1]
        elif VEL[p][1] == leading:
            at[p] = SLOT[p] - (0 if leading == 1 else 1)
            uu[at[p] : at[p] + 2, :] = post[p]
    mg[...] = uu[:, 0 : NZ * RX].T
    return at


def patched(p, z, half, leading, at, mg, value, lane):
    start = (z ^ zflip(p)) * RX + PAD + 8 * half - VEL[p][0]
    width = 2 if VEL[p][1] else 1
    first = 0 if leading == 1 else NY - width
    patch = pltpu.roll(mg[start : start + 8, :], (first - at[p]) % NY, 1)
    return jnp.where((lane >= first) & (lane < first + width), patch, value)


def near_right(shape):
    lane = lax.broadcasted_iota(jnp.int32, shape, 1)
    return (lane < 24) | (((lane < 40) | ((lane >= 88) & (lane < 104))) & (lane % 2 == 0))


def exchange(
    sizes, f_hbm, g_hbm, fo, go, fe, ge, ao, yb, fv, gv, fc, gc, corner, q, w, xs, xb, tr, uu, mg,
    sems, ready,
):
    nx_dev, ny_dev = sizes
    ix, iy = lax.axis_index("gx"), lax.axis_index("gy")

    def device(dx, dy):
        return (lax.rem(ix + dx + nx_dev, nx_dev), lax.rem(iy + dy + ny_dev, ny_dev))

    block = SEAM if ny_dev % SEAM == 0 else ny_dev
    place = lax.rem(iy, block)
    is_first, is_last, is_before = place == 0, place == block - 1, place == block - 2

    sent, centers_in, corners_in, below_in, beside_in = (sems.at[k] for k in range(5))
    loaded = [sems.at[5 + half] for half in range(2)]
    corner_loaded = [sems.at[7 + side] for side in range(2)]

    def wait(semaphore, rows):
        pltpu.make_async_copy(q.at[0:rows], q.at[0:rows], semaphore).wait()

    @pl.when(is_last)
    def _():
        for side, r in enumerate((0, NX - 2)):
            pltpu.make_async_copy(f_hbm.at[:, :, r : r + 2], fc.at[side], corner_loaded[side]).start()
            pltpu.make_async_copy(g_hbm.at[:, :, :, r : r + 2], gc.at[side], corner_loaded[side]).start()

    barrier = pltpu.get_barrier_semaphore()

    def greet(steps, semaphore):
        for dx, dy in steps:
            pl.semaphore_signal(semaphore, inc=1, device_id=device(dx, dy), device_id_type=MESH)

    above = [(-1, 1), (0, 1), (1, 1)]

    @pl.when(is_last)
    def _():
        pl.semaphore_wait(barrier, 3)
        greet([(0, 1)], ready)

    for half in range(2):
        rows = slice(8 * half, 8 * half + 8)
        pltpu.make_async_copy(f_hbm.at[:, :, rows], fv.at[:, :, rows], loaded[half]).start()
        pltpu.make_async_copy(g_hbm.at[:, :, :, rows], gv.at[:, :, :, rows], loaded[half]).start()

    beside = [(-1, 0), (1, 0)]
    below = [(-1, -1), (0, -1), (1, -1)]

    @pl.when(is_last)
    def _():
        greet(below, barrier)

    @pl.when(jnp.logical_not(is_last))
    def _():
        greet(below + beside, barrier)

        @pl.when(jnp.logical_not(is_before))
        def _():
            greet(above, barrier)

    low, high, own = slice(0, 8), slice(24, 32), slice(8, 24)
    first, last = slice(8, 16), slice(16, 24)

    def to(src, dst, dx, dy, semaphore):
        return pltpu.make_async_remote_copy(
            src_ref=src, dst_ref=dst, send_sem=sent, recv_sem=semaphore,
            device_id=device(dx, dy), device_id_type=MESH,
        )

    def corners(block, side, dy, semaphore, lo, hi):
        return [
            to(block.at[:, lo : lo + 2], yb.at[side, :, 24:26], -1, dy, semaphore),
            to(block.at[:, hi : hi + 2], yb.at[side, :, 6:8], 1, dy, semaphore),
        ]

    early = [
        to(corner.at[0], yb.at[0, :, 24:26], -1, 1, corners_in),
        to(corner.at[1], yb.at[0, :, 6:8], 1, 1, corners_in),
    ]
    above_corners = corners(ao, 0, 1, corners_in, 8, 22)
    above_center = to(ao.at[:, own], yb.at[0, :, own], 0, 1, centers_in)
    to_below = corners(ao, 1, -1, below_in, 8, 22) + [to(ao.at[:, own], yb.at[1, :, own], 0, -1, below_in)]
    with_corners = to(ao.at[:, 6:26], yb.at[1, :, 6:26], 0, -1, below_in)
    to_beside = [
        to(xs.at[0], xb.at[0, :, 0:40], 1, 0, beside_in),
        to(xs.at[1], xb.at[1, :, 8:48], -1, 0, beside_in),
        to(ao.at[:, last], ao.at[:, low], 1, 0, beside_in),
        to(ao.at[:, first], ao.at[:, high], -1, 0, beside_in),
    ]

    def start(copies):
        for copy in copies:
            copy.start()

    @pl.when(is_last)
    def _():
        lane = lax.broadcasted_iota(jnp.int32, (2, NY), 1)
        columns = [(p, SLOT[p], NY - 1 - (1 if VEL[p][1] else 0)) for p in Y0 + YP]
        columns += [(p, SLOT[p] + 64, NY - 1) for p in YP]
        for side in range(2):
            wait(corner_loaded[side], 2 * NZ * NPOP)
            up = [[jnp.zeros((2, NY), F32) for _ in range(4)] for _ in range(NZ)]
            for z in range(NZ):
                pops = [fc[side, p, z] for p in range(19)] + [gc[side, a, j, z] for a in range(3) for j in range(7)]
                post = collide(pops)
                for k, (p, s, column) in enumerate(columns):
                    part = up[z ^ zflip(p)]
                    part[k % 4] = jnp.where(lane == s, pltpu.roll(post[p], (s - column) % NY, 1), part[k % 4])
            for z in range(NZ):
                corner[side, z] = (up[z][0] + up[z][1]) + (up[z][2] + up[z][3])
            early[side].start()

    lane = lax.broadcasted_iota(jnp.int32, (8, NY), 1)
    for half in range(2):
        rows = slice(8 * half, 8 * half + 8)
        at = slice(PAD + 8 * half, PAD + 8 * half + 8)
        up = [jnp.zeros((8, NY), F32) for _ in range(NZ)]
        down = [jnp.zeros((8, NY), F32) for _ in range(NZ)]
        wait(loaded[half], 8 * NZ * NPOP)
        for z in range(NZ):
            pops = [fv[p, z, rows, :] for p in range(19)]
            pops += [gv[a, j, z, rows, :] for a in range(3) for j in range(7)]
            post = collide(pops)
            for p in range(NPOP):
                zz = z ^ zflip(p)
                q[plane(p, zz, 8 * half), :] = post[p]
                s = SLOT[p]
                if VEL[p][1] == 0:
                    moved = pltpu.roll(post[p], s + 1, 1)
                    up[zz] = jnp.where(lane == s, moved, up[zz])
                    down[zz] = jnp.where(lane == s + 1, moved, down[zz])
                elif VEL[p][1] == 1:
                    moved = pltpu.roll(post[p], s + 2, 1)
                    up[zz] = jnp.where((lane == s) | (lane == s + 1), moved, up[zz])
                else:
                    moved = pltpu.roll(post[p], s, 1)
                    down[zz] = jnp.where((lane == s) | (lane == s + 1), moved, down[zz])
        for z in range(NZ):
            here = jnp.where((lane < 24) | ((lane < 40) & (lane % 2 == 0)), up[z], down[z])
            there = jnp.where((lane >= 25) & (lane < 40) & (lane % 2 == 1), up[z], down[z])
            ao[z, at, :] = jnp.where(lane < 64, here, pltpu.roll(there, 63, 1))
    @pl.when(is_first)
    def _():
        pl.semaphore_wait(barrier, 5)

    @pl.when(jnp.logical_not(is_first | is_last))
    def _():
        pl.semaphore_wait(barrier, 8)

    @pl.when(is_before)
    def _():
        greet([(0, 1)], ready)

    @pl.when(jnp.logical_not(is_last))
    def _():
        start(above_corners)

    above_center.start()

    def row(first, count, z, r):
        return q[pl.ds(first * NZ * RX + z * RX + PAD + r, count, stride=NZ * RX), :]

    for z in range(NZ):
        xs[0, z, 0:8, :] = row(0, 8, z, NX - 2)
        xs[0, z, 8:32, :] = row(8, 24, z, NX - 1)
        xs[0, z, 32:40, :] = row(0, 8, z, NX - 1)
        xs[1, z, 0:24, :] = row(8, 24, z, 0)
        xs[1, z, 24:32, :] = row(32, 8, z, 0)
        xs[1, z, 32:40, :] = row(32, 8, z, 1)
        xb[0, z, 40:48, :] = row(32, 8, z, 0)
        xb[1, z, 0:8, :] = row(0, 8, z, NX - 1)

    @pl.when(is_last)
    def _():
        pl.semaphore_wait(ready, 1)

    start(to_beside)

    @pl.when(jnp.logical_not(is_first))
    def _():
        start(to_below)

    wait(beside_in, 2 * NZ * 48)

    def turn(p, value):
        return pltpu.roll(value, VEL[p][1] % NY, 1) if VEL[p][1] else value

    for i in range(8):
        for z in range(NZ):
            q[plane(XP[i], z, -1, 1), :] = xb[0, z, 32 + i : 33 + i, :]
            q[plane(XM[i], z, NX, 1), :] = xb[1, z, 32 + i : 33 + i, :]
    edges = []
    for p in range(NPOP):
        at = slice(XOFF[p], XOFF[p] + 1)
        edges.append(turn(p, jnp.concatenate([xb[side, z, at, :] for side in range(2) for z in range(NZ)], axis=0)))
    edges = collide(edges)
    for p in range(NPOP):
        for z in range(NZ):
            zz = z ^ zflip(p)
            if VEL[p][0] == 1:
                w[plane(p, zz, -1, 1), :] = edges[p][z : z + 1]
            elif VEL[p][0] == -1:
                w[plane(p, zz, NX, 1), :] = edges[p][NZ + z : NZ + z + 1]
    for z in range(NZ):
        for half in range(2):
            post = collide([turn(p, q[plane(p, z, 8 * half - VEL[p][0]), :]) for p in range(NPOP)])
            for p in range(NPOP):
                w[plane(p, z ^ zflip(p), 8 * half), :] = post[p]
    for p in range(NPOP):
        for z in range(NZ):
            for half in range(2):
                value = turn(p, w[plane(p, z, 8 * half - VEL[p][0]), :])
                rows = slice(8 * half, 8 * half + 8)
                if p < 19:
                    fo[p, z, rows, :] = value
                else:
                    go[(p - 19) // 7, (p - 19) % 7, z, rows, :] = value

    wait(below_in, NZ * 20)
    tall = near_right((NZ * RX, NY))
    flat = ao[...].reshape(NZ * RX, NY)

    def patch(leading, block):
        places = edge_rows(block, leading, tr, uu, mg)
        for p in places:
            for z in range(NZ):
                for half in range(2):
                    rows = slice(8 * half, 8 * half + 8)
                    if p < 19:
                        fo[p, z, rows, :] = patched(p, z, half, leading, places, mg, fo[p, z, rows, :], lane)
                    else:
                        a, j = (p - 19) // 7, (p - 19) % 7
                        go[a, j, z, rows, :] = patched(p, z, half, leading, places, mg, go[a, j, z, rows, :], lane)

    patch(-1, jnp.where(tall, flat, yb[1].reshape(NZ * RX, NY)))

    @pl.when(is_first)
    def _():
        pl.semaphore_wait(ready, 1)
        with_corners.start()

    wait(centers_in, NZ * NX)
    middle = [
        part
        for z in range(NZ)
        for part in (ao[z, low], jnp.where(tall[0:NX], yb[0, z, own], ao[z, own]), ao[z, high])
    ]
    patch(1, jnp.concatenate(middle, axis=0))
    for z in range(NZ):
        for side, r in enumerate((0, NX - 2)):
            to = slice(4 * z + 2 * side, 4 * z + 2 * side + 2)
            for p in range(19):
                fe[p, to, :] = fo[p, z, r : r + 2, :]
            for a in range(3):
                for j in range(7):
                    ge[a, j, to, :] = go[a, j, z, r : r + 2, :]

    wait(sent, NZ * (20 + 20) + 2 * NZ * 48)
    wait(corners_in, NZ * 4)


def finish(fi, gi, fe, ge, ao, yb, f_hbm, g_hbm, near, post_rows, fo, go, out_sem):
    stored_f, stored_g = out_sem.at[0], out_sem.at[1]
    pltpu.make_async_copy(fi.at[:, :, 2 : NX - 2], f_hbm.at[:, :, 2 : NX - 2], stored_f).start()
    pltpu.make_async_copy(gi.at[:, :, :, 2 : NX - 2], g_hbm.at[:, :, :, 2 : NX - 2], stored_g).start()

    mask = near_right((2, NY))
    for cx in (-1, 0, 1):
        for z in range(NZ):
            for k, r in enumerate((-1, NX - 1)):
                first = z * RX + PAD + r - cx
                rows = slice(first, first + 2)
                near[cx % 3, 4 * z + 2 * k : 4 * z + 2 * k + 2, :] = jnp.where(mask, yb[0, rows, :], ao[rows, :])
    sources = [near[cx] for cx in range(3)]
    post = collide([pltpu.roll(sources[VEL[p][0] % 3], (64 - SLOT[p]) % NY, 1) for p in range(NPOP)])
    lane = lax.broadcasted_iota(jnp.int32, (8, NY), 1)
    row = lax.broadcasted_iota(jnp.int32, (8, NY), 0)
    row = row % 4
    for p in range(NPOP):
        cx, cy, _ = VEL[p]
        at = (fe, fo, p) if p < 19 else (ge, go, ((p - 19) // 7, (p - 19) % 7))
        value = at[0][at[2]]
        if cy >= 0:
            new = post[p]
            if cy:
                new = jnp.where(lane == 0, pltpu.roll(new, 64, 1), pltpu.roll(new, 1, 1))
            turned = 4 * zflip(p)
            if turned or not cx:
                base = 16 * p
                post_rows[base : base + 8, :] = new
                post_rows[base + 8 : base + 16, :] = new
            if cx:
                if turned:
                    new = post_rows[base + turned : base + turned + 8, :]
                reached = row < 2 if cx > 0 else row >= 2
                value = jnp.where(reached & (lane <= cy), new, value)
            else:
                for shift, reached in ((1, row == 0), (-1, row == 3)):
                    first = base + (turned + shift) % 8
                    value = jnp.where(reached & (lane <= cy), post_rows[first : first + 8, :], value)
        at[1][at[2]] = value
    for z in range(NZ):
        for side, r in enumerate((0, NX - 2)):
            rows = slice(4 * z + 2 * side, 4 * z + 2 * side + 2)
            pltpu.make_async_copy(fo.at[:, rows], f_hbm.at[:, z, r : r + 2], stored_f).start()
            pltpu.make_async_copy(go.at[:, :, rows], g_hbm.at[:, :, z, r : r + 2], stored_g).start()
    pltpu.make_async_copy(fi, f_hbm, stored_f).wait()
    pltpu.make_async_copy(gi, g_hbm, stored_g).wait()


def per_device(sizes, fluid_pops, magnet_pops):
    vmem = pl.BlockSpec(memory_space=pltpu.VMEM)
    hbm = pl.BlockSpec(memory_space=pltpu.HBM)
    fluid, magnet = (19, NZ, NX, NY), (3, 7, NZ, NX, NY)
    columns = (NZ, RX, NY)
    turned = [pltpu.VMEM((NY + 64, NY), F32), pltpu.VMEM((NY, NY), F32), pltpu.VMEM((NZ * RX, NY), F32)]
    edge_f, edge_g = (19, 8, NY), (3, 7, 8, NY)
    fo, go, fe, ge, ao, yb = pl.pallas_call(
        functools.partial(exchange, sizes),
        out_shape=[pltpu.VMEM(shape, F32) for shape in (fluid, magnet, edge_f, edge_g, columns, (2, *columns))],
        in_specs=[hbm] * 2,
        out_specs=[vmem] * 6,
        scratch_shapes=[
            pltpu.VMEM(fluid, F32),
            pltpu.VMEM(magnet, F32),
            pltpu.VMEM((2, 19, NZ, 2, NY), F32),
            pltpu.VMEM((2, 3, 7, NZ, 2, NY), F32),
            pltpu.VMEM((2, NZ, 2, NY), F32),
            pltpu.VMEM(((NPOP + 1) * NZ * RX, NY), F32),
            pltpu.VMEM((NPOP * NZ * RX, NY), F32),
            pltpu.VMEM((2, NZ, 40, NY), F32),
            pltpu.VMEM((2, NZ, 48, NY), F32),
            *turned,
            pltpu.SemaphoreType.DMA((9,)),
            pltpu.SemaphoreType.REGULAR,
        ],
        compiler_params=pltpu.CompilerParams(
            collective_id=0, has_side_effects=True, vmem_limit_bytes=VMEM_LIMIT
        ),
    )(
        pltpu.with_memory_space_constraint(fluid_pops, pltpu.HBM),
        pltpu.with_memory_space_constraint(magnet_pops, pltpu.HBM),
    )
    return pl.pallas_call(
        finish,
        out_shape=[jax.ShapeDtypeStruct(fluid, F32), jax.ShapeDtypeStruct(magnet, F32)],
        in_specs=[vmem] * 6,
        out_specs=[hbm] * 2,
        scratch_shapes=[
            pltpu.VMEM((3, 8, NY), F32),
            pltpu.VMEM((16 * NPOP, NY), F32),
            pltpu.VMEM(edge_f, F32),
            pltpu.VMEM(edge_g, F32),
            pltpu.SemaphoreType.DMA((2,)),
        ],
        compiler_params=pltpu.CompilerParams(vmem_limit_bytes=VMEM_LIMIT),
    )(fo, go, fe, ge, ao.reshape(NZ * RX, NY), yb.reshape(2, NZ * RX, NY))


VMEM_LIMIT = 48 << 20
SEAM = 16


def solution(mesh):
    specs = (P(None, None, "gx", "gy"), P(None, None, None, "gx", "gy"))
    return jax.shard_map(
        functools.partial(per_device, (mesh.shape["gx"], mesh.shape["gy"])),
        mesh=mesh,
        in_specs=specs,
        out_specs=specs,
        check_vma=False,
    )
```

```python
import functools

import jax
import jax.numpy as jnp
from jax import lax
from jax.experimental import pallas as pl
from jax.experimental.pallas import tpu as pltpu
from jax.sharding import PartitionSpec as P

MESH = pl.DeviceIdType.MESH
F32 = jnp.float32

FLUID = [
    (0, 0, 0),
    (1, 0, 0), (-1, 0, 0), (0, 1, 0), (0, -1, 0), (0, 0, 1), (0, 0, -1),
    (1, 1, 0), (-1, -1, 0), (1, -1, 0), (-1, 1, 0),
    (1, 0, 1), (-1, 0, -1), (1, 0, -1), (-1, 0, 1),
    (0, 1, 1), (0, -1, -1), (0, 1, -1), (0, -1, 1),
]
VEL = FLUID + FLUID[:7] * 3
NPOP = 40
OM_F = 1.0 / 0.9
OM_G = 1.0 / 0.8

XP = [p for p in range(NPOP) if VEL[p][0] == 1]
X0 = [p for p in range(NPOP) if VEL[p][0] == 0]
XM = [p for p in range(NPOP) if VEL[p][0] == -1]
ORDER = XP + X0 + XM
POS = {p: i for i, p in enumerate(ORDER)}
XOFF = {}
for i, p in enumerate(XP):
    XOFF[p] = i
for i, p in enumerate(X0):
    XOFF[p] = 8 + i
for i, p in enumerate(XM):
    XOFF[p] = 40 + i
YP = [p for p in range(NPOP) if VEL[p][1] == 1]
Y0 = [p for p in range(NPOP) if VEL[p][1] == 0]
YM = [p for p in range(NPOP) if VEL[p][1] == -1]
SLOT = {}
for i, p in enumerate(Y0):
    SLOT[p] = i
for i, p in enumerate(YP):
    SLOT[p] = 24 + 2 * i
for i, p in enumerate(YM):
    SLOT[p] = 25 + 2 * i
NX, NY, NZ = 16, 128, 2
PAD = 8
RX = NX + 2 * PAD


def zflip(p):
    return abs(VEL[p][2])


def plane(p, z, r, count=8):
    first = (POS[p] * NZ + z) * RX + PAD + r
    return slice(first, first + count)


def collide(pops):
    f, g = pops[:19], [pops[19 + 7 * a : 26 + 7 * a] for a in range(3)]
    pairs = [(i, i + 1) for i in range(1, 19, 2)]
    even = [f[i] + f[j] for i, j in pairs]
    odd = [f[i] - f[j] for i, j in pairs]
    rho = f[0] + ((even[0] + even[1]) + (even[2] + even[3])) + ((even[4] + even[5]) + ((even[6] + even[7]) + even[8]))
    mom = []
    for a in range(3):
        terms = [(odd[k], VEL[pairs[k][0]][a]) for k in range(9) if VEL[pairs[k][0]][a]]
        total = terms[0][0]
        for value, sign in terms[1:]:
            total = total + value if sign > 0 else total - value
        mom.append(total)
    u = [m / rho for m in mom]
    b = [((g[a][0] + g[a][1]) + (g[a][2] + g[a][3])) + ((g[a][4] + g[a][5]) + g[a][6]) for a in range(3)]
    half = 0.5 * (b[0] * b[0] + b[1] * b[1] + b[2] * b[2])
    diag = [mom[a] * u[a] - b[a] * b[a] + half for a in range(3)]
    cross = {(a, c): mom[a] * u[c] - b[a] * b[c] for a, c in ((0, 1), (0, 2), (1, 2))}
    trace = diag[0] + diag[1] + diag[2]
    base = (OM_F / 36.0) * (rho - 1.5 * trace)
    d45 = [(4.5 * OM_F / 36.0) * d for d in diag]
    c9 = {k: (9.0 * OM_F / 36.0) * v for k, v in cross.items()}
    m3 = [(3.0 * OM_F / 36.0) * m for m in mom]
    keep = 1.0 - OM_F
    out = [None] * NPOP
    out[0] = keep * f[0] + 12.0 * base
    for k, (i, j) in enumerate(pairs):
        c = VEL[i]
        axes = [a for a in range(3) if c[a]]
        if len(axes) == 1:
            s = 2.0 * (base + d45[axes[0]])
            t = 2.0 * m3[axes[0]]
        else:
            a, d = axes
            s = base + d45[a] + d45[d]
            if c[a] * c[d] > 0:
                s = s + c9[(a, d)]
            else:
                s = s - c9[(a, d)]
            first = m3[a] if c[a] > 0 else -m3[a]
            t = first + m3[d] if c[d] > 0 else first - m3[d]
        out[i] = keep * f[i] + (s + t)
        out[j] = keep * f[j] + (s - t)
    keep = 1.0 - OM_G
    for a in range(3):
        rest = (OM_G / 8.0) * b[a]
        out[19 + 7 * a] = keep * g[a][0] + 2.0 * rest
        for d in range(3):
            plus, minus = rest, rest
            if d != a:
                flux = (4.0 * OM_G / 8.0) * (u[d] * b[a] - b[d] * u[a])
                plus, minus = rest + flux, rest - flux
            out[19 + 7 * a + 1 + 2 * d] = keep * g[a][1 + 2 * d] + plus
            out[19 + 7 * a + 2 + 2 * d] = keep * g[a][2 + 2 * d] + minus
    return out


def edge_rows(block, leading, tr, uu, mg):
    tr[0:NY, 0 : NZ * RX] = block.T

    def turn(p, value):
        return pltpu.roll(value, VEL[p][0] % NY, 1) if VEL[p][0] else value

    post = collide([turn(p, tr[pl.ds(SLOT[p], 2, stride=64), :]) for p in range(NPOP)])
    own = 1 if leading == 1 else 0
    at = {}
    for p in range(NPOP):
        if VEL[p][1] == 0:
            at[p] = SLOT[p]
            uu[at[p] : at[p] + 1, :] = post[p][own : own + 1]
        elif VEL[p][1] == leading:
            at[p] = SLOT[p] - (0 if leading == 1 else 1)
            uu[at[p] : at[p] + 2, :] = post[p]
    mg[...] = uu[:, 0 : NZ * RX].T
    return at


def patched(p, z, half, leading, at, mg, value, lane):
    start = (z ^ zflip(p)) * RX + PAD + 8 * half - VEL[p][0]
    width = 2 if VEL[p][1] else 1
    first = 0 if leading == 1 else NY - width
    patch = pltpu.roll(mg[start : start + 8, :], (first - at[p]) % NY, 1)
    return jnp.where((lane >= first) & (lane < first + width), patch, value)


def near_right(shape):
    lane = lax.broadcasted_iota(jnp.int32, shape, 1)
    return (lane < 24) | (((lane < 40) | ((lane >= 88) & (lane < 104))) & (lane % 2 == 0))


def exchange(
    sizes, f_hbm, g_hbm, fo, go, fe, ge, ao, yb, fv, gv, fc, gc, corner, q, w, xs, xb, tr, uu, mg,
    sems, ready,
):
    nx_dev, ny_dev = sizes
    ix, iy = lax.axis_index("gx"), lax.axis_index("gy")

    def device(dx, dy):
        return (lax.rem(ix + dx + nx_dev, nx_dev), lax.rem(iy + dy + ny_dev, ny_dev))

    block = SEAM if ny_dev % SEAM == 0 else ny_dev
    place = lax.rem(iy, block)
    is_first, is_last, is_before = place == 0, place == block - 1, place == block - 2

    sent, centers_in, corners_in, below_in, beside_in = (sems.at[k] for k in range(5))
    loaded = [sems.at[5 + half] for half in range(2)]
    corner_loaded = [sems.at[7 + side] for side in range(2)]

    def wait(semaphore, rows):
        pltpu.make_async_copy(q.at[0:rows], q.at[0:rows], semaphore).wait()

    @pl.when(is_last)
    def _():
        for side, r in enumerate((0, NX - 2)):
            pltpu.make_async_copy(f_hbm.at[:, :, r : r + 2], fc.at[side], corner_loaded[side]).start()
            pltpu.make_async_copy(g_hbm.at[:, :, :, r : r + 2], gc.at[side], corner_loaded[side]).start()

    barrier = pltpu.get_barrier_semaphore()

    def greet(steps, semaphore):
        for dx, dy in steps:
            pl.semaphore_signal(semaphore, inc=1, device_id=device(dx, dy), device_id_type=MESH)

    above = [(-1, 1), (0, 1), (1, 1)]

    @pl.when(is_last)
    def _():
        pl.semaphore_wait(barrier, 3)
        greet([(0, 1)], ready)

    for half in range(2):
        rows = slice(8 * half, 8 * half + 8)
        pltpu.make_async_copy(f_hbm.at[:, :, rows], fv.at[:, :, rows], loaded[half]).start()
        pltpu.make_async_copy(g_hbm.at[:, :, :, rows], gv.at[:, :, :, rows], loaded[half]).start()

    beside = [(-1, 0), (1, 0)]
    below = [(-1, -1), (0, -1), (1, -1)]

    @pl.when(is_last)
    def _():
        greet(below, barrier)

    @pl.when(jnp.logical_not(is_last))
    def _():
        greet(below + beside, barrier)

        @pl.when(jnp.logical_not(is_before))
        def _():
            greet(above, barrier)

    low, high, own = slice(0, 8), slice(24, 32), slice(8, 24)
    first, last = slice(8, 16), slice(16, 24)

    def to(src, dst, dx, dy, semaphore):
        return pltpu.make_async_remote_copy(
            src_ref=src, dst_ref=dst, send_sem=sent, recv_sem=semaphore,
            device_id=device(dx, dy), device_id_type=MESH,
        )

    def corners(block, side, dy, semaphore, lo, hi):
        return [
            to(block.at[:, lo : lo + 2], yb.at[side, :, 24:26], -1, dy, semaphore),
            to(block.at[:, hi : hi + 2], yb.at[side, :, 6:8], 1, dy, semaphore),
        ]

    early = [
        to(corner.at[0], yb.at[0, :, 24:26], -1, 1, corners_in),
        to(corner.at[1], yb.at[0, :, 6:8], 1, 1, corners_in),
    ]
    above_corners = corners(ao, 0, 1, corners_in, 8, 22)
    above_center = to(ao.at[:, own], yb.at[0, :, own], 0, 1, centers_in)
    to_below = corners(ao, 1, -1, below_in, 8, 22) + [to(ao.at[:, own], yb.at[1, :, own], 0, -1, below_in)]
    with_corners = to(ao.at[:, 6:26], yb.at[1, :, 6:26], 0, -1, below_in)
    to_beside = [
        to(xs.at[0], xb.at[0, :, 0:40], 1, 0, beside_in),
        to(xs.at[1], xb.at[1, :, 8:48], -1, 0, beside_in),
        to(ao.at[:, last], ao.at[:, low], 1, 0, beside_in),
        to(ao.at[:, first], ao.at[:, high], -1, 0, beside_in),
    ]

    def start(copies):
        for copy in copies:
            copy.start()

    @pl.when(is_last)
    def _():
        lane = lax.broadcasted_iota(jnp.int32, (2, NY), 1)
        columns = [(p, SLOT[p], NY - 1 - (1 if VEL[p][1] else 0)) for p in Y0 + YP]
        columns += [(p, SLOT[p] + 64, NY - 1) for p in YP]
        for side in range(2):
            wait(corner_loaded[side], 2 * NZ * NPOP)
            up = [[jnp.zeros((2, NY), F32) for _ in range(4)] for _ in range(NZ)]
            for z in range(NZ):
                pops = [fc[side, p, z] for p in range(19)] + [gc[side, a, j, z] for a in range(3) for j in range(7)]
                post = collide(pops)
                for k, (p, s, column) in enumerate(columns):
                    part = up[z ^ zflip(p)]
                    part[k % 4] = jnp.where(lane == s, pltpu.roll(post[p], (s - column) % NY, 1), part[k % 4])
            for z in range(NZ):
                corner[side, z] = (up[z][0] + up[z][1]) + (up[z][2] + up[z][3])
            early[side].start()

    lane = lax.broadcasted_iota(jnp.int32, (8, NY), 1)
    for half in range(2):
        rows = slice(8 * half, 8 * half + 8)
        at = slice(PAD + 8 * half, PAD + 8 * half + 8)
        up = [jnp.zeros((8, NY), F32) for _ in range(NZ)]
        down = [jnp.zeros((8, NY), F32) for _ in range(NZ)]
        wait(loaded[half], 8 * NZ * NPOP)
        for z in range(NZ):
            pops = [fv[p, z, rows, :] for p in range(19)]
            pops += [gv[a, j, z, rows, :] for a in range(3) for j in range(7)]
            post = collide(pops)
            for p in range(NPOP):
                zz = z ^ zflip(p)
                q[plane(p, zz, 8 * half), :] = post[p]
                s = SLOT[p]
                if VEL[p][1] == 0:
                    moved = pltpu.roll(post[p], s + 1, 1)
                    up[zz] = jnp.where(lane == s, moved, up[zz])
                    down[zz] = jnp.where(lane == s + 1, moved, down[zz])
                elif VEL[p][1] == 1:
                    moved = pltpu.roll(post[p], s + 2, 1)
                    up[zz] = jnp.where((lane == s) | (lane == s + 1), moved, up[zz])
                else:
                    moved = pltpu.roll(post[p], s, 1)
                    down[zz] = jnp.where((lane == s) | (lane == s + 1), moved, down[zz])
        for z in range(NZ):
            here = jnp.where((lane < 24) | ((lane < 40) & (lane % 2 == 0)), up[z], down[z])
            there = jnp.where((lane >= 25) & (lane < 40) & (lane % 2 == 1), up[z], down[z])
            ao[z, at, :] = jnp.where(lane < 64, here, pltpu.roll(there, 63, 1))
    @pl.when(is_first)
    def _():
        pl.semaphore_wait(barrier, 5)

    @pl.when(jnp.logical_not(is_first | is_last))
    def _():
        pl.semaphore_wait(barrier, 8)

    @pl.when(is_before)
    def _():
        greet([(0, 1)], ready)

    @pl.when(jnp.logical_not(is_last))
    def _():
        start(above_corners)

    above_center.start()

    def row(first, count, z, r):
        return q[pl.ds(first * NZ * RX + z * RX + PAD + r, count, stride=NZ * RX), :]

    for z in range(NZ):
        xs[0, z, 0:8, :] = row(0, 8, z, NX - 2)
        xs[0, z, 8:32, :] = row(8, 24, z, NX - 1)
        xs[0, z, 32:40, :] = row(0, 8, z, NX - 1)
        xs[1, z, 0:24, :] = row(8, 24, z, 0)
        xs[1, z, 24:32, :] = row(32, 8, z, 0)
        xs[1, z, 32:40, :] = row(32, 8, z, 1)
        xb[0, z, 40:48, :] = row(32, 8, z, 0)
        xb[1, z, 0:8, :] = row(0, 8, z, NX - 1)

    @pl.when(is_last)
    def _():
        pl.semaphore_wait(ready, 1)

    start(to_beside)

    @pl.when(jnp.logical_not(is_first))
    def _():
        start(to_below)

    wait(beside_in, 2 * NZ * 48)

    def turn(p, value):
        return pltpu.roll(value, VEL[p][1] % NY, 1) if VEL[p][1] else value

    for i in range(8):
        for z in range(NZ):
            q[plane(XP[i], z, -1, 1), :] = xb[0, z, 32 + i : 33 + i, :]
            q[plane(XM[i], z, NX, 1), :] = xb[1, z, 32 + i : 33 + i, :]
    edges = []
    for p in range(NPOP):
        at = slice(XOFF[p], XOFF[p] + 1)
        edges.append(turn(p, jnp.concatenate([xb[side, z, at, :] for side in range(2) for z in range(NZ)], axis=0)))
    edges = collide(edges)
    for p in range(NPOP):
        for z in range(NZ):
            zz = z ^ zflip(p)
            if VEL[p][0] == 1:
                w[plane(p, zz, -1, 1), :] = edges[p][z : z + 1]
            elif VEL[p][0] == -1:
                w[plane(p, zz, NX, 1), :] = edges[p][NZ + z : NZ + z + 1]
    for z in range(NZ):
        for half in range(2):
            post = collide([turn(p, q[plane(p, z, 8 * half - VEL[p][0]), :]) for p in range(NPOP)])
            for p in range(NPOP):
                w[plane(p, z ^ zflip(p), 8 * half), :] = post[p]
    for p in range(NPOP):
        for z in range(NZ):
            for half in range(2):
                value = turn(p, w[plane(p, z, 8 * half - VEL[p][0]), :])
                rows = slice(8 * half, 8 * half + 8)
                if p < 19:
                    fo[p, z, rows, :] = value
                else:
                    go[(p - 19) // 7, (p - 19) % 7, z, rows, :] = value

    wait(below_in, NZ * 20)
    tall = near_right((NZ * RX, NY))
    flat = ao[...].reshape(NZ * RX, NY)

    def patch(leading, block):
        places = edge_rows(block, leading, tr, uu, mg)
        for p in places:
            for z in range(NZ):
                for half in range(2):
                    rows = slice(8 * half, 8 * half + 8)
                    if p < 19:
                        fo[p, z, rows, :] = patched(p, z, half, leading, places, mg, fo[p, z, rows, :], lane)
                    else:
                        a, j = (p - 19) // 7, (p - 19) % 7
                        go[a, j, z, rows, :] = patched(p, z, half, leading, places, mg, go[a, j, z, rows, :], lane)

    patch(-1, jnp.where(tall, flat, yb[1].reshape(NZ * RX, NY)))

    @pl.when(is_first)
    def _():
        pl.semaphore_wait(ready, 1)
        with_corners.start()

    wait(centers_in, NZ * NX)
    middle = [
        part
        for z in range(NZ)
        for part in (ao[z, low], jnp.where(tall[0:NX], yb[0, z, own], ao[z, own]), ao[z, high])
    ]
    patch(1, jnp.concatenate(middle, axis=0))
    for z in range(NZ):
        for side, r in enumerate((0, NX - 2)):
            to = slice(4 * z + 2 * side, 4 * z + 2 * side + 2)
            for p in range(19):
                fe[p, to, :] = fo[p, z, r : r + 2, :]
            for a in range(3):
                for j in range(7):
                    ge[a, j, to, :] = go[a, j, z, r : r + 2, :]

    wait(sent, NZ * (20 + 20) + 2 * NZ * 48)
    wait(corners_in, NZ * 4)


def finish(fi, gi, fe, ge, ao, yb, f_hbm, g_hbm, near, post_rows, fo, go, out_sem):
    stored_f, stored_g = out_sem.at[0], out_sem.at[1]
    pltpu.make_async_copy(fi.at[:, :, 2 : NX - 2], f_hbm.at[:, :, 2 : NX - 2], stored_f).start()
    pltpu.make_async_copy(gi.at[:, :, :, 2 : NX - 2], g_hbm.at[:, :, :, 2 : NX - 2], stored_g).start()

    mask = near_right((2, NY))
    for cx in (-1, 0, 1):
        for z in range(NZ):
            for k, r in enumerate((-1, NX - 1)):
                first = z * RX + PAD + r - cx
                rows = slice(first, first + 2)
                near[cx % 3, 4 * z + 2 * k : 4 * z + 2 * k + 2, :] = jnp.where(mask, yb[0, rows, :], ao[rows, :])
    sources = [near[cx] for cx in range(3)]
    post = collide([pltpu.roll(sources[VEL[p][0] % 3], (64 - SLOT[p]) % NY, 1) for p in range(NPOP)])
    lane = lax.broadcasted_iota(jnp.int32, (8, NY), 1)
    row = lax.broadcasted_iota(jnp.int32, (8, NY), 0)
    row = row % 4
    strips = [
        (z, r, slice(4 * z + 2 * side, 4 * z + 2 * side + 2))
        for z in range(NZ)
        for side, r in enumerate((0, NX - 2))
    ]
    for p in [*range(19, NPOP), *range(19)]:
        cx, cy, _ = VEL[p]
        at = (fe, fo, p) if p < 19 else (ge, go, ((p - 19) // 7, (p - 19) % 7))
        value = at[0][at[2]]
        if cy >= 0:
            new = post[p]
            if cy:
                new = jnp.where(lane == 0, pltpu.roll(new, 64, 1), pltpu.roll(new, 1, 1))
            turned = 4 * zflip(p)
            if turned or not cx:
                base = 16 * p
                post_rows[base : base + 8, :] = new
                post_rows[base + 8 : base + 16, :] = new
            if cx:
                if turned:
                    new = post_rows[base + turned : base + turned + 8, :]
                reached = row < 2 if cx > 0 else row >= 2
                value = jnp.where(reached & (lane <= cy), new, value)
            else:
                for shift, reached in ((1, row == 0), (-1, row == 3)):
                    first = base + (turned + shift) % 8
                    value = jnp.where(reached & (lane <= cy), post_rows[first : first + 8, :], value)
        at[1][at[2]] = value
        if p == 39:
            for z, r, rows in strips:
                pltpu.make_async_copy(go.at[:, :, rows], g_hbm.at[:, :, z, r : r + 2], stored_g).start()
    for z, r, rows in strips:
        pltpu.make_async_copy(fo.at[:, rows], f_hbm.at[:, z, r : r + 2], stored_f).start()
    pltpu.make_async_copy(fi, f_hbm, stored_f).wait()
    pltpu.make_async_copy(gi, g_hbm, stored_g).wait()


def per_device(sizes, fluid_pops, magnet_pops):
    vmem = pl.BlockSpec(memory_space=pltpu.VMEM)
    hbm = pl.BlockSpec(memory_space=pltpu.HBM)
    fluid, magnet = (19, NZ, NX, NY), (3, 7, NZ, NX, NY)
    columns = (NZ, RX, NY)
    turned = [pltpu.VMEM((NY + 64, NY), F32), pltpu.VMEM((NY, NY), F32), pltpu.VMEM((NZ * RX, NY), F32)]
    edge_f, edge_g = (19, 8, NY), (3, 7, 8, NY)
    fo, go, fe, ge, ao, yb = pl.pallas_call(
        functools.partial(exchange, sizes),
        out_shape=[pltpu.VMEM(shape, F32) for shape in (fluid, magnet, edge_f, edge_g, columns, (2, *columns))],
        in_specs=[hbm] * 2,
        out_specs=[vmem] * 6,
        scratch_shapes=[
            pltpu.VMEM(fluid, F32),
            pltpu.VMEM(magnet, F32),
            pltpu.VMEM((2, 19, NZ, 2, NY), F32),
            pltpu.VMEM((2, 3, 7, NZ, 2, NY), F32),
            pltpu.VMEM((2, NZ, 2, NY), F32),
            pltpu.VMEM(((NPOP + 1) * NZ * RX, NY), F32),
            pltpu.VMEM((NPOP * NZ * RX, NY), F32),
            pltpu.VMEM((2, NZ, 40, NY), F32),
            pltpu.VMEM((2, NZ, 48, NY), F32),
            *turned,
            pltpu.SemaphoreType.DMA((9,)),
            pltpu.SemaphoreType.REGULAR,
        ],
        compiler_params=pltpu.CompilerParams(
            collective_id=0, has_side_effects=True, vmem_limit_bytes=VMEM_LIMIT
        ),
    )(
        pltpu.with_memory_space_constraint(fluid_pops, pltpu.HBM),
        pltpu.with_memory_space_constraint(magnet_pops, pltpu.HBM),
    )
    return pl.pallas_call(
        finish,
        out_shape=[jax.ShapeDtypeStruct(fluid, F32), jax.ShapeDtypeStruct(magnet, F32)],
        in_specs=[vmem] * 6,
        out_specs=[hbm] * 2,
        scratch_shapes=[
            pltpu.VMEM((3, 8, NY), F32),
            pltpu.VMEM((16 * NPOP, NY), F32),
            pltpu.VMEM(edge_f, F32),
            pltpu.VMEM(edge_g, F32),
            pltpu.SemaphoreType.DMA((2,)),
        ],
        compiler_params=pltpu.CompilerParams(vmem_limit_bytes=VMEM_LIMIT),
    )(fo, go, fe, ge, ao.reshape(NZ * RX, NY), yb.reshape(2, NZ * RX, NY))


VMEM_LIMIT = 48 << 20
SEAM = 16


def solution(mesh):
    specs = (P(None, None, "gx", "gy"), P(None, None, None, "gx", "gy"))
    return jax.shard_map(
        functools.partial(per_device, (mesh.shape["gx"], mesh.shape["gy"])),
        mesh=mesh,
        in_specs=specs,
        out_specs=specs,
        check_vma=False,
    )
```

```python
import functools

import jax
import jax.numpy as jnp
from jax import lax
from jax.experimental import pallas as pl
from jax.experimental.pallas import tpu as pltpu
from jax.sharding import PartitionSpec as P

MESH = pl.DeviceIdType.MESH
F32 = jnp.float32

FLUID = [
    (0, 0, 0),
    (1, 0, 0), (-1, 0, 0), (0, 1, 0), (0, -1, 0), (0, 0, 1), (0, 0, -1),
    (1, 1, 0), (-1, -1, 0), (1, -1, 0), (-1, 1, 0),
    (1, 0, 1), (-1, 0, -1), (1, 0, -1), (-1, 0, 1),
    (0, 1, 1), (0, -1, -1), (0, 1, -1), (0, -1, 1),
]
VEL = FLUID + FLUID[:7] * 3
NPOP = 40
OM_F = 1.0 / 0.9
OM_G = 1.0 / 0.8

XP = [p for p in range(NPOP) if VEL[p][0] == 1]
X0 = [p for p in range(NPOP) if VEL[p][0] == 0]
XM = [p for p in range(NPOP) if VEL[p][0] == -1]
ORDER = XP + X0 + XM
POS = {p: i for i, p in enumerate(ORDER)}
XOFF = {}
for i, p in enumerate(XP):
    XOFF[p] = i
for i, p in enumerate(X0):
    XOFF[p] = 8 + i
for i, p in enumerate(XM):
    XOFF[p] = 40 + i
YP = [p for p in range(NPOP) if VEL[p][1] == 1]
Y0 = [p for p in range(NPOP) if VEL[p][1] == 0]
YM = [p for p in range(NPOP) if VEL[p][1] == -1]
SLOT = {}
for i, p in enumerate(Y0):
    SLOT[p] = i
for i, p in enumerate(YP):
    SLOT[p] = 24 + 2 * i
for i, p in enumerate(YM):
    SLOT[p] = 25 + 2 * i
NX, NY, NZ = 16, 128, 2
PAD = 8
RX = NX + 2 * PAD


def zflip(p):
    return abs(VEL[p][2])


def plane(p, z, r, count=8):
    first = (POS[p] * NZ + z) * RX + PAD + r
    return slice(first, first + count)


def collide(pops):
    f, g = pops[:19], [pops[19 + 7 * a : 26 + 7 * a] for a in range(3)]
    pairs = [(i, i + 1) for i in range(1, 19, 2)]
    even = [f[i] + f[j] for i, j in pairs]
    odd = [f[i] - f[j] for i, j in pairs]
    rho = f[0] + ((even[0] + even[1]) + (even[2] + even[3])) + ((even[4] + even[5]) + ((even[6] + even[7]) + even[8]))
    mom = []
    for a in range(3):
        terms = [(odd[k], VEL[pairs[k][0]][a]) for k in range(9) if VEL[pairs[k][0]][a]]
        total = terms[0][0]
        for value, sign in terms[1:]:
            total = total + value if sign > 0 else total - value
        mom.append(total)
    u = [m / rho for m in mom]
    b = [((g[a][0] + g[a][1]) + (g[a][2] + g[a][3])) + ((g[a][4] + g[a][5]) + g[a][6]) for a in range(3)]
    half = 0.5 * (b[0] * b[0] + b[1] * b[1] + b[2] * b[2])
    diag = [mom[a] * u[a] - b[a] * b[a] + half for a in range(3)]
    cross = {(a, c): mom[a] * u[c] - b[a] * b[c] for a, c in ((0, 1), (0, 2), (1, 2))}
    trace = diag[0] + diag[1] + diag[2]
    base = (OM_F / 36.0) * (rho - 1.5 * trace)
    d45 = [(4.5 * OM_F / 36.0) * d for d in diag]
    c9 = {k: (9.0 * OM_F / 36.0) * v for k, v in cross.items()}
    m3 = [(3.0 * OM_F / 36.0) * m for m in mom]
    keep = 1.0 - OM_F
    out = [None] * NPOP
    out[0] = keep * f[0] + 12.0 * base
    for k, (i, j) in enumerate(pairs):
        c = VEL[i]
        axes = [a for a in range(3) if c[a]]
        if len(axes) == 1:
            s = 2.0 * (base + d45[axes[0]])
            t = 2.0 * m3[axes[0]]
        else:
            a, d = axes
            s = base + d45[a] + d45[d]
            if c[a] * c[d] > 0:
                s = s + c9[(a, d)]
            else:
                s = s - c9[(a, d)]
            first = m3[a] if c[a] > 0 else -m3[a]
            t = first + m3[d] if c[d] > 0 else first - m3[d]
        out[i] = keep * f[i] + (s + t)
        out[j] = keep * f[j] + (s - t)
    keep = 1.0 - OM_G
    for a in range(3):
        rest = (OM_G / 8.0) * b[a]
        out[19 + 7 * a] = keep * g[a][0] + 2.0 * rest
        for d in range(3):
            plus, minus = rest, rest
            if d != a:
                flux = (4.0 * OM_G / 8.0) * (u[d] * b[a] - b[d] * u[a])
                plus, minus = rest + flux, rest - flux
            out[19 + 7 * a + 1 + 2 * d] = keep * g[a][1 + 2 * d] + plus
            out[19 + 7 * a + 2 + 2 * d] = keep * g[a][2 + 2 * d] + minus
    return out


def edge_rows(block, leading, tr, uu, mg):
    tr[0:NY, 0 : NZ * RX] = block.T

    def turn(p, value):
        return pltpu.roll(value, VEL[p][0] % NY, 1) if VEL[p][0] else value

    post = collide([turn(p, tr[pl.ds(SLOT[p], 2, stride=64), :]) for p in range(NPOP)])
    own = 1 if leading == 1 else 0
    at = {}
    for p in range(NPOP):
        if VEL[p][1] == 0:
            at[p] = SLOT[p]
            uu[at[p] : at[p] + 1, :] = post[p][own : own + 1]
        elif VEL[p][1] == leading:
            at[p] = SLOT[p] - (0 if leading == 1 else 1)
            uu[at[p] : at[p] + 2, :] = post[p]
    mg[...] = uu[:, 0 : NZ * RX].T
    return at


def patched(p, z, half, leading, at, mg, value, lane):
    start = (z ^ zflip(p)) * RX + PAD + 8 * half - VEL[p][0]
    width = 2 if VEL[p][1] else 1
    first = 0 if leading == 1 else NY - width
    patch = pltpu.roll(mg[start : start + 8, :], (first - at[p]) % NY, 1)
    return jnp.where((lane >= first) & (lane < first + width), patch, value)


def near_right(shape):
    lane = lax.broadcasted_iota(jnp.int32, shape, 1)
    return (lane < 24) | (((lane < 40) | ((lane >= 88) & (lane < 104))) & (lane % 2 == 0))


def exchange(
    sizes, f_hbm, g_hbm, fo, go, fe, ge, ao, yb, fv, gv, fc, gc, corner, q, w, xs, xb, tr, uu, mg,
    sems, ready,
):
    nx_dev, ny_dev = sizes
    ix, iy = lax.axis_index("gx"), lax.axis_index("gy")

    def device(dx, dy):
        return (lax.rem(ix + dx + nx_dev, nx_dev), lax.rem(iy + dy + ny_dev, ny_dev))

    block = SEAM if ny_dev % SEAM == 0 else ny_dev
    place = lax.rem(iy, block)
    is_first, is_last, is_before = place == 0, place == block - 1, place == block - 2

    sent, centers_in, corners_in, others_in = (sems.at[k] for k in range(4))
    loaded = [sems.at[4 + half] for half in range(2)]
    corner_loaded = [sems.at[6 + side] for side in range(2)]

    def wait(semaphore, rows):
        pltpu.make_async_copy(q.at[0:rows], q.at[0:rows], semaphore).wait()

    @pl.when(is_last)
    def _():
        for side, r in enumerate((0, NX - 2)):
            pltpu.make_async_copy(f_hbm.at[:, :, r : r + 2], fc.at[side], corner_loaded[side]).start()
            pltpu.make_async_copy(g_hbm.at[:, :, :, r : r + 2], gc.at[side], corner_loaded[side]).start()

    barrier = pltpu.get_barrier_semaphore()

    def greet(steps, semaphore):
        for dx, dy in steps:
            pl.semaphore_signal(semaphore, inc=1, device_id=device(dx, dy), device_id_type=MESH)

    above = [(-1, 1), (0, 1), (1, 1)]

    @pl.when(is_last)
    def _():
        pl.semaphore_wait(barrier, 3)
        greet([(0, 1)], ready)

    for half in range(2):
        rows = slice(8 * half, 8 * half + 8)
        pltpu.make_async_copy(f_hbm.at[:, :, rows], fv.at[:, :, rows], loaded[half]).start()
        pltpu.make_async_copy(g_hbm.at[:, :, :, rows], gv.at[:, :, :, rows], loaded[half]).start()

    beside = [(-1, 0), (1, 0)]
    below = [(-1, -1), (0, -1), (1, -1)]

    @pl.when(is_last)
    def _():
        greet(below, barrier)

    @pl.when(jnp.logical_not(is_last))
    def _():
        greet(below + beside, barrier)

        @pl.when(jnp.logical_not(is_before))
        def _():
            greet(above, barrier)

    low, high, own = slice(0, 8), slice(24, 32), slice(8, 24)
    first, last = slice(8, 16), slice(16, 24)

    def to(src, dst, dx, dy, semaphore):
        return pltpu.make_async_remote_copy(
            src_ref=src, dst_ref=dst, send_sem=sent, recv_sem=semaphore,
            device_id=device(dx, dy), device_id_type=MESH,
        )

    def corners(block, side, dy, semaphore, lo, hi):
        return [
            to(block.at[:, lo : lo + 2], yb.at[side, :, 24:26], -1, dy, semaphore),
            to(block.at[:, hi : hi + 2], yb.at[side, :, 6:8], 1, dy, semaphore),
        ]

    early = [
        to(corner.at[0], yb.at[0, :, 24:26], -1, 1, corners_in),
        to(corner.at[1], yb.at[0, :, 6:8], 1, 1, corners_in),
    ]
    above_corners = corners(ao, 0, 1, corners_in, 8, 22)
    above_center = to(ao.at[:, own], yb.at[0, :, own], 0, 1, centers_in)
    to_below = corners(ao, 1, -1, others_in, 8, 22) + [to(ao.at[:, own], yb.at[1, :, own], 0, -1, others_in)]
    with_corners = to(ao.at[:, 6:26], yb.at[1, :, 6:26], 0, -1, others_in)
    to_beside = [
        to(xs.at[0], xb.at[0, :, 0:40], 1, 0, others_in),
        to(xs.at[1], xb.at[1, :, 8:48], -1, 0, others_in),
        to(ao.at[:, last], ao.at[:, low], 1, 0, others_in),
        to(ao.at[:, first], ao.at[:, high], -1, 0, others_in),
    ]

    def start(copies):
        for copy in copies:
            copy.start()

    @pl.when(is_last)
    def _():
        lane = lax.broadcasted_iota(jnp.int32, (2, NY), 1)
        columns = [(p, SLOT[p], NY - 1 - (1 if VEL[p][1] else 0)) for p in Y0 + YP]
        columns += [(p, SLOT[p] + 64, NY - 1) for p in YP]
        for side in range(2):
            wait(corner_loaded[side], 2 * NZ * NPOP)
            up = [[jnp.zeros((2, NY), F32) for _ in range(4)] for _ in range(NZ)]
            for z in range(NZ):
                pops = [fc[side, p, z] for p in range(19)] + [gc[side, a, j, z] for a in range(3) for j in range(7)]
                post = collide(pops)
                for k, (p, s, column) in enumerate(columns):
                    part = up[z ^ zflip(p)]
                    part[k % 4] = jnp.where(lane == s, pltpu.roll(post[p], (s - column) % NY, 1), part[k % 4])
            for z in range(NZ):
                corner[side, z] = (up[z][0] + up[z][1]) + (up[z][2] + up[z][3])
            early[side].start()

    lane = lax.broadcasted_iota(jnp.int32, (8, NY), 1)
    for half in range(2):
        rows = slice(8 * half, 8 * half + 8)
        at = slice(PAD + 8 * half, PAD + 8 * half + 8)
        up = [jnp.zeros((8, NY), F32) for _ in range(NZ)]
        down = [jnp.zeros((8, NY), F32) for _ in range(NZ)]
        wait(loaded[half], 8 * NZ * NPOP)
        for z in range(NZ):
            pops = [fv[p, z, rows, :] for p in range(19)]
            pops += [gv[a, j, z, rows, :] for a in range(3) for j in range(7)]
            post = collide(pops)
            for p in range(NPOP):
                zz = z ^ zflip(p)
                q[plane(p, zz, 8 * half), :] = post[p]
                s = SLOT[p]
                if VEL[p][1] == 0:
                    moved = pltpu.roll(post[p], s + 1, 1)
                    up[zz] = jnp.where(lane == s, moved, up[zz])
                    down[zz] = jnp.where(lane == s + 1, moved, down[zz])
                elif VEL[p][1] == 1:
                    moved = pltpu.roll(post[p], s + 2, 1)
                    up[zz] = jnp.where((lane == s) | (lane == s + 1), moved, up[zz])
                else:
                    moved = pltpu.roll(post[p], s, 1)
                    down[zz] = jnp.where((lane == s) | (lane == s + 1), moved, down[zz])
        for z in range(NZ):
            here = jnp.where((lane < 24) | ((lane < 40) & (lane % 2 == 0)), up[z], down[z])
            there = jnp.where((lane >= 25) & (lane < 40) & (lane % 2 == 1), up[z], down[z])
            ao[z, at, :] = jnp.where(lane < 64, here, pltpu.roll(there, 63, 1))
    @pl.when(is_first)
    def _():
        pl.semaphore_wait(barrier, 5)

    @pl.when(jnp.logical_not(is_first | is_last))
    def _():
        pl.semaphore_wait(barrier, 8)

    @pl.when(is_before)
    def _():
        greet([(0, 1)], ready)

    @pl.when(jnp.logical_not(is_last))
    def _():
        start(above_corners)

    above_center.start()

    def row(first, count, z, r):
        return q[pl.ds(first * NZ * RX + z * RX + PAD + r, count, stride=NZ * RX), :]

    for z in range(NZ):
        xs[0, z, 0:8, :] = row(0, 8, z, NX - 2)
        xs[0, z, 8:32, :] = row(8, 24, z, NX - 1)
        xs[0, z, 32:40, :] = row(0, 8, z, NX - 1)
        xs[1, z, 0:24, :] = row(8, 24, z, 0)
        xs[1, z, 24:32, :] = row(32, 8, z, 0)
        xs[1, z, 32:40, :] = row(32, 8, z, 1)
        xb[0, z, 40:48, :] = row(32, 8, z, 0)
        xb[1, z, 0:8, :] = row(0, 8, z, NX - 1)

    @pl.when(is_last)
    def _():
        pl.semaphore_wait(ready, 1)

    start(to_beside)

    @pl.when(jnp.logical_not(is_first))
    def _():
        start(to_below)

    wait(others_in, 2 * NZ * 48 + NZ * 20)

    def turn(p, value):
        return pltpu.roll(value, VEL[p][1] % NY, 1) if VEL[p][1] else value

    for i in range(8):
        for z in range(NZ):
            q[plane(XP[i], z, -1, 1), :] = xb[0, z, 32 + i : 33 + i, :]
            q[plane(XM[i], z, NX, 1), :] = xb[1, z, 32 + i : 33 + i, :]
    edges = []
    for p in range(NPOP):
        at = slice(XOFF[p], XOFF[p] + 1)
        edges.append(turn(p, jnp.concatenate([xb[side, z, at, :] for side in range(2) for z in range(NZ)], axis=0)))
    edges = collide(edges)
    for p in range(NPOP):
        for z in range(NZ):
            zz = z ^ zflip(p)
            if VEL[p][0] == 1:
                w[plane(p, zz, -1, 1), :] = edges[p][z : z + 1]
            elif VEL[p][0] == -1:
                w[plane(p, zz, NX, 1), :] = edges[p][NZ + z : NZ + z + 1]
    for z in range(NZ):
        for half in range(2):
            post = collide([turn(p, q[plane(p, z, 8 * half - VEL[p][0]), :]) for p in range(NPOP)])
            for p in range(NPOP):
                w[plane(p, z ^ zflip(p), 8 * half), :] = post[p]
    for p in range(NPOP):
        for z in range(NZ):
            for half in range(2):
                value = turn(p, w[plane(p, z, 8 * half - VEL[p][0]), :])
                rows = slice(8 * half, 8 * half + 8)
                if p < 19:
                    fo[p, z, rows, :] = value
                else:
                    go[(p - 19) // 7, (p - 19) % 7, z, rows, :] = value

    tall = near_right((NZ * RX, NY))
    flat = ao[...].reshape(NZ * RX, NY)

    def patch(leading, block):
        places = edge_rows(block, leading, tr, uu, mg)
        for p in places:
            for z in range(NZ):
                for half in range(2):
                    rows = slice(8 * half, 8 * half + 8)
                    if p < 19:
                        fo[p, z, rows, :] = patched(p, z, half, leading, places, mg, fo[p, z, rows, :], lane)
                    else:
                        a, j = (p - 19) // 7, (p - 19) % 7
                        go[a, j, z, rows, :] = patched(p, z, half, leading, places, mg, go[a, j, z, rows, :], lane)

    patch(-1, jnp.where(tall, flat, yb[1].reshape(NZ * RX, NY)))

    @pl.when(is_first)
    def _():
        pl.semaphore_wait(ready, 1)
        with_corners.start()

    wait(centers_in, NZ * NX)
    middle = [
        part
        for z in range(NZ)
        for part in (ao[z, low], jnp.where(tall[0:NX], yb[0, z, own], ao[z, own]), ao[z, high])
    ]
    patch(1, jnp.concatenate(middle, axis=0))
    for z in range(NZ):
        for side, r in enumerate((0, NX - 2)):
            to = slice(4 * z + 2 * side, 4 * z + 2 * side + 2)
            for p in range(19):
                fe[p, to, :] = fo[p, z, r : r + 2, :]
            for a in range(3):
                for j in range(7):
                    ge[a, j, to, :] = go[a, j, z, r : r + 2, :]

    wait(sent, NZ * (20 + 20) + 2 * NZ * 48)
    wait(corners_in, NZ * 4)


def finish(fi, gi, fe, ge, ao, yb, f_hbm, g_hbm, near, post_rows, fo, go, out_sem):
    stored_f, stored_g = out_sem.at[0], out_sem.at[1]
    pltpu.make_async_copy(fi.at[:, :, 2 : NX - 2], f_hbm.at[:, :, 2 : NX - 2], stored_f).start()
    pltpu.make_async_copy(gi.at[:, :, :, 2 : NX - 2], g_hbm.at[:, :, :, 2 : NX - 2], stored_g).start()

    mask = near_right((2, NY))
    for cx in (-1, 0, 1):
        for z in range(NZ):
            for k, r in enumerate((-1, NX - 1)):
                first = z * RX + PAD + r - cx
                rows = slice(first, first + 2)
                near[cx % 3, 4 * z + 2 * k : 4 * z + 2 * k + 2, :] = jnp.where(mask, yb[0, rows, :], ao[rows, :])
    sources = [near[cx] for cx in range(3)]
    post = collide([pltpu.roll(sources[VEL[p][0] % 3], (64 - SLOT[p]) % NY, 1) for p in range(NPOP)])
    lane = lax.broadcasted_iota(jnp.int32, (8, NY), 1)
    row = lax.broadcasted_iota(jnp.int32, (8, NY), 0)
    row = row % 4
    strips = [
        (z, r, slice(4 * z + 2 * side, 4 * z + 2 * side + 2))
        for z in range(NZ)
        for side, r in enumerate((0, NX - 2))
    ]
    for p in [*range(19, NPOP), *range(19)]:
        cx, cy, _ = VEL[p]
        at = (fe, fo, p) if p < 19 else (ge, go, ((p - 19) // 7, (p - 19) % 7))
        value = at[0][at[2]]
        if cy >= 0:
            new = post[p]
            if cy:
                new = jnp.where(lane == 0, pltpu.roll(new, 64, 1), pltpu.roll(new, 1, 1))
            turned = 4 * zflip(p)
            if turned or not cx:
                base = 16 * p
                post_rows[base : base + 8, :] = new
                post_rows[base + 8 : base + 16, :] = new
            if cx:
                if turned:
                    new = post_rows[base + turned : base + turned + 8, :]
                reached = row < 2 if cx > 0 else row >= 2
                value = jnp.where(reached & (lane <= cy), new, value)
            else:
                for shift, reached in ((1, row == 0), (-1, row == 3)):
                    first = base + (turned + shift) % 8
                    value = jnp.where(reached & (lane <= cy), post_rows[first : first + 8, :], value)
        at[1][at[2]] = value
        if p == 39:
            for z, r, rows in strips:
                pltpu.make_async_copy(go.at[:, :, rows], g_hbm.at[:, :, z, r : r + 2], stored_g).start()
    for z, r, rows in strips:
        pltpu.make_async_copy(fo.at[:, rows], f_hbm.at[:, z, r : r + 2], stored_f).start()
    pltpu.make_async_copy(fi, f_hbm, stored_f).wait()
    pltpu.make_async_copy(gi, g_hbm, stored_g).wait()


def per_device(sizes, fluid_pops, magnet_pops):
    vmem = pl.BlockSpec(memory_space=pltpu.VMEM)
    hbm = pl.BlockSpec(memory_space=pltpu.HBM)
    fluid, magnet = (19, NZ, NX, NY), (3, 7, NZ, NX, NY)
    columns = (NZ, RX, NY)
    turned = [pltpu.VMEM((NY + 64, NY), F32), pltpu.VMEM((NY, NY), F32), pltpu.VMEM((NZ * RX, NY), F32)]
    edge_f, edge_g = (19, 8, NY), (3, 7, 8, NY)
    fo, go, fe, ge, ao, yb = pl.pallas_call(
        functools.partial(exchange, sizes),
        out_shape=[pltpu.VMEM(shape, F32) for shape in (fluid, magnet, edge_f, edge_g, columns, (2, *columns))],
        in_specs=[hbm] * 2,
        out_specs=[vmem] * 6,
        scratch_shapes=[
            pltpu.VMEM(fluid, F32),
            pltpu.VMEM(magnet, F32),
            pltpu.VMEM((2, 19, NZ, 2, NY), F32),
            pltpu.VMEM((2, 3, 7, NZ, 2, NY), F32),
            pltpu.VMEM((2, NZ, 2, NY), F32),
            pltpu.VMEM(((NPOP + 1) * NZ * RX, NY), F32),
            pltpu.VMEM((NPOP * NZ * RX, NY), F32),
            pltpu.VMEM((2, NZ, 40, NY), F32),
            pltpu.VMEM((2, NZ, 48, NY), F32),
            *turned,
            pltpu.SemaphoreType.DMA((8,)),
            pltpu.SemaphoreType.REGULAR,
        ],
        compiler_params=pltpu.CompilerParams(
            collective_id=0, has_side_effects=True, vmem_limit_bytes=VMEM_LIMIT
        ),
    )(
        pltpu.with_memory_space_constraint(fluid_pops, pltpu.HBM),
        pltpu.with_memory_space_constraint(magnet_pops, pltpu.HBM),
    )
    return pl.pallas_call(
        finish,
        out_shape=[jax.ShapeDtypeStruct(fluid, F32), jax.ShapeDtypeStruct(magnet, F32)],
        in_specs=[vmem] * 6,
        out_specs=[hbm] * 2,
        scratch_shapes=[
            pltpu.VMEM((3, 8, NY), F32),
            pltpu.VMEM((16 * NPOP, NY), F32),
            pltpu.VMEM(edge_f, F32),
            pltpu.VMEM(edge_g, F32),
            pltpu.SemaphoreType.DMA((2,)),
        ],
        compiler_params=pltpu.CompilerParams(vmem_limit_bytes=VMEM_LIMIT),
    )(fo, go, fe, ge, ao.reshape(NZ * RX, NY), yb.reshape(2, NZ * RX, NY))


VMEM_LIMIT = 48 << 20
SEAM = 16


def solution(mesh):
    specs = (P(None, None, "gx", "gy"), P(None, None, None, "gx", "gy"))
    return jax.shard_map(
        functools.partial(per_device, (mesh.shape["gx"], mesh.shape["gy"])),
        mesh=mesh,
        in_specs=specs,
        out_specs=specs,
        check_vma=False,
    )
```
